32 devices in a mesh: theta: 8 (over y, x, core), phi: 4 (over z).
Axes of the slice: x: 2, y: 2, z: 4, core: 2. Of those that a mesh axis runs over, the one named last changes fastest.
Arguments:
- child_out: float32 [8, 192, 384, 128], P(None, 'theta', 'phi'), may hold values from -6 to 6
- child_slot: int32 [128], replicated, may hold values from 0 to 127, each once
- sources_child: int32 [128, 12], replicated, may hold values from 0 to 127
- kinds_child: int32 [128, 12], replicated, may hold values from 0 to 127
- table_child: float32 [2, 192, 384, 128], P(None, 'theta', 'phi'), may hold values from -4 to 4
- sources_parent: int32 [16, 12], replicated, may hold values from 0 to 15
- kinds_parent: int32 [16, 12], replicated, may hold values from 0 to 127
- table_parent: float32 [2, 352, 704, 128], P(None, 'theta', 'phi'), may hold values from -1.5 to 1.5
Outputs:
- child_in: float32 [8, 192, 384, 128], P(None, 'theta', 'phi')
The draws below stay inside these ranges and needn't reach their ends.
Inputs may be any that keep to these rules, and one draw needn't show every extreme that they name: Each value occurs once; child b belongs to parent child_slot[b] % 16 as octant child_slot[b] // 16.
All inputs are finite; a program needn't handle non-finite values.
Results may differ from the reference program's by a relative error of at most 0.00012.
Values sent between devices are 32-bit elements; how exact they have to be, the bound alone decides.
No kernel may reach another device: no remote copies, remote signals or barrier semaphores. Data moves between devices by JAX's collectives and lax.ppermute only.
A program may use at most 256 MiB of HBM per device.

```python
import math
import jax
import jax.numpy as jnp
import numpy as np
from jax import lax

TH1 = 192
PH1 = 384
TH2 = 352
PH2 = 704
BAND1 = 180
NB1 = 128
NB2 = 16
LIST = 12
NTR = 128


def touch_ends(result, stream_key, least, high):
    index_at = [jax.random.randint(jax.random.fold_in(stream_key, axis), (), 0, length) for axis, length in enumerate(result.shape)]
    longest = result.shape.index(max(result.shape))
    beside = index_at[:longest] + [(index_at[longest] + 1) % result.shape[longest]] + index_at[longest + 1:]
    return result.at[tuple(index_at)].set(least).at[tuple(beside)].set(high)


def block_scale(key, dims, split, low, top_value):
    def one(axis_at, blocks):
        steps = jax.random.uniform(jax.random.fold_in(jax.random.fold_in(key, 6), axis_at), (blocks,), jnp.float32, low / len(split), top_value / len(split))
        return jnp.repeat(jnp.exp(steps), dims[axis_at] // blocks).reshape((-1,) + (1,) * (len(dims) - axis_at - 1))

    gain = one(*split[0])
    for cut in split[1:]:
        gain = gain * one(*cut)
    return gain


def scatter_about(rng, shape, spread, reach, pieces=(), kind=jnp.bfloat16):
    array = spread * jax.random.normal(rng, shape, jnp.float32)
    if pieces:
        array = array * block_scale(rng, shape, pieces, -0.22, 0.18)
    return jnp.clip(array, -reach, reach).astype(kind)


def setup_inputs(seed: int = 0) -> dict:
    key_list = jax.random.split(jax.random.key(seed), 9)
    return {
        "child_out": scatter_about(key_list[0], (8, TH1, PH1, NB1), 1.0, 6.0, ((1, 8), (2, 4)), jnp.float32),
        "child_slot": jax.random.permutation(key_list[1], NB1).astype(jnp.int32),
        "sources_child": touch_ends(jax.random.randint(key_list[2], (NB1, LIST), 0, NB1), jax.random.fold_in(key_list[2], 1), 0, NB1 - 1).astype(jnp.int32),
        "kinds_child": touch_ends(jax.random.randint(key_list[3], (NB1, LIST), 0, NTR), jax.random.fold_in(key_list[3], 1), 0, NTR - 1).astype(jnp.int32),
        "table_child": scatter_about(key_list[4], (2, TH1, PH1, NTR), 0.25, 4.0, ((1, 8), (2, 4)), jnp.float32),
        "sources_parent": touch_ends(jax.random.randint(key_list[5], (NB2, LIST), 0, NB2), jax.random.fold_in(key_list[5], 1), 0, NB2 - 1).astype(jnp.int32),
        "kinds_parent": touch_ends(jax.random.randint(key_list[6], (NB2, LIST), 0, NTR), jax.random.fold_in(key_list[6], 1), 0, NTR - 1).astype(jnp.int32),
        "table_parent": scatter_about(key_list[7], (2, TH2, PH2, NTR), 0.1, 1.5, ((1, 8), (2, 4)), jnp.float32),
    }


def stencil_entries(count_out, count_in, centered, out_rows):
    entries = []
    for row_out in out_rows:
        if centered:
            numerator = (2 * row_out + 1) * count_in - count_out
        else:
            numerator = 2 * row_out * count_in
        denominator = 2 * count_out
        base_index = numerator // denominator
        fraction = (numerator - base_index * denominator) / denominator
        for offset_a in range(-2, 4):
            weight = 1.0
            for offset_b in range(-2, 4):
                if offset_b != offset_a:
                    weight = weight * (fraction - offset_b) / (offset_a - offset_b)
            entries.append((row_out, base_index + offset_a, weight))
    return entries

def global_matrix(count_out, count_in, centered, periodic):
    matrix = np.zeros((count_out, count_in))
    for row_out, column, weight in stencil_entries(count_out, count_in, centered, range(count_out)):
        if periodic:
            matrix[row_out, column % count_in] += weight
        elif 0 <= column < count_in:
            matrix[row_out, column] += weight
    return jnp.asarray(matrix, jnp.float32)

def phase_table(count_polar, count_azimuth, polar_first, azimuth_first, rows_here, columns_here):
    polar = ((jnp.arange(rows_here, dtype=jnp.int32) + polar_first).astype(jnp.float32) + 0.5) * (math.pi / count_polar)
    azimuth = (jnp.arange(columns_here, dtype=jnp.int32) + azimuth_first).astype(jnp.float32) * (2.0 * math.pi / count_azimuth)
    octant = jnp.arange(8, dtype=jnp.int32)
    east_sign = (2 * (octant % 2) - 1).astype(jnp.float32)
    north_sign = (2 * (octant // 2 % 2) - 1).astype(jnp.float32)
    upper_sign = (2 * (octant // 4) - 1).astype(jnp.float32)
    sin_polar = jnp.sin(polar)[:, None, None]
    cos_polar = jnp.cos(polar)[:, None, None]
    cos_azimuth = jnp.cos(azimuth)[None, :, None]
    sin_azimuth = jnp.sin(azimuth)[None, :, None]
    phase_angle = BAND1 / (2.0 * math.sqrt(3.0)) * (sin_polar * cos_azimuth * east_sign + sin_polar * sin_azimuth * north_sign + cos_polar * upper_sign)
    return jnp.stack([jnp.cos(phase_angle), jnp.sin(phase_angle)])

def complex_times(pattern, factor):
    halves = pattern.reshape((2, 4) + pattern.shape[1:])
    cosine = factor[0][None]
    sine_part = factor[1][None]
    real_out = halves[0] * cosine - halves[1] * sine_part
    imag_out = halves[0] * sine_part + halves[1] * cosine
    return jnp.concatenate([real_out, imag_out], axis=0)

def aggregate(grouped, phase):
    halves = grouped.reshape((2, 4) + grouped.shape[1:])
    cosine = phase[0][None, :, :, :, None]
    sine_part = phase[1][None, :, :, :, None]
    real_out = lax.optimization_barrier(jnp.sum(halves[0] * cosine - halves[1] * sine_part, axis=3))
    imag_out = lax.optimization_barrier(jnp.sum(halves[0] * sine_part + halves[1] * cosine, axis=3))
    return jnp.concatenate([real_out, imag_out], axis=0)

def translate(pattern, sources, kinds, table):

    def accumulate(summed, columns):
        source_column, kind_column = columns
        gathered = jnp.take(pattern, source_column, axis=3)
        factor = jnp.take(table, kind_column, axis=3)
        return (summed + complex_times(gathered, factor), None)
    start = jnp.zeros(pattern.shape[:3] + (sources.shape[0],), jnp.float32)
    summed, unused = lax.scan(accumulate, start, (sources.T, kinds.T))
    return summed

def reference(child_out, child_slot, sources_child, kinds_child, table_child, sources_parent, kinds_parent, table_parent):
    exact_mode = lax.Precision.HIGHEST
    polar_up = global_matrix(TH2, TH1, True, False)
    azimuth_up = global_matrix(PH2, PH1, False, True)
    phase_up = phase_table(TH2, PH2, 0, 0, TH2, PH2)
    inverse = jnp.zeros((NB1,), jnp.int32).at[child_slot].set(jnp.arange(NB1, dtype=jnp.int32))
    children = inverse.reshape(8, NB2).T

    def one_parent(members):
        picked = jnp.take(child_out, members, axis=3)
        row_pass = jnp.einsum('pt,ctfo->cpfo', polar_up, picked, precision=exact_mode)
        interpolated = jnp.einsum('qf,cpfo->cpqo', azimuth_up, row_pass, precision=exact_mode)
        return aggregate(interpolated[..., None], phase_up)[..., 0]
    parents = lax.map(one_parent, children)
    parent_out = jnp.transpose(parents, (1, 2, 3, 0))
    parent_in = translate(parent_out, sources_parent, kinds_parent, table_parent)
    columns_back = jnp.einsum('qf,cpqb->cpfb', azimuth_up, parent_in, precision=exact_mode)
    lowered = jnp.einsum('pt,cpfb->ctfb', polar_up, columns_back, precision=exact_mode)
    expanded = jnp.take(lowered, child_slot % NB2, axis=3)
    phase_down = phase_table(TH1, PH1, 0, 0, TH1, PH1)
    box_phase = jnp.take(phase_down, child_slot // NB2, axis=3)
    factor = jnp.stack([box_phase[0], -box_phase[1]])
    child_local = translate(child_out, sources_child, kinds_child, table_child)
    return complex_times(expanded, factor) + child_local
```

```python
import functools
import math

import jax
import jax.numpy as jnp
import numpy as np
from jax import lax
from jax.experimental import pallas as pl
from jax.experimental.pallas import tpu as pltpu
from jax.sharding import PartitionSpec as P

BAND1 = 180
WAVE = BAND1 / (2.0 * math.sqrt(3.0))
LANES = 128
MIB = 1 << 20
F32 = jnp.float32
BF16 = jnp.bfloat16


def round_up(count, step):
    return -(-count // step) * step


def stencil_entries(count_out, count_in, centered, out_rows):
    entries = []
    for row_out in out_rows:
        if centered:
            numerator = (2 * row_out + 1) * count_in - count_out
        else:
            numerator = 2 * row_out * count_in
        denominator = 2 * count_out
        base_index = numerator // denominator
        fraction = (numerator - base_index * denominator) / denominator
        for offset_a in range(-2, 4):
            weight = 1.0
            for offset_b in range(-2, 4):
                if offset_b != offset_a:
                    weight = weight * (fraction - offset_b) / (offset_a - offset_b)
            entries.append((row_out, base_index + offset_a, weight))
    return entries


def local_up(count_out, count_in, centered, rows_out, rows_in, below, shape):
    matrix = np.zeros(shape)
    for row_out, column, weight in stencil_entries(count_out, count_in, centered, range(rows_out)):
        assert -below <= column < rows_in + 3 or abs(weight) < 1e-12
        if column >= 0:
            matrix[row_out, column] += weight
        elif column >= -below:
            matrix[row_out, rows_in + 3 + below + column] += weight
    return matrix.astype(np.float32)


def split(x):
    high = x.astype(BF16)
    return high, (x - high.astype(F32)).astype(BF16)


def split_constant(matrix):
    high = matrix.astype(jnp.bfloat16)
    return high, (matrix - high.astype(np.float32)).astype(jnp.bfloat16)


def dot(a, b):
    return jnp.dot(a, b, preferred_element_type=F32)


def dot_transposed(a, b):
    return lax.dot_general(a, b, (((1,), (1,)), ((), ())), preferred_element_type=F32)


def local_kernel(entries, child_ref, table_ref, source_ref, kind_ref, *rest):
    out_ref = rest[-1]
    rows, columns = child_ref.shape[1], child_ref.shape[2]

    def one_tile(step, carry):
        row = step // (columns // 8)
        at = pl.ds(pl.multiple_of(step % (columns // 8) * 8, 8), 8)
        pattern = [child_ref[c, row, at, :] for c in range(8)]
        table = [table_ref[c, row, at, :] for c in range(2)]
        total = [None] * 8
        for entry in range(entries):
            source, kind = source_ref[entry], kind_ref[entry]
            real, imag = (jnp.take_along_axis(t, kind, axis=1, mode="promise_in_bounds") for t in table)
            for c in range(4):
                x = jnp.take_along_axis(pattern[c], source, axis=1, mode="promise_in_bounds")
                y = jnp.take_along_axis(pattern[4 + c], source, axis=1, mode="promise_in_bounds")
                re = x * real - y * imag
                im = x * imag + y * real
                total[c] = re if entry == 0 else total[c] + re
                total[4 + c] = im if entry == 0 else total[4 + c] + im
        for c in range(8):
            out_ref[c, row, at, :] = total[c]
        return carry

    lax.fori_loop(0, rows * (columns // 8), one_tile, 0)


def child_translate(child_out, table, sources, kinds, first, count, onto):
    _, rows, columns, boxes = child_out.shape
    entries = sources.shape[0]
    block = next(b for b in (4, 3, 2, 1) if count % b == 0 and first % b == 0)
    at = first // block

    def place(i):
        return (0, at + i, 0, 0)

    whole = pl.BlockSpec((entries, 8, boxes), lambda i: (0, 0, 0))
    in_specs = [
        pl.BlockSpec((8, block, columns, boxes), place),
        pl.BlockSpec((2, block, columns, boxes), place),
        whole,
        whole,
    ]
    operands = [child_out, table, sources, kinds]
    aliases = {}
    if onto is not None:
        in_specs.append(pl.BlockSpec(memory_space=pl.ANY))
        operands.append(onto)
        aliases = {4: 0}
    samples = count * columns * boxes
    return pl.pallas_call(
        functools.partial(local_kernel, entries),
        grid=(count // block,),
        in_specs=in_specs,
        out_specs=pl.BlockSpec((8, block, columns, boxes), place),
        out_shape=jax.ShapeDtypeStruct(child_out.shape, F32),
        input_output_aliases=aliases,
        compiler_params=pltpu.CompilerParams(vmem_limit_bytes=40 * MIB),
        cost_estimate=pl.CostEstimate(
            flops=samples * entries * 32, bytes_accessed=samples * 72, transcendentals=0
        ),
        name="child_translate",
    )(*operands)


def parent_kernel(
    sizes,
    source_ref,
    kind_ref,
    child_ref,
    next_ref,
    previous_ref,
    side_ref,
    table_ref,
    combine_ref,
    polar_cos_ref,
    polar_sin_ref,
    azimuth_up_ref,
    polar_down_ref,
    azimuth_down_ref,
    phase_ref,
    out_ref,
    wide,
    rows_done,
    table_by_kind,
    parent_out,
    in_high,
    in_low,
    lowered,
):
    (rows, columns, rows_up, columns_up, parents, entries, table_steps, table_rows) = sizes
    t_pad, p_pad, f_pad, q_pad = wide.shape[1] // 128, parent_out.shape[3], wide.shape[2], parent_out.shape[4]
    step = pl.program_id(0)
    half = 4 * parents

    @pl.when(step == 0)
    def _():
        for part in range(2):
            for t in range(rows + 6, t_pad):
                wide[part, pl.ds(t, 128, stride=t_pad), :] = jnp.zeros((128, f_pad), F32)
        for part in range(2):
            for p in range(rows_up, p_pad):
                for lane in range(0, q_pad, LANES):
                    table_by_kind[lane // LANES, pl.ds(part * p_pad + p, 128, stride=2 * p_pad), :] = jnp.zeros(
                        (128, LANES), F32
                    )

    @pl.when(step < table_steps)
    def _():
        def one_row(r, carry):
            for part in range(2):
                x = table_ref[part, r]
                if q_pad > columns_up:
                    x = jnp.concatenate([x, jnp.zeros((q_pad - columns_up, LANES), F32)], axis=0)
                for lane in range(0, q_pad, LANES):
                    turned = x[lane : lane + LANES].T
                    at = pl.ds(part * p_pad + step * table_rows + r, 128, stride=2 * p_pad)
                    table_by_kind[lane // LANES, at, :] = turned
            return carry

        lax.fori_loop(0, table_rows, one_row, 0)

    combine = combine_ref[...]

    def turn(main_ref, r, t):
        for part in range(2):
            x = jnp.concatenate(
                [
                    main_ref[part, 0, r],
                    side_ref[part, 0, t],
                    jnp.zeros((f_pad - columns - 8, LANES), F32),
                ],
                axis=0,
            )
            high, low = split(x)
            wide[part, pl.ds(t, 128, stride=t_pad), :] = dot_transposed(
                combine, jnp.concatenate([high, low], axis=1)
            )

    def main_row(r, carry):
        turn(child_ref, r, r)
        return carry

    def edge_row(r, carry):
        turn(next_ref, r, rows + r)
        turn(previous_ref, r, rows + 3 + r)
        return carry

    lax.fori_loop(0, rows, main_row, 0)
    lax.fori_loop(0, 3, edge_row, 0)

    polar = []
    for sign in (-1.0, 1.0):
        both = jnp.concatenate([polar_cos_ref[...], sign * polar_sin_ref[...]], axis=1)
        high, low = split(both)
        polar.append(jnp.concatenate([high, high, low], axis=1))
    azimuth = azimuth_up_ref[...]
    for part in range(2):
        for kind in range(2):
            for difference in range(2):
                first = (kind * 2 + difference) * parents

                def one_pair(pair, carry, part=part, first=first):
                    at = first + 2 * pair
                    stacked = []
                    for source, offset in ((part, 0), (1 - part, half)):
                        stacked.append(
                            jnp.concatenate(
                                [
                                    wide[source, pl.ds(pl.multiple_of((offset + at + i) * t_pad, 8), t_pad), :]
                                    for i in range(2)
                                ],
                                axis=1,
                            )
                        )
                    high, low = split(jnp.concatenate(stacked, axis=0))
                    result = dot(polar[part], jnp.concatenate([high, low, high], axis=0))
                    high, low = split(result)
                    for i in range(2):
                        lanes = slice(i * f_pad, (i + 1) * f_pad)
                        rows_done[pl.ds(pl.multiple_of((2 * pair + i) * p_pad, 16), p_pad), :] = jnp.concatenate(
                            [high[:, lanes], low[:, lanes], high[:, lanes]], axis=1
                        )
                    return carry

                lax.fori_loop(0, parents // 2, one_pair, 0)
                target = part if difference == 0 else 1 - part
                phase = phase_ref[2 * kind + difference]
                if difference == 1 and part == 1:
                    phase = -phase
                fresh = kind == 0 and difference == part

                starts = kind == 0 and part == 0

                def one_group(group, carry, target=target, phase=phase, starts=starts):
                    per = 4
                    x = rows_done[pl.ds(pl.multiple_of(group * per * p_pad, 16), per * p_pad), :]
                    y = dot(x, azimuth)
                    for i in range(per):
                        term = y[i * p_pad : (i + 1) * p_pad] * phase
                        if starts:
                            parent_out[target, step, group * per + i] = term
                        else:
                            parent_out[target, step, group * per + i] += term
                    return carry

                lax.fori_loop(0, parents // 4, one_group, 0)

    @pl.when(step == 3)
    def _():
        tiles = q_pad // LANES

        def one_tile(tile, carry):
            box = tile // (p_pad // 16)
            row = tile % (p_pad // 16) * 16
            sources = [source_ref[box, e] for e in range(entries)]
            kinds = [kind_ref[box, e] * (2 * p_pad) + row for e in range(entries)]
            for lane_tile in range(tiles):
                lanes = slice(lane_tile * LANES, (lane_tile + 1) * LANES)
                total = [None] * 8
                for e in range(entries):
                    real = table_by_kind[lane_tile, pl.ds(pl.multiple_of(kinds[e], 16), 16), :]
                    imag = table_by_kind[lane_tile, pl.ds(pl.multiple_of(kinds[e] + p_pad, 16), 16), :]
                    for c in range(4):
                        x = parent_out[0, c, sources[e], pl.ds(pl.multiple_of(row, 16), 16), lanes]
                        y = parent_out[1, c, sources[e], pl.ds(pl.multiple_of(row, 16), 16), lanes]
                        re = x * real - y * imag
                        im = x * imag + y * real
                        total[c] = re if e == 0 else total[c] + re
                        total[4 + c] = im if e == 0 else total[4 + c] + im
                for c in range(8):
                    high, low = split(total[c])
                    at = pl.ds(pl.multiple_of((c * parents + box) * p_pad + row, 16), 16)
                    in_high[at, lanes] = high
                    in_low[at, lanes] = low
            return carry

        lax.fori_loop(0, parents * (p_pad // 16), one_tile, 0)

        down = azimuth_down_ref[...]
        down_high = down[:, :f_pad]
        high, low = split(polar_down_ref[...])
        polar_back = jnp.concatenate([high, high, low], axis=1)
        per = 4

        def one_group(group, carry):
            at = pl.ds(pl.multiple_of(group * per * p_pad, 16), per * p_pad)
            high = in_high[at, :]
            low = in_low[at, :]
            both = dot(high, down)
            y = both[:, :f_pad] + both[:, f_pad:] + dot(low, down_high)
            for i in range(0, per, 2):
                x = jnp.concatenate([y[i * p_pad : (i + 1) * p_pad], y[(i + 1) * p_pad : (i + 2) * p_pad]], axis=1)
                high, low = split(x)
                z = dot(polar_back, jnp.concatenate([high, low, high], axis=0))
                for j in range(2):
                    lowered[pl.ds(pl.multiple_of((group * per + i + j) * t_pad, 8), t_pad), :] = z[
                        :, j * f_pad : (j + 1) * f_pad
                    ]
            return carry

        lax.fori_loop(0, 8 * parents // per, one_group, 0)

        def one_row(t, carry):
            turned = lowered[pl.ds(t, 8 * parents, stride=t_pad), :].T
            out_ref[t] = turned[: columns + 8]
            return carry

        lax.fori_loop(0, rows + 6, one_row, 0)


def parent_level(child_out, after, before, side, table, sources, kinds, combine, polar_cos, polar_sin, phase):
    _, rows, columns, boxes = child_out.shape
    _, rows_up, columns_up, translators = table.shape
    assert boxes == LANES and translators == LANES
    parents, entries = sources.shape
    t_pad, p_pad = polar_cos.shape[1], polar_cos.shape[0]
    f_pad, q_pad = round_up(columns + 8, LANES), round_up(columns_up, LANES)
    assert f_pad == LANES
    table_steps = next(s for s in (4, 2, 1) if rows_up % s == 0)
    table_rows = rows_up // table_steps
    n_theta, n_phi = lax.axis_size("theta"), lax.axis_size("phi")
    polar_up = local_up(rows_up * n_theta, rows * n_theta, True, rows_up, rows, 3, (p_pad, t_pad))
    azimuth_up = local_up(columns_up * n_phi, columns * n_phi, False, columns_up, columns, 2, (q_pad, f_pad))
    high, low = split_constant(np.ascontiguousarray(azimuth_up.T))
    azimuth_three = jnp.asarray(np.concatenate([high, high, low], axis=0))
    high, low = split_constant(azimuth_up)
    azimuth_down = jnp.asarray(np.concatenate([high, low], axis=1))
    polar_down = jnp.asarray(np.ascontiguousarray(polar_up.T))

    def whole(array):
        return pl.BlockSpec(array.shape, lambda g: (0,) * array.ndim)

    def channel(shape):
        return pl.BlockSpec((2, 1) + shape, lambda g: (0, g, 0, 0, 0))

    smem = pl.BlockSpec(memory_space=pltpu.SMEM)
    constants = [combine, polar_cos, polar_sin, azimuth_three, polar_down, azimuth_down, phase]
    return pl.pallas_call(
        functools.partial(
            parent_kernel, (rows, columns, rows_up, columns_up, parents, entries, table_steps, table_rows)
        ),
        grid=(4,),
        in_specs=[
            smem,
            smem,
            channel((rows, columns, boxes)),
            channel((3, columns, boxes)),
            channel((3, columns, boxes)),
            channel((rows + 6, 8, boxes)),
            pl.BlockSpec(
                (2, table_rows, columns_up, translators), lambda g: (0, jnp.minimum(g, table_steps - 1), 0, 0)
            ),
        ]
        + [whole(c) for c in constants],
        out_specs=pl.BlockSpec((rows + 6, columns + 8, 8 * parents), lambda g: (0, 0, 0)),
        out_shape=jax.ShapeDtypeStruct((rows + 6, columns + 8, 8 * parents), F32),
        scratch_shapes=[
            pltpu.VMEM((2, 128 * t_pad, f_pad), F32),
            pltpu.VMEM((parents * p_pad, 3 * f_pad), BF16),
            pltpu.VMEM((q_pad // LANES, translators * 2 * p_pad, LANES), F32),
            pltpu.VMEM((2, 4, parents, p_pad, q_pad), F32),
            pltpu.VMEM((8 * parents * p_pad, q_pad), BF16),
            pltpu.VMEM((8 * parents * p_pad, q_pad), BF16),
            pltpu.VMEM((8 * parents * t_pad, f_pad), F32),
        ],
        compiler_params=pltpu.CompilerParams(vmem_limit_bytes=60 * MIB),
        cost_estimate=pl.CostEstimate(
            flops=20_000_000_000, bytes_accessed=child_out.size * 8, transcendentals=0
        ),
        name="parent_level",
    )(
        sources,
        kinds,
        child_out.reshape((2, 4) + child_out.shape[1:]),
        after.reshape((2, 4) + after.shape[1:]),
        before.reshape((2, 4) + before.shape[1:]),
        side.reshape((2, 4) + side.shape[1:]),
        table,
        *constants,
    )


def final_kernel(local_ref, lowered_ref, phase_ref, parent_ref, octant_ref, out_ref):
    rows, columns = local_ref.shape[1], local_ref.shape[2]

    def one_row(row, carry):
        phase = phase_ref[row]
        turned = jnp.concatenate([phase, jnp.zeros((LANES - 16, phase.shape[1]), F32)], axis=0).T
        for tile in range(columns // 8):
            at = slice(tile * 8, tile * 8 + 8)
            cosine = jnp.take_along_axis(turned[at], octant_ref[0], axis=1, mode="promise_in_bounds")
            sine = jnp.take_along_axis(turned[at], octant_ref[1], axis=1, mode="promise_in_bounds")
            lowered = lowered_ref[row, at]
            for c in range(4):
                x = jnp.take_along_axis(lowered, parent_ref[c], axis=1, mode="promise_in_bounds")
                y = jnp.take_along_axis(lowered, parent_ref[4 + c], axis=1, mode="promise_in_bounds")
                out_ref[c, row, at] = local_ref[c, row, at] + (x * cosine + y * sine)
                out_ref[4 + c, row, at] = local_ref[4 + c, row, at] + (y * cosine - x * sine)
        return carry

    lax.fori_loop(0, rows, one_row, 0)


def final_sum(local, lowered, phase, parent_lanes, octant_lanes):
    _, rows, columns, boxes = local.shape
    block = next(b for b in (4, 3, 2, 1) if rows % b == 0)
    patterns = pl.BlockSpec((8, block, columns, boxes), lambda i: (0, i, 0, 0))
    return pl.pallas_call(
        final_kernel,
        grid=(rows // block,),
        in_specs=[
            patterns,
            pl.BlockSpec((block, columns, lowered.shape[2]), lambda i: (i, 0, 0)),
            pl.BlockSpec((block,) + phase.shape[1:], lambda i: (i, 0, 0)),
            pl.BlockSpec(parent_lanes.shape, lambda i: (0, 0, 0)),
            pl.BlockSpec(octant_lanes.shape, lambda i: (0, 0, 0)),
        ],
        out_specs=patterns,
        out_shape=jax.ShapeDtypeStruct(local.shape, F32),
        input_output_aliases={0: 0},
        compiler_params=pltpu.CompilerParams(vmem_limit_bytes=40 * MIB),
        cost_estimate=pl.CostEstimate(flops=local.size * 4, bytes_accessed=local.size * 9, transcendentals=0),
        name="final_sum",
    )(local, lowered, phase, parent_lanes, octant_lanes)


def chain(count, periodic):
    pairs = [(i, i + 1) for i in range(count - 1)]
    return pairs + [(count - 1, 0)] if periodic else pairs


def send(block, axis, up):
    pairs = chain(lax.axis_size(axis), axis == "phi")
    return lax.ppermute(block, axis, pairs if up else [(b, a) for a, b in pairs])


def angles(count, all_count, axis, centered):
    index = jnp.arange(count, dtype=jnp.int32) + lax.axis_index(axis) * count
    if centered:
        return (index.astype(F32) + 0.5) * (math.pi / all_count)
    return index.astype(F32) * (2.0 * math.pi / all_count)


def padded(array, shape):
    return jnp.pad(array, [(0, n - m) for m, n in zip(array.shape, shape)])


def per_device(
    child_out,
    child_slot,
    sources_child,
    kinds_child,
    table_child,
    sources_parent,
    kinds_parent,
    table_parent,
):
    _, rows, columns, boxes = child_out.shape
    _, rows_up, columns_up, _ = table_parent.shape
    parents = boxes // 8
    n_theta, n_phi = lax.axis_size("theta"), lax.axis_size("phi")
    t_pad, p_pad = round_up(rows + 6, 16), round_up(rows_up, 16)
    q_pad = round_up(columns_up, LANES)

    after = send(child_out[:, :3], "theta", False)
    before = send(child_out[:, rows - 3 :], "theta", True)
    right = send(child_out[:, :, :3], "phi", False)
    left = send(child_out[:, :, columns - 2 :], "phi", True)
    poles = jnp.concatenate([after, before], axis=1)
    right_poles = send(poles[:, :, :3], "phi", False)
    left_poles = send(poles[:, :, columns - 2 :], "phi", True)
    side = jnp.concatenate(
        [
            jnp.concatenate([right, right_poles], axis=1),
            jnp.concatenate([left, left_poles], axis=1),
            jnp.zeros((8, rows + 6, 3, boxes), F32),
        ],
        axis=2,
    )

    parent_of = child_slot % parents
    octant_of = child_slot // parents
    east = 2 * (octant_of % 2) - 1
    north = 2 * (octant_of // 2 % 2) - 1
    upper = 2 * (octant_of // 4) - 1
    upper_weight = jnp.stack([jnp.ones_like(upper), upper])[:, None, None, None, :]
    alike = (jnp.arange(2)[:, None] == (east != north).astype(jnp.int32)[None, :])[None, :, None, None, :]
    east_weight = jnp.stack([jnp.ones_like(east), east])[None, None, :, None, :]
    same_parent = (jnp.arange(parents)[:, None] == parent_of[None, :])[None, None, None, :, :]
    combine = jnp.where(alike & same_parent, upper_weight * east_weight, 0).reshape(8 * parents, boxes).astype(BF16)
    combine = jnp.concatenate([combine, combine], axis=1)

    def spread(index):
        return jnp.broadcast_to(index.T[:, None, :], (index.shape[1], 8, index.shape[0])).astype(jnp.int32)

    component = jnp.arange(8, dtype=jnp.int32)
    parent_lanes = spread(parent_of[:, None] + component[None, :] * parents)
    octant_lanes = spread(octant_of[:, None] + jnp.array([[0, 8]], jnp.int32))

    polar = angles(rows_up, rows_up * n_theta, "theta", True)
    azimuth = angles(columns_up, columns_up * n_phi, "phi", False)
    upright = WAVE * jnp.cos(polar)
    polar_up = jnp.asarray(local_up(rows_up * n_theta, rows * n_theta, True, rows_up, rows, 3, (p_pad, t_pad)))
    polar_cos = polar_up * padded(jnp.cos(upright), (p_pad,))[:, None]
    polar_sin = polar_up * padded(jnp.sin(upright), (p_pad,))[:, None]
    flat = WAVE * jnp.sin(polar)[None, :, None]
    turned = jnp.stack([jnp.cos(azimuth) + jnp.sin(azimuth), jnp.cos(azimuth) - jnp.sin(azimuth)])[:, None, :]
    phase = flat * turned
    phase = jnp.stack([jnp.cos(phase), jnp.sin(phase)], axis=1).reshape(4, rows_up, columns_up)
    phase = padded(phase, (4, p_pad, q_pad))

    polar = angles(rows, rows * n_theta, "theta", True)[:, None, None]
    azimuth = angles(columns, columns * n_phi, "phi", False)[None, None, :]
    octant = jnp.arange(8, dtype=jnp.int32)[None, :, None]
    signs = [(2 * (octant // n % 2) - 1).astype(F32) for n in (1, 2, 4)]
    angle = WAVE * (
        jnp.sin(polar) * jnp.cos(azimuth) * signs[0]
        + jnp.sin(polar) * jnp.sin(azimuth) * signs[1]
        + jnp.cos(polar) * signs[2]
    )
    phase_child = padded(
        jnp.concatenate([jnp.cos(angle), jnp.sin(angle)], axis=1), (rows, 16, round_up(columns, LANES))
    )

    first = rows // 2
    sources, kinds = spread(sources_child), spread(kinds_child)
    local = child_translate(child_out, table_child, sources, kinds, 0, first, None)

    lowered = parent_level(
        child_out,
        after,
        before,
        side,
        table_parent,
        sources_parent,
        kinds_parent,
        combine,
        polar_cos,
        polar_sin,
        phase,
    )
    local, lowered = lax.optimization_barrier((local, lowered))

    low = send(lowered[rows : rows + 3], "theta", True)
    high = send(lowered[rows + 3 : rows + 6], "theta", False)
    here = lowered[:rows]
    here = here + jnp.pad(low, ((0, rows - 3), (0, 0), (0, 0))) + jnp.pad(high, ((rows - 3, 0), (0, 0), (0, 0)))
    low = send(here[:, columns : columns + 3], "phi", True)
    high = send(here[:, columns + 3 : columns + 5], "phi", False)
    here = here[:, :columns]
    here = here + jnp.pad(low, ((0, 0), (0, columns - 3), (0, 0))) + jnp.pad(high, ((0, 0), (columns - 2, 0), (0, 0)))

    local = child_translate(child_out, table_child, sources, kinds, first, rows - first, local)
    return final_sum(local, here, phase_child, parent_lanes, octant_lanes)


def solution(mesh):
    placed = (
        P(None, "theta", "phi", None),
        P(),
        P(),
        P(),
        P(None, "theta", "phi", None),
        P(),
        P(),
        P(None, "theta", "phi", None),
    )
    return jax.shard_map(
        per_device,
        mesh=mesh,
        in_specs=placed,
        out_specs=P(None, "theta", "phi", None),
        check_vma=False,
    )
```

```python
import functools
import math

import jax
import jax.numpy as jnp
import numpy as np
from jax import lax
from jax.experimental import pallas as pl
from jax.experimental.pallas import tpu as pltpu
from jax.sharding import PartitionSpec as P

BAND1 = 180
WAVE = BAND1 / (2.0 * math.sqrt(3.0))
LANES = 128
MIB = 1 << 20
F32 = jnp.float32
BF16 = jnp.bfloat16


def round_up(count, step):
    return -(-count // step) * step


def stencil_entries(count_out, count_in, centered, out_rows):
    entries = []
    for row_out in out_rows:
        if centered:
            numerator = (2 * row_out + 1) * count_in - count_out
        else:
            numerator = 2 * row_out * count_in
        denominator = 2 * count_out
        base_index = numerator // denominator
        fraction = (numerator - base_index * denominator) / denominator
        for offset_a in range(-2, 4):
            weight = 1.0
            for offset_b in range(-2, 4):
                if offset_b != offset_a:
                    weight = weight * (fraction - offset_b) / (offset_a - offset_b)
            entries.append((row_out, base_index + offset_a, weight))
    return entries


def local_up(count_out, count_in, centered, rows_out, rows_in, below, shape):
    matrix = np.zeros(shape)
    for row_out, column, weight in stencil_entries(count_out, count_in, centered, range(rows_out)):
        assert -below <= column < rows_in + 3 or abs(weight) < 1e-12
        if column >= 0:
            matrix[row_out, column] += weight
        elif column >= -below:
            matrix[row_out, rows_in + 3 + below + column] += weight
    return matrix.astype(np.float32)


def split(x):
    high = x.astype(BF16)
    return high, (x - high.astype(F32)).astype(BF16)


def split_constant(matrix):
    high = matrix.astype(jnp.bfloat16)
    return high, (matrix - high.astype(np.float32)).astype(jnp.bfloat16)


def dot(a, b):
    return jnp.dot(a, b, preferred_element_type=F32)


def dot_transposed(a, b):
    return lax.dot_general(a, b, (((1,), (1,)), ((), ())), preferred_element_type=F32)


def segments(samples):
    full, rest = divmod(samples, 8 * LANES)
    found = [(0, full, 1, 8)] if full else []
    if rest:
        rows = -(-rest // LANES)
        packed = 4 if rows <= 2 else 2 if rows <= 4 else 1
        found.append((full, 1, packed, rows))
    return found


def lie_across(from_rows, to_tiles, plane, offsets, row):
    turned = from_rows.T
    for offset in offsets:
        to_tiles[plane, pl.ds(offset + row, LANES, stride=8), :] = turned


def translate_kernel(entries, packed, rows, source_ref, kind_ref, child_ref, table_ref, out_ref, pattern, table):
    groups, per = 4 // packed, 8 // packed

    for row in range(rows):
        at = slice(row * LANES, (row + 1) * LANES)
        for part in range(2):
            lie_across(table_ref[part, at], table, part, [c * per for c in range(packed)], row)

    def one_channel(c, carry):
        for part in range(2):
            for row in range(rows):
                lie_across(
                    child_ref[part, c, row * LANES : (row + 1) * LANES],
                    pattern,
                    part * groups + c // packed,
                    [c % packed * per],
                    row,
                )
        return carry

    lax.fori_loop(0, 4, one_channel, 0)

    def one_box(box, carry):
        total = [None] * (2 * groups)
        for entry in range(entries):
            source = pl.ds(pl.multiple_of(source_ref[box * entries + entry], 8), 8)
            kind = pl.ds(pl.multiple_of(kind_ref[box * entries + entry], 8), 8)
            real, imag = table[0, kind, :], table[1, kind, :]
            for g in range(groups):
                x, y = pattern[g, source, :], pattern[groups + g, source, :]
                re = x * real - y * imag
                im = x * imag + y * real
                total[g] = re if entry == 0 else total[g] + re
                total[groups + g] = im if entry == 0 else total[groups + g] + im
        for g in range(2 * groups):
            out_ref[0, g, pl.ds(pl.multiple_of(box * 8, 8), 8), :] = total[g]
        return carry

    lax.fori_loop(0, LANES, one_box, 0, unroll=2)


def child_translate(child, table, sources, kinds, segment):
    first, count, packed, rows = segment
    entries = sources.shape[0] // LANES
    planes = 8 // packed
    smem = pl.BlockSpec(memory_space=pltpu.SMEM)
    work = count * rows * LANES * LANES
    return pl.pallas_call(
        functools.partial(translate_kernel, entries, packed, rows),
        grid=(count,),
        in_specs=[
            smem,
            smem,
            pl.BlockSpec((2, 4, 8 * LANES, LANES), lambda i: (0, 0, first + i, 0)),
            pl.BlockSpec((2, 8 * LANES, LANES), lambda i: (0, first + i, 0)),
        ],
        out_specs=pl.BlockSpec((1, planes, 8 * LANES, LANES), lambda i: (i, 0, 0, 0)),
        out_shape=jax.ShapeDtypeStruct((count, planes, 8 * LANES, LANES), F32),
        scratch_shapes=[
            pltpu.VMEM((planes, 8 * LANES, LANES), F32),
            pltpu.VMEM((2, 8 * LANES, LANES), F32),
        ],
        compiler_params=pltpu.CompilerParams(vmem_limit_bytes=60 * MIB),
        cost_estimate=pl.CostEstimate(flops=work * entries * 32, bytes_accessed=work * 72, transcendentals=0),
        name="child_translate",
    )(sources, kinds, child, table)


def sum_kernel(packed, rows, parents, parent_ref, octant_ref, local_ref, lowered_ref, phase_ref, *rest):
    out_ref, lowered, total = rest[-3:]
    groups, per = 4 // packed, 8 // packed

    for row in range(rows):
        lie_across(lowered_ref[row * LANES : (row + 1) * LANES], lowered, 0, [0], row)

    def one_box(box, carry):
        parent = parent_ref[box]
        octant = octant_ref[box]
        cosine, sine = phase_ref[octant], phase_ref[8 + octant]
        here = pl.ds(pl.multiple_of(box * 8, 8), 8)
        for c in range(4):
            x = lowered[0, pl.ds(pl.multiple_of(parent + c * parents * 8, 8), 8), :][:per]
            y = lowered[0, pl.ds(pl.multiple_of(parent + (4 + c) * parents * 8, 8), 8), :][:per]
            re = x * cosine[:per] + y * sine[:per]
            im = y * cosine[:per] - x * sine[:per]
            if packed == 1:
                total[c, here, :] = local_ref[0, c, here, :] + re
                total[4 + c, here, :] = local_ref[0, 4 + c, here, :] + im
            else:
                here = pl.ds(pl.multiple_of(box * 8, 8) + c % packed * per, per)
                total[c // packed, here, :] = local_ref[0, c // packed, here, :] + re
                total[groups + c // packed, here, :] = local_ref[0, groups + c // packed, here, :] + im
        return carry

    lax.fori_loop(0, LANES, one_box, 0, unroll=4)

    def one_channel(c, carry):
        for part in range(2):
            for row in range(rows):
                turned = total[part * groups + c // packed, pl.ds(c % packed * per + row, LANES, stride=8), :].T
                out_ref[part, c, row * LANES : (row + 1) * LANES] = turned
        return carry

    lax.fori_loop(0, 4, one_channel, 0)


def final_sum(shape, local, lowered, phase, parent, octant, segment, onto):
    first, count, packed, rows = segment
    planes = 8 // packed
    smem = pl.BlockSpec(memory_space=pltpu.SMEM)
    in_specs = [
        smem,
        smem,
        pl.BlockSpec((1, planes, 8 * LANES, LANES), lambda i: (i, 0, 0, 0)),
        pl.BlockSpec((8 * LANES, LANES), lambda i: (first + i, 0)),
        pl.BlockSpec((16, 8, LANES), lambda i: (0, first + i, 0)),
    ]
    operands = [parent, octant, local, lowered, phase]
    aliases = {}
    if onto is not None:
        in_specs.append(pl.BlockSpec(memory_space=pl.ANY))
        operands.append(onto)
        aliases = {5: 0}
    work = count * rows * LANES * LANES
    return pl.pallas_call(
        functools.partial(sum_kernel, packed, rows, LANES // 8),
        grid=(count,),
        in_specs=in_specs,
        out_specs=pl.BlockSpec((2, 4, 8 * LANES, LANES), lambda i: (0, 0, first + i, 0)),
        out_shape=jax.ShapeDtypeStruct(shape, F32),
        input_output_aliases=aliases,
        scratch_shapes=[
            pltpu.VMEM((1, 8 * LANES, LANES), F32),
            pltpu.VMEM((planes, 8 * LANES, LANES), F32),
        ],
        compiler_params=pltpu.CompilerParams(vmem_limit_bytes=60 * MIB),
        cost_estimate=pl.CostEstimate(flops=work * 32, bytes_accessed=work * 72, transcendentals=0),
        name="final_sum",
    )(*operands)


def parent_kernel(
    sizes,
    source_ref,
    kind_ref,
    child_ref,
    next_ref,
    previous_ref,
    side_ref,
    table_ref,
    combine_ref,
    polar_cos_ref,
    polar_sin_ref,
    azimuth_up_ref,
    polar_down_ref,
    azimuth_down_ref,
    phase_ref,
    out_ref,
    wide,
    rows_done,
    table_by_kind,
    parent_out,
    in_high,
    in_low,
    lowered,
):
    (rows, columns, rows_up, columns_up, parents, entries, table_steps, table_rows) = sizes
    t_pad, p_pad, f_pad, q_pad = wide.shape[1] // 128, parent_out.shape[3], wide.shape[2], parent_out.shape[4]
    step = pl.program_id(0)
    half = 4 * parents

    @pl.when(step == 0)
    def _():
        for part in range(2):
            for t in range(rows + 6, t_pad):
                wide[part, pl.ds(t, 128, stride=t_pad), :] = jnp.zeros((128, f_pad), F32)
        for part in range(2):
            for p in range(rows_up, p_pad):
                for lane in range(0, q_pad, LANES):
                    table_by_kind[lane // LANES, pl.ds(part * p_pad + p, 128, stride=2 * p_pad), :] = jnp.zeros(
                        (128, LANES), F32
                    )

    @pl.when(step < table_steps)
    def _():
        for r in range(table_rows):
            for part in range(2):
                x = table_ref[part, r]
                if q_pad > columns_up:
                    x = jnp.concatenate([x, jnp.zeros((q_pad - columns_up, LANES), F32)], axis=0)
                for lane in range(0, q_pad, LANES):
                    turned = x[lane : lane + LANES].T
                    at = pl.ds(part * p_pad + step * table_rows + r, 128, stride=2 * p_pad)
                    table_by_kind[lane // LANES, at, :] = turned

    combine = combine_ref[...]

    def samples(part, main_ref, r, t):
        x = jnp.concatenate(
            [main_ref[part, 0, r], side_ref[part, 0, t], jnp.zeros((f_pad - columns - 8, LANES), F32)], axis=0
        )
        high, low = split(x)
        return jnp.concatenate([high, low], axis=1)

    def turn(pieces):
        for part in range(2):
            for i in range(0, len(pieces), 2):
                both = jnp.concatenate([samples(part, *piece) for piece in pieces[i : i + 2]], axis=0)
                turned = dot_transposed(combine, both)
                for j, piece in enumerate(pieces[i : i + 2]):
                    at = pl.ds(piece[2], 128, stride=t_pad)
                    wide[part, at, :] = turned[:, j * f_pad : (j + 1) * f_pad]

    per_turn = next(n for n in (4, 3, 2, 1) if rows % n == 0)

    def main_rows(i, carry):
        turn([(child_ref, per_turn * i + r, per_turn * i + r) for r in range(per_turn)])
        return carry

    lax.fori_loop(0, rows // per_turn, main_rows, 0)
    turn([(next_ref, r, rows + r) for r in range(3)] + [(previous_ref, r, rows + 3 + r) for r in range(3)])

    polar = []
    for sign in (-1.0, 1.0):
        both = jnp.concatenate([polar_cos_ref[...], sign * polar_sin_ref[...]], axis=1)
        high, low = split(both)
        polar.append(jnp.concatenate([high, high, low], axis=1))
    azimuth = azimuth_up_ref[...]
    per = 4
    for target in range(2):
        for difference in range(2):
            part = target if difference == 0 else 1 - target

            def one_kind(kind, carry, part=part, difference=difference):
                first = (kind * 2 + difference) * parents
                for pair in range(parents // 2):
                    stacked = []
                    for source, offset in ((part, 0), (1 - part, half)):
                        at = (offset + first + 2 * pair) * t_pad
                        stacked.append(
                            jnp.concatenate(
                                [wide[source, pl.ds(pl.multiple_of(at + i * t_pad, 8), t_pad), :] for i in range(2)],
                                axis=1,
                            )
                        )
                    high, low = split(jnp.concatenate(stacked, axis=0))
                    result = dot(polar[part], jnp.concatenate([high, low, high], axis=0))
                    high, low = split(result)
                    for i in range(2):
                        lanes = slice(i * f_pad, (i + 1) * f_pad)
                        rows_done[kind * 2 + difference, pl.ds((2 * pair + i) * p_pad, p_pad), :] = jnp.concatenate(
                            [high[:, lanes], low[:, lanes], high[:, lanes]], axis=1
                        )
                return carry

            lax.fori_loop(0, 2, one_kind, 0)

        def one_group(group, carry, target=target):
            at = pl.ds(pl.multiple_of(group * per * p_pad, 16), per * p_pad)
            y = dot(jnp.concatenate([rows_done[k, at, :] for k in range(4)], axis=0), azimuth)
            for i in range(per):
                terms = [y[(k * per + i) * p_pad : (k * per + i + 1) * p_pad] * phase_ref[k] for k in range(4)]
                if target == 0:
                    value = (terms[0] - terms[1]) + (terms[2] - terms[3])
                else:
                    value = (terms[0] + terms[1]) + (terms[2] + terms[3])
                parent_out[target, step, group * per + i] = value
            return carry

        lax.fori_loop(0, parents // per, one_group, 0)

    @pl.when(step == 3)
    def _():
        tiles = q_pad // LANES

        def one_tile(tile, carry):
            box = tile // (p_pad // 16)
            row = tile % (p_pad // 16) * 16
            sources = [source_ref[box, e] for e in range(entries)]
            kinds = [kind_ref[box, e] * (2 * p_pad) + row for e in range(entries)]
            for lane_tile in range(tiles):
                lanes = slice(lane_tile * LANES, (lane_tile + 1) * LANES)
                total = [None] * 8
                for e in range(entries):
                    real = table_by_kind[lane_tile, pl.ds(pl.multiple_of(kinds[e], 16), 16), :]
                    imag = table_by_kind[lane_tile, pl.ds(pl.multiple_of(kinds[e] + p_pad, 16), 16), :]
                    for c in range(4):
                        x = parent_out[0, c, sources[e], pl.ds(pl.multiple_of(row, 16), 16), lanes]
                        y = parent_out[1, c, sources[e], pl.ds(pl.multiple_of(row, 16), 16), lanes]
                        re = x * real - y * imag
                        im = x * imag + y * real
                        total[c] = re if e == 0 else total[c] + re
                        total[4 + c] = im if e == 0 else total[4 + c] + im
                for c in range(8):
                    high, low = split(total[c])
                    at = pl.ds(pl.multiple_of((c * parents + box) * p_pad + row, 16), 16)
                    in_high[at, lanes] = high
                    in_low[at, lanes] = low
            return carry

        lax.fori_loop(0, parents * (p_pad // 16), one_tile, 0)

        down = azimuth_down_ref[...]
        down_high = down[:, :f_pad]
        high, low = split(polar_down_ref[...])
        polar_back = jnp.concatenate([high, high, low], axis=1)
        per = parents

        def one_group(group, carry):
            at = pl.ds(pl.multiple_of(group * per * p_pad, 16), per * p_pad)
            high = in_high[at, :]
            low = in_low[at, :]
            both = dot(high, down)
            y = both[:, :f_pad] + both[:, f_pad:] + dot(low, down_high)
            for i in range(0, per, 2):
                x = jnp.concatenate([y[i * p_pad : (i + 1) * p_pad], y[(i + 1) * p_pad : (i + 2) * p_pad]], axis=1)
                high, low = split(x)
                z = dot(polar_back, jnp.concatenate([high, low, high], axis=0))
                for j in range(2):
                    lowered[pl.ds(pl.multiple_of((group * per + i + j) * t_pad, 8), t_pad), :] = z[
                        :, j * f_pad : (j + 1) * f_pad
                    ]
            return carry

        lax.fori_loop(0, 8 * parents // per, one_group, 0)

        per_turn = next(n for n in (6, 5, 3, 2, 1) if (rows + 6) % n == 0)

        def some_rows(i, carry):
            for r in range(per_turn):
                turned = lowered[pl.ds(i * per_turn + r, 8 * parents, stride=t_pad), :].T
                out_ref[i * per_turn + r] = turned[: columns + 8]
            return carry

        lax.fori_loop(0, (rows + 6) // per_turn, some_rows, 0)


def parent_level(child_out, after, before, side, table, sources, kinds, combine, polar_cos, polar_sin, phase):
    _, rows, columns, boxes = child_out.shape
    _, rows_up, columns_up, translators = table.shape
    assert boxes == LANES and translators == LANES
    parents, entries = sources.shape
    t_pad, p_pad = polar_cos.shape[1], polar_cos.shape[0]
    f_pad, q_pad = round_up(columns + 8, LANES), round_up(columns_up, LANES)
    assert f_pad == LANES
    table_steps = next(s for s in (4, 2, 1) if rows_up % s == 0)
    table_rows = rows_up // table_steps
    n_theta, n_phi = lax.axis_size("theta"), lax.axis_size("phi")
    polar_up = local_up(rows_up * n_theta, rows * n_theta, True, rows_up, rows, 3, (p_pad, t_pad))
    azimuth_up = local_up(columns_up * n_phi, columns * n_phi, False, columns_up, columns, 2, (q_pad, f_pad))
    high, low = split_constant(np.ascontiguousarray(azimuth_up.T))
    azimuth_three = jnp.asarray(np.concatenate([high, high, low], axis=0))
    high, low = split_constant(azimuth_up)
    azimuth_down = jnp.asarray(np.concatenate([high, low], axis=1))
    polar_down = jnp.asarray(np.ascontiguousarray(polar_up.T))

    def whole(array):
        return pl.BlockSpec(array.shape, lambda g: (0,) * array.ndim)

    def channel(shape):
        return pl.BlockSpec((2, 1) + shape, lambda g: (0, g, 0, 0, 0))

    smem = pl.BlockSpec(memory_space=pltpu.SMEM)
    constants = [combine, polar_cos, polar_sin, azimuth_three, polar_down, azimuth_down, phase]
    return pl.pallas_call(
        functools.partial(
            parent_kernel, (rows, columns, rows_up, columns_up, parents, entries, table_steps, table_rows)
        ),
        grid=(4,),
        in_specs=[
            smem,
            smem,
            channel((rows, columns, boxes)),
            channel((3, columns, boxes)),
            channel((3, columns, boxes)),
            channel((rows + 6, 8, boxes)),
            pl.BlockSpec(
                (2, table_rows, columns_up, translators), lambda g: (0, jnp.minimum(g, table_steps - 1), 0, 0)
            ),
        ]
        + [whole(c) for c in constants],
        out_specs=pl.BlockSpec((rows + 6, columns + 8, 8 * parents), lambda g: (0, 0, 0)),
        out_shape=jax.ShapeDtypeStruct((rows + 6, columns + 8, 8 * parents), F32),
        scratch_shapes=[
            pltpu.VMEM((2, 128 * t_pad, f_pad), F32),
            pltpu.VMEM((4, parents * p_pad, 3 * f_pad), BF16),
            pltpu.VMEM((q_pad // LANES, translators * 2 * p_pad, LANES), F32),
            pltpu.VMEM((2, 4, parents, p_pad, q_pad), F32),
            pltpu.VMEM((8 * parents * p_pad, q_pad), BF16),
            pltpu.VMEM((8 * parents * p_pad, q_pad), BF16),
            pltpu.VMEM((8 * parents * t_pad, f_pad), F32),
        ],
        compiler_params=pltpu.CompilerParams(vmem_limit_bytes=60 * MIB),
        cost_estimate=pl.CostEstimate(
            flops=20_000_000_000, bytes_accessed=child_out.size * 8, transcendentals=0
        ),
        name="parent_level",
    )(
        sources,
        kinds,
        child_out.reshape((2, 4) + child_out.shape[1:]),
        after.reshape((2, 4) + after.shape[1:]),
        before.reshape((2, 4) + before.shape[1:]),
        side.reshape((2, 4) + side.shape[1:]),
        table,
        *constants,
    )


def chain(count, periodic):
    pairs = [(i, i + 1) for i in range(count - 1)]
    return pairs + [(count - 1, 0)] if periodic else pairs


def send(block, axis, up):
    pairs = chain(lax.axis_size(axis), axis == "phi")
    return lax.ppermute(block, axis, pairs if up else [(b, a) for a, b in pairs])


def send_diagonal(block, polar_step, azimuth_step):
    n_theta, n_phi = lax.axis_size("theta"), lax.axis_size("phi")
    pairs = [
        ((i + polar_step) * n_phi + (j + azimuth_step) % n_phi, i * n_phi + j)
        for i in range(n_theta)
        for j in range(n_phi)
        if 0 <= i + polar_step < n_theta
    ]
    return lax.ppermute(block, ("theta", "phi"), pairs)


def angles(count, all_count, axis, centered):
    index = jnp.arange(count, dtype=jnp.int32) + lax.axis_index(axis) * count
    if centered:
        return (index.astype(F32) + 0.5) * (math.pi / all_count)
    return index.astype(F32) * (2.0 * math.pi / all_count)


def padded(array, shape):
    return jnp.pad(array, [(0, n - m) for m, n in zip(array.shape, shape)])


def per_device(
    child_out,
    child_slot,
    sources_child,
    kinds_child,
    table_child,
    sources_parent,
    kinds_parent,
    table_parent,
):
    _, rows, columns, boxes = child_out.shape
    _, rows_up, columns_up, _ = table_parent.shape
    parents = boxes // 8
    n_theta, n_phi = lax.axis_size("theta"), lax.axis_size("phi")
    t_pad, p_pad = round_up(rows + 6, 16), round_up(rows_up, 16)
    q_pad = round_up(columns_up, LANES)

    after = send(child_out[:, :3], "theta", False)
    before = send(child_out[:, rows - 3 :], "theta", True)
    right = send(child_out[:, :, :3], "phi", False)
    left = send(child_out[:, :, columns - 2 :], "phi", True)
    corners = [
        [
            send_diagonal(child_out[:, at_rows, at_columns], polar_step, azimuth_step)
            for at_columns, azimuth_step in ((slice(0, 3), 1), (slice(columns - 2, columns), -1))
        ]
        for at_rows, polar_step in ((slice(0, 3), 1), (slice(rows - 3, rows), -1))
    ]
    side = jnp.concatenate(
        [
            jnp.concatenate([right, corners[0][0], corners[1][0]], axis=1),
            jnp.concatenate([left, corners[0][1], corners[1][1]], axis=1),
            jnp.zeros((8, rows + 6, 3, boxes), F32),
        ],
        axis=2,
    )

    parent_of = child_slot % parents
    octant_of = child_slot // parents
    east = 2 * (octant_of % 2) - 1
    north = 2 * (octant_of // 2 % 2) - 1
    upper = 2 * (octant_of // 4) - 1
    upper_weight = jnp.stack([jnp.ones_like(upper), upper])[:, None, None, None, :]
    alike = (jnp.arange(2)[:, None] == (east != north).astype(jnp.int32)[None, :])[None, :, None, None, :]
    east_weight = jnp.stack([jnp.ones_like(east), east])[None, None, :, None, :]
    same_parent = (jnp.arange(parents)[:, None] == parent_of[None, :])[None, None, None, :, :]
    combine = jnp.where(alike & same_parent, upper_weight * east_weight, 0).reshape(8 * parents, boxes).astype(BF16)
    combine = jnp.concatenate([combine, combine], axis=1)

    polar = angles(rows_up, rows_up * n_theta, "theta", True)
    azimuth = angles(columns_up, columns_up * n_phi, "phi", False)
    upright = WAVE * jnp.cos(polar)
    polar_up = jnp.asarray(local_up(rows_up * n_theta, rows * n_theta, True, rows_up, rows, 3, (p_pad, t_pad)))
    polar_cos = polar_up * padded(jnp.cos(upright), (p_pad,))[:, None]
    polar_sin = polar_up * padded(jnp.sin(upright), (p_pad,))[:, None]
    flat = WAVE * jnp.sin(polar)[None, :, None]
    turned = jnp.stack([jnp.cos(azimuth) + jnp.sin(azimuth), jnp.cos(azimuth) - jnp.sin(azimuth)])[:, None, :]
    phase = flat * turned
    phase = jnp.stack([jnp.cos(phase), jnp.sin(phase)], axis=1).reshape(4, rows_up, columns_up)
    phase = padded(phase, (4, p_pad, q_pad))

    samples = rows * columns
    sample_rows = -(-samples // LANES)
    sample = jnp.arange(sample_rows * LANES, dtype=jnp.int32).reshape(1, sample_rows, LANES)
    polar = (sample // columns + lax.axis_index("theta") * rows).astype(F32) + 0.5
    polar = polar * (math.pi / (rows * n_theta))
    azimuth = (sample % columns + lax.axis_index("phi") * columns).astype(F32)
    azimuth = azimuth * (2.0 * math.pi / (columns * n_phi))
    octant = jnp.arange(8, dtype=jnp.int32)[:, None, None]
    signs = [(2 * (octant // n % 2) - 1).astype(F32) for n in (1, 2, 4)]
    angle = WAVE * (
        jnp.sin(polar) * jnp.cos(azimuth) * signs[0]
        + jnp.sin(polar) * jnp.sin(azimuth) * signs[1]
        + jnp.cos(polar) * signs[2]
    )
    phase_child = jnp.concatenate([jnp.cos(angle), jnp.sin(angle)], axis=0)

    flat_child = child_out.reshape(2, 4, samples, boxes)
    flat_table = table_child.reshape(2, samples, table_child.shape[3])
    sources, kinds = sources_child.reshape(-1) * 8, kinds_child.reshape(-1) * 8
    pieces = segments(samples)
    local = [child_translate(flat_child, flat_table, sources, kinds, pieces[0])]

    lowered = parent_level(
        child_out,
        after,
        before,
        side,
        table_parent,
        sources_parent,
        kinds_parent,
        combine,
        polar_cos,
        polar_sin,
        phase,
    )
    lowered, flat_table = lax.optimization_barrier((lowered, flat_table))

    low = send(lowered[rows : rows + 3], "theta", True)
    high = send(lowered[rows + 3 : rows + 6], "theta", False)
    local += [child_translate(flat_child, flat_table, sources, kinds, piece) for piece in pieces[1:]]
    local, lowered = lax.optimization_barrier((local, lowered))
    here = lowered[:rows]
    here = here + jnp.pad(low, ((0, rows - 3), (0, 0), (0, 0))) + jnp.pad(high, ((rows - 3, 0), (0, 0), (0, 0)))
    low = send(here[:, columns : columns + 3], "phi", True)
    high = send(here[:, columns + 3 : columns + 5], "phi", False)
    here = here[:, :columns]
    here = here + jnp.pad(low, ((0, 0), (0, columns - 3), (0, 0))) + jnp.pad(high, ((0, 0), (columns - 2, 0), (0, 0)))
    here = here.reshape(samples, boxes)

    result = None
    for piece, part in zip(pieces, local):
        result = final_sum(
            flat_child.shape, part, here, phase_child, parent_of * 8, octant_of, piece, result
        )
    return result.reshape(child_out.shape)


def solution(mesh):
    placed = (
        P(None, "theta", "phi", None),
        P(),
        P(),
        P(),
        P(None, "theta", "phi", None),
        P(),
        P(),
        P(None, "theta", "phi", None),
    )
    return jax.shard_map(
        per_device,
        mesh=mesh,
        in_specs=placed,
        out_specs=P(None, "theta", "phi", None),
        check_vma=False,
    )
```

```python
import functools
import math

import jax
import jax.numpy as jnp
import numpy as np
from jax import lax
from jax.experimental import pallas as pl
from jax.experimental.pallas import tpu as pltpu
from jax.sharding import PartitionSpec as P

BAND1 = 180
WAVE = BAND1 / (2.0 * math.sqrt(3.0))
LANES = 128
MIB = 1 << 20
F32 = jnp.float32
BF16 = jnp.bfloat16


def round_up(count, step):
    return -(-count // step) * step


def stencil_entries(count_out, count_in, centered, out_rows):
    entries = []
    for row_out in out_rows:
        if centered:
            numerator = (2 * row_out + 1) * count_in - count_out
        else:
            numerator = 2 * row_out * count_in
        denominator = 2 * count_out
        base_index = numerator // denominator
        fraction = (numerator - base_index * denominator) / denominator
        for offset_a in range(-2, 4):
            weight = 1.0
            for offset_b in range(-2, 4):
                if offset_b != offset_a:
                    weight = weight * (fraction - offset_b) / (offset_a - offset_b)
            entries.append((row_out, base_index + offset_a, weight))
    return entries


def local_up(count_out, count_in, centered, rows_out, rows_in, below, shape):
    matrix = np.zeros(shape)
    for row_out, column, weight in stencil_entries(count_out, count_in, centered, range(rows_out)):
        assert -below <= column < rows_in + 3 or abs(weight) < 1e-12
        if column >= 0:
            matrix[row_out, column] += weight
        elif column >= -below:
            matrix[row_out, rows_in + 3 + below + column] += weight
    return matrix.astype(np.float32)


def split(x):
    high = x.astype(BF16)
    return high, (x - high.astype(F32)).astype(BF16)


def split_constant(matrix):
    high = matrix.astype(jnp.bfloat16)
    return high, (matrix - high.astype(np.float32)).astype(jnp.bfloat16)


def dot(a, b):
    return jnp.dot(a, b, preferred_element_type=F32)


def dot_transposed(a, b):
    return lax.dot_general(a, b, (((1,), (1,)), ((), ())), preferred_element_type=F32)


def segments(samples):
    full, rest = divmod(samples, 8 * LANES)
    found = [(i, 1, 1, 8) for i in range(full)]
    if rest:
        rows = -(-rest // LANES)
        packed = 4 if rows <= 2 else 2 if rows <= 4 else 1
        found.append((full, 1, packed, rows))
    return found


def lie_across(from_rows, to_tiles, plane, offsets, row):
    turned = from_rows.T
    for offset in offsets:
        to_tiles[plane, pl.ds(offset + row, LANES, stride=8), :] = turned


def translate_kernel(packed, rows, source_ref, kind_ref, child_ref, table_ref, out_ref, pattern, table):
    groups, per = 4 // packed, 8 // packed
    entries = source_ref.shape[0]

    for row in range(rows):
        at = slice(row * LANES, (row + 1) * LANES)
        for part in range(2):
            lie_across(table_ref[part, at], table, part, [c * per for c in range(packed)], row)

    def one_channel(c, carry):
        for part in range(2):
            for row in range(rows):
                lie_across(
                    child_ref[part, c, row * LANES : (row + 1) * LANES],
                    pattern,
                    part * groups + c // packed,
                    [c % packed * per],
                    row,
                )
        return carry

    lax.fori_loop(0, 4, one_channel, 0)

    def one_box(box, carry):
        total = [None] * (2 * groups)
        for entry in range(entries):
            source = pl.ds(pl.multiple_of(source_ref[entry, box] * 8, 8), 8)
            kind = pl.ds(pl.multiple_of(kind_ref[entry, box] * 8, 8), 8)
            real, imag = table[0, kind, :], table[1, kind, :]
            for g in range(groups):
                x, y = pattern[g, source, :], pattern[groups + g, source, :]
                re = x * real - y * imag
                im = x * imag + y * real
                total[g] = re if entry == 0 else total[g] + re
                total[groups + g] = im if entry == 0 else total[groups + g] + im
        for g in range(2 * groups):
            out_ref[0, g, pl.ds(pl.multiple_of(box * 8, 8), 8), :] = total[g]
        return carry

    lax.fori_loop(0, LANES, one_box, 0, unroll=8)


def child_translate(child, table, sources, kinds, segment):
    first, count, packed, rows = segment
    entries = sources.shape[0]
    planes = 8 // packed
    smem = pl.BlockSpec(memory_space=pltpu.SMEM)
    work = count * rows * LANES * LANES
    return pl.pallas_call(
        functools.partial(translate_kernel, packed, rows),
        grid=(count,),
        in_specs=[
            smem,
            smem,
            pl.BlockSpec((2, 4, 8 * LANES, LANES), lambda i: (0, 0, first + i, 0)),
            pl.BlockSpec((2, 8 * LANES, LANES), lambda i: (0, first + i, 0)),
        ],
        out_specs=pl.BlockSpec((1, planes, 8 * LANES, LANES), lambda i: (i, 0, 0, 0)),
        out_shape=jax.ShapeDtypeStruct((count, planes, 8 * LANES, LANES), F32),
        scratch_shapes=[
            pltpu.VMEM((planes, 8 * LANES, LANES), F32),
            pltpu.VMEM((2, 8 * LANES, LANES), F32),
        ],
        compiler_params=pltpu.CompilerParams(vmem_limit_bytes=60 * MIB),
        cost_estimate=pl.CostEstimate(flops=work * entries * 32, bytes_accessed=work * 72, transcendentals=0),
        name="child_translate",
    )(sources, kinds, child, table)


def sum_kernel(packed, rows, parents, slot_ref, local_ref, lowered_ref, phase_ref, *rest):
    out_ref, lowered, total = rest[-3:]
    groups, per = 4 // packed, 8 // packed

    for row in range(rows):
        lie_across(lowered_ref[row * LANES : (row + 1) * LANES], lowered, 0, [0], row)

    def one_box(box, carry):
        slot = slot_ref[box]
        parent = slot % parents * 8
        octant = slot // parents
        cosine, sine = phase_ref[octant], phase_ref[8 + octant]
        here = pl.ds(pl.multiple_of(box * 8, 8), 8)
        for c in range(4):
            x = lowered[0, pl.ds(pl.multiple_of(parent + c * parents * 8, 8), 8), :][:per]
            y = lowered[0, pl.ds(pl.multiple_of(parent + (4 + c) * parents * 8, 8), 8), :][:per]
            re = x * cosine[:per] + y * sine[:per]
            im = y * cosine[:per] - x * sine[:per]
            if packed == 1:
                total[c, here, :] = local_ref[0, c, here, :] + re
                total[4 + c, here, :] = local_ref[0, 4 + c, here, :] + im
            else:
                here = pl.ds(pl.multiple_of(box * 8, 8) + c % packed * per, per)
                total[c // packed, here, :] = local_ref[0, c // packed, here, :] + re
                total[groups + c // packed, here, :] = local_ref[0, groups + c // packed, here, :] + im
        return carry

    lax.fori_loop(0, LANES, one_box, 0, unroll=4)

    def one_channel(c, carry):
        for part in range(2):
            for row in range(rows):
                turned = total[part * groups + c // packed, pl.ds(c % packed * per + row, LANES, stride=8), :].T
                out_ref[part, c, row * LANES : (row + 1) * LANES] = turned
        return carry

    lax.fori_loop(0, 4, one_channel, 0)


def final_sum(shape, local, lowered, phase, slots, segment, onto):
    first, count, packed, rows = segment
    planes = 8 // packed
    smem = pl.BlockSpec(memory_space=pltpu.SMEM)
    in_specs = [
        smem,
        pl.BlockSpec((1, planes, 8 * LANES, LANES), lambda i: (i, 0, 0, 0)),
        pl.BlockSpec((8 * LANES, LANES), lambda i: (first + i, 0)),
        pl.BlockSpec((16, 8, LANES), lambda i: (0, first + i, 0)),
    ]
    operands = [slots, local, lowered, phase]
    aliases = {}
    if onto is not None:
        in_specs.append(pl.BlockSpec(memory_space=pl.ANY))
        operands.append(onto)
        aliases = {4: 0}
    work = count * rows * LANES * LANES
    return pl.pallas_call(
        functools.partial(sum_kernel, packed, rows, LANES // 8),
        grid=(count,),
        in_specs=in_specs,
        out_specs=pl.BlockSpec((2, 4, 8 * LANES, LANES), lambda i: (0, 0, first + i, 0)),
        out_shape=jax.ShapeDtypeStruct(shape, F32),
        input_output_aliases=aliases,
        scratch_shapes=[
            pltpu.VMEM((1, 8 * LANES, LANES), F32),
            pltpu.VMEM((planes, 8 * LANES, LANES), F32),
        ],
        compiler_params=pltpu.CompilerParams(vmem_limit_bytes=60 * MIB),
        cost_estimate=pl.CostEstimate(flops=work * 32, bytes_accessed=work * 72, transcendentals=0),
        name="final_sum",
    )(*operands)


def cos_sin(x):
    turns = jnp.floor(x * (2.0 / math.pi) + 0.5)
    rest = ((x - turns * 1.5703125) - turns * 4.837512969970703e-4) - turns * 7.54978995489188e-8
    square = rest * rest
    sine = rest + rest * square * (
        -1.6666654611e-1 + square * (8.3321608736e-3 + square * -1.9515295891e-4)
    )
    cosine = (1.0 - 0.5 * square) + square * square * (
        4.166664568298827e-2 + square * (-1.388731625493765e-3 + square * 2.443315711809948e-5)
    )
    quarter = turns.astype(jnp.int32)
    odd = (quarter & 1) == 1
    first, second = jnp.where(odd, sine, cosine), jnp.where(odd, cosine, sine)
    first = jnp.where(((quarter + 1) & 2) == 2, -first, first)
    second = jnp.where((quarter & 2) == 2, -second, second)
    return first, second


def tables_kernel(sizes, slot_ref, polar_up_ref, combine_ref, cos_ref, sin_ref, phase_ref, child_ref):
    rows, columns, rows_up, columns_up, parents, n_theta, n_phi = sizes
    polar_index, azimuth_index = lax.axis_index("theta"), lax.axis_index("phi")

    def iota(shape, axis):
        return lax.broadcasted_iota(jnp.int32, shape, axis)

    boxes = slot_ref.shape[1]
    slot = jnp.broadcast_to(slot_ref[...], (parents, boxes))
    same = (slot & (parents - 1)) == iota((parents, boxes), 0)
    octant = slot >> (parents.bit_length() - 1)
    east, north, upper = (2 * ((octant >> n) & 1) - 1 for n in range(3))
    blocks = []
    for z in range(2):
        for kind in range(2):
            for difference in range(2):
                chosen = same & ((east == north) if kind == 0 else (east != north))
                weight = (upper if z else 1) * (east if difference else 1)
                weight = jnp.where(chosen, weight, 0).astype(F32)
                blocks.append(weight)
    combine = jnp.concatenate(blocks, axis=0).astype(BF16)
    combine_ref[...] = jnp.concatenate([combine, combine], axis=1)

    p_pad, t_pad = cos_ref.shape
    q_pad = phase_ref.shape[2]
    polar = (iota((p_pad, LANES), 0) + polar_index * rows_up).astype(F32) + 0.5
    cosine, sine = cos_sin(polar * (math.pi / (rows_up * n_theta)))
    up_cos, up_sin = cos_sin(WAVE * cosine)
    cos_ref[...] = polar_up_ref[...] * up_cos[:, :t_pad]
    sin_ref[...] = polar_up_ref[...] * up_sin[:, :t_pad]
    azimuth = (iota((8, q_pad), 1) + azimuth_index * columns_up).astype(F32)
    east, north = cos_sin(azimuth * (2.0 * math.pi / (columns_up * n_phi)))
    flat = WAVE * sine
    valid = iota((p_pad, LANES), 0) < rows_up
    for lane in range(0, q_pad, LANES):
        lanes = slice(lane, lane + LANES)
        inside = valid & (iota((p_pad, LANES), 1) + lane < columns_up)
        for kind in range(2):
            turned = (east - north if kind else east + north)[:1, lanes]
            found = cos_sin(flat * turned)
            for i in range(2):
                phase_ref[2 * kind + i, :, lanes] = jnp.where(inside, found[i], 0.0)

    count = child_ref.shape[1]
    sample = iota((count, LANES), 0) * LANES + iota((count, LANES), 1)
    row = jnp.floor((sample.astype(F32) + 0.5) * (1.0 / columns))
    polar = row + (polar_index * rows).astype(F32) + 0.5
    azimuth = sample.astype(F32) - row * columns + (azimuth_index * columns).astype(F32)
    up, flat = cos_sin(polar * (math.pi / (rows * n_theta)))
    east, north = cos_sin(azimuth * (2.0 * math.pi / (columns * n_phi)))
    for octant in range(4):
        signs = [2 * ((octant >> n) & 1) - 1 for n in range(3)]
        found = cos_sin(WAVE * (flat * east * signs[0] + flat * north * signs[1] + up * signs[2]))
        child_ref[octant] = found[0]
        child_ref[7 - octant] = found[0]
        child_ref[8 + octant] = found[1]
        child_ref[15 - octant] = -found[1]


def tables(slots, sizes, p_pad, t_pad, q_pad, polar_up):
    rows, columns, rows_up, columns_up, parents, n_theta, n_phi = sizes
    boxes = slots.shape[0]
    assert parents & (parents - 1) == 0
    return pl.pallas_call(
        functools.partial(tables_kernel, sizes),
        out_shape=[
            jax.ShapeDtypeStruct((8 * parents, 2 * boxes), BF16),
            jax.ShapeDtypeStruct((p_pad, t_pad), F32),
            jax.ShapeDtypeStruct((p_pad, t_pad), F32),
            jax.ShapeDtypeStruct((4, p_pad, q_pad), F32),
            jax.ShapeDtypeStruct((16, -(-rows * columns // LANES), LANES), F32),
        ],
        compiler_params=pltpu.CompilerParams(vmem_limit_bytes=60 * MIB),
        name="tables",
    )(slots.reshape(1, boxes), polar_up)


def parent_kernel(
    sizes,
    source_ref,
    kind_ref,
    child_ref,
    next_ref,
    previous_ref,
    side_ref,
    table_ref,
    combine_ref,
    polar_cos_ref,
    polar_sin_ref,
    azimuth_up_ref,
    polar_down_ref,
    azimuth_down_ref,
    phase_ref,
    out_ref,
    wide,
    rows_done,
    table_by_kind,
    parent_out,
    in_high,
    in_low,
    lowered,
):
    (rows, columns, rows_up, columns_up, parents, entries, table_steps, table_rows) = sizes
    t_pad, p_pad, f_pad, q_pad = wide.shape[1] // 128, parent_out.shape[3], wide.shape[2], parent_out.shape[4]
    step = pl.program_id(0)
    half = 4 * parents
    table_first = jnp.minimum(step, table_steps - 1) * table_rows

    @pl.when(step == 0)
    def _():
        for part in range(2):
            for t in range(rows + 6, t_pad):
                wide[part, pl.ds(t, 128, stride=t_pad), :] = jnp.zeros((128, f_pad), F32)
        for part in range(2):
            for p in range(rows_up, p_pad):
                for lane in range(0, q_pad, LANES):
                    table_by_kind[lane // LANES, pl.ds(part * p_pad + p, 128, stride=2 * p_pad), :] = jnp.zeros(
                        (128, LANES), F32
                    )

    combine = combine_ref[...]

    def samples(part, main_ref, r, t):
        x = jnp.concatenate(
            [main_ref[part, 0, r], side_ref[part, 0, t], jnp.zeros((f_pad - columns - 8, LANES), F32)], axis=0
        )
        high, low = split(x)
        return jnp.concatenate([high, low], axis=1)

    def turn(pieces):
        for part in range(2):
            for i in range(0, len(pieces), 2):
                both = jnp.concatenate([samples(part, *piece) for piece in pieces[i : i + 2]], axis=0)
                turned = dot_transposed(combine, both)
                for j, piece in enumerate(pieces[i : i + 2]):
                    at = pl.ds(piece[2], 128, stride=t_pad)
                    wide[part, at, :] = turned[:, j * f_pad : (j + 1) * f_pad]

    per_turn = next(n for n in (4, 3, 2, 1) if rows % n == 0)

    turns = rows // per_turn
    table_per_turn = -(-table_rows // turns)

    def main_rows(i, carry):
        turn([(child_ref, per_turn * i + r, per_turn * i + r) for r in range(per_turn)])
        for j in range(table_per_turn):
            r = jnp.minimum(i * table_per_turn + j, table_rows - 1)
            for part in range(2):
                x = table_ref[part, r]
                if q_pad > columns_up:
                    x = jnp.concatenate([x, jnp.zeros((q_pad - columns_up, LANES), F32)], axis=0)
                for lane in range(0, q_pad, LANES):
                    turned = x[lane : lane + LANES].T
                    at = pl.ds(part * p_pad + table_first + r, 128, stride=2 * p_pad)
                    table_by_kind[lane // LANES, at, :] = turned
        return carry

    lax.fori_loop(0, turns, main_rows, 0)
    turn([(next_ref, r, rows + r) for r in range(3)] + [(previous_ref, r, rows + 3 + r) for r in range(3)])

    polar = []
    for sign in (-1.0, 1.0):
        both = jnp.concatenate([polar_cos_ref[...], sign * polar_sin_ref[...]], axis=1)
        high, low = split(both)
        polar.append(jnp.concatenate([high, high, low], axis=1))
    azimuth = azimuth_up_ref[...]
    per = 4
    for target in range(2):
        for difference in range(2):
            part = target if difference == 0 else 1 - target

            def one_kind(kind, carry, part=part, difference=difference):
                first = (kind * 2 + difference) * parents
                for pair in range(parents // 2):
                    stacked = []
                    for source, offset in ((part, 0), (1 - part, half)):
                        at = (offset + first + 2 * pair) * t_pad
                        stacked.append(
                            jnp.concatenate(
                                [wide[source, pl.ds(pl.multiple_of(at + i * t_pad, 8), t_pad), :] for i in range(2)],
                                axis=1,
                            )
                        )
                    high, low = split(jnp.concatenate(stacked, axis=0))
                    result = dot(polar[part], jnp.concatenate([high, low, high], axis=0))
                    high, low = split(result)
                    for i in range(2):
                        lanes = slice(i * f_pad, (i + 1) * f_pad)
                        rows_done[kind * 2 + difference, pl.ds((2 * pair + i) * p_pad, p_pad), :] = jnp.concatenate(
                            [high[:, lanes], low[:, lanes], high[:, lanes]], axis=1
                        )
                return carry

            lax.fori_loop(0, 2, one_kind, 0)

        def one_group(group, carry, target=target):
            at = pl.ds(pl.multiple_of(group * per * p_pad, 16), per * p_pad)
            y = dot(jnp.concatenate([rows_done[k, at, :] for k in range(4)], axis=0), azimuth)
            for i in range(per):
                terms = [y[(k * per + i) * p_pad : (k * per + i + 1) * p_pad] * phase_ref[k] for k in range(4)]
                if target == 0:
                    value = (terms[0] - terms[1]) + (terms[2] - terms[3])
                else:
                    value = (terms[0] + terms[1]) + (terms[2] + terms[3])
                parent_out[target, step, group * per + i] = value
            return carry

        lax.fori_loop(0, parents // per, one_group, 0)

    @pl.when(step == 3)
    def _():
        tiles = q_pad // LANES

        def one_tile(tile, carry):
            box = tile // (p_pad // 16)
            row = tile % (p_pad // 16) * 16
            sources = [source_ref[box, e] for e in range(entries)]
            kinds = [kind_ref[box, e] * (2 * p_pad) + row for e in range(entries)]
            for lane_tile in range(tiles):
                lanes = slice(lane_tile * LANES, (lane_tile + 1) * LANES)
                total = [None] * 8
                for e in range(entries):
                    real = table_by_kind[lane_tile, pl.ds(pl.multiple_of(kinds[e], 16), 16), :]
                    imag = table_by_kind[lane_tile, pl.ds(pl.multiple_of(kinds[e] + p_pad, 16), 16), :]
                    for c in range(4):
                        x = parent_out[0, c, sources[e], pl.ds(pl.multiple_of(row, 16), 16), lanes]
                        y = parent_out[1, c, sources[e], pl.ds(pl.multiple_of(row, 16), 16), lanes]
                        re = x * real - y * imag
                        im = x * imag + y * real
                        total[c] = re if e == 0 else total[c] + re
                        total[4 + c] = im if e == 0 else total[4 + c] + im
                for c in range(8):
                    high, low = split(total[c])
                    at = pl.ds(pl.multiple_of((c * parents + box) * p_pad + row, 16), 16)
                    in_high[at, lanes] = high
                    in_low[at, lanes] = low
            return carry

        lax.fori_loop(0, parents * (p_pad // 16), one_tile, 0)

        down = azimuth_down_ref[...]
        down_high = down[:, :f_pad]
        high, low = split(polar_down_ref[...])
        polar_back = jnp.concatenate([high, high, low], axis=1)
        per = parents

        def one_group(group, carry):
            at = pl.ds(pl.multiple_of(group * per * p_pad, 16), per * p_pad)
            high = in_high[at, :]
            low = in_low[at, :]
            both = dot(high, down)
            y = both[:, :f_pad] + both[:, f_pad:] + dot(low, down_high)
            for i in range(0, per, 2):
                x = jnp.concatenate([y[i * p_pad : (i + 1) * p_pad], y[(i + 1) * p_pad : (i + 2) * p_pad]], axis=1)
                high, low = split(x)
                z = dot(polar_back, jnp.concatenate([high, low, high], axis=0))
                for j in range(2):
                    lowered[pl.ds(pl.multiple_of((group * per + i + j) * t_pad, 8), t_pad), :] = z[
                        :, j * f_pad : (j + 1) * f_pad
                    ]
            return carry

        lax.fori_loop(0, 8 * parents // per, one_group, 0)

        per_turn = next(n for n in (6, 5, 3, 2, 1) if (rows + 6) % n == 0)

        def some_rows(i, carry):
            for r in range(per_turn):
                turned = lowered[pl.ds(i * per_turn + r, 8 * parents, stride=t_pad), :].T
                out_ref[i * per_turn + r] = turned[: columns + 8]
            return carry

        lax.fori_loop(0, (rows + 6) // per_turn, some_rows, 0)


def parent_level(child_out, after, before, side, table, sources, kinds, combine, polar_cos, polar_sin, phase):
    _, rows, columns, boxes = child_out.shape
    _, rows_up, columns_up, translators = table.shape
    assert boxes == LANES and translators == LANES
    parents, entries = sources.shape
    t_pad, p_pad = polar_cos.shape[1], polar_cos.shape[0]
    f_pad, q_pad = round_up(columns + 8, LANES), round_up(columns_up, LANES)
    assert f_pad == LANES
    table_steps = next(s for s in (4, 2, 1) if rows_up % s == 0)
    table_rows = rows_up // table_steps
    n_theta, n_phi = lax.axis_size("theta"), lax.axis_size("phi")
    polar_up = local_up(rows_up * n_theta, rows * n_theta, True, rows_up, rows, 3, (p_pad, t_pad))
    azimuth_up = local_up(columns_up * n_phi, columns * n_phi, False, columns_up, columns, 2, (q_pad, f_pad))
    high, low = split_constant(np.ascontiguousarray(azimuth_up.T))
    azimuth_three = jnp.asarray(np.concatenate([high, high, low], axis=0))
    high, low = split_constant(azimuth_up)
    azimuth_down = jnp.asarray(np.concatenate([high, low], axis=1))
    polar_down = jnp.asarray(np.ascontiguousarray(polar_up.T))

    def whole(array):
        return pl.BlockSpec(array.shape, lambda g: (0,) * array.ndim)

    def channel(shape):
        return pl.BlockSpec((2, 1) + shape, lambda g: (0, g, 0, 0, 0))

    smem = pl.BlockSpec(memory_space=pltpu.SMEM)
    constants = [combine, polar_cos, polar_sin, azimuth_three, polar_down, azimuth_down, phase]
    return pl.pallas_call(
        functools.partial(
            parent_kernel, (rows, columns, rows_up, columns_up, parents, entries, table_steps, table_rows)
        ),
        grid=(4,),
        in_specs=[
            smem,
            smem,
            channel((rows, columns, boxes)),
            channel((3, columns, boxes)),
            channel((3, columns, boxes)),
            channel((rows + 6, 8, boxes)),
            pl.BlockSpec(
                (2, table_rows, columns_up, translators), lambda g: (0, jnp.minimum(g, table_steps - 1), 0, 0)
            ),
        ]
        + [whole(c) for c in constants],
        out_specs=pl.BlockSpec((rows + 6, columns + 8, 8 * parents), lambda g: (0, 0, 0)),
        out_shape=jax.ShapeDtypeStruct((rows + 6, columns + 8, 8 * parents), F32),
        scratch_shapes=[
            pltpu.VMEM((2, 128 * t_pad, f_pad), F32),
            pltpu.VMEM((4, parents * p_pad, 3 * f_pad), BF16),
            pltpu.VMEM((q_pad // LANES, translators * 2 * p_pad, LANES), F32),
            pltpu.VMEM((2, 4, parents, p_pad, q_pad), F32),
            pltpu.VMEM((8 * parents * p_pad, q_pad), BF16),
            pltpu.VMEM((8 * parents * p_pad, q_pad), BF16),
            pltpu.VMEM((8 * parents * t_pad, f_pad), F32),
        ],
        compiler_params=pltpu.CompilerParams(vmem_limit_bytes=60 * MIB),
        cost_estimate=pl.CostEstimate(
            flops=20_000_000_000, bytes_accessed=child_out.size * 8, transcendentals=0
        ),
        name="parent_level",
    )(
        sources,
        kinds,
        child_out.reshape((2, 4) + child_out.shape[1:]),
        after.reshape((2, 4) + after.shape[1:]),
        before.reshape((2, 4) + before.shape[1:]),
        side.reshape((2, 4) + side.shape[1:]),
        table,
        *constants,
    )


def chain(count, periodic):
    pairs = [(i, i + 1) for i in range(count - 1)]
    return pairs + [(count - 1, 0)] if periodic else pairs


def send(block, axis, up):
    pairs = chain(lax.axis_size(axis), axis == "phi")
    return lax.ppermute(block, axis, pairs if up else [(b, a) for a, b in pairs])


def per_device(
    child_out,
    child_slot,
    sources_child,
    kinds_child,
    table_child,
    sources_parent,
    kinds_parent,
    table_parent,
):
    _, rows, columns, boxes = child_out.shape
    _, rows_up, columns_up, _ = table_parent.shape
    parents = boxes // 8
    n_theta, n_phi = lax.axis_size("theta"), lax.axis_size("phi")
    t_pad, p_pad = round_up(rows + 6, 16), round_up(rows_up, 16)
    q_pad = round_up(columns_up, LANES)
    barrier = lax.optimization_barrier

    polar_up = local_up(rows_up * n_theta, rows * n_theta, True, rows_up, rows, 3, (p_pad, t_pad))
    sizes = (rows, columns, rows_up, columns_up, parents, n_theta, n_phi)
    combine, polar_cos, polar_sin, phase, phase_child = tables(
        child_slot, sizes, p_pad, t_pad, q_pad, jnp.asarray(polar_up)
    )

    samples = rows * columns
    flat_child = child_out.reshape(2, 4, samples, boxes)
    flat_table = table_child.reshape(2, samples, table_child.shape[3])
    pieces = segments(samples)
    local = []

    def translate_next(child):
        if len(local) < len(pieces):
            local.append(child_translate(child, flat_table, sources_child.T, kinds_child.T, pieces[len(local)]))

    after = send(child_out[:, :3], "theta", False)
    before = send(child_out[:, rows - 3 :], "theta", True)
    translate_next(flat_child)
    after, before, local = barrier((after, before, local))

    low, high = (
        jnp.concatenate([edge[:, :, at] for edge in (child_out, after, before)], axis=1)
        for at in (slice(0, 3), slice(columns - 2, columns))
    )
    low, high, later_child = barrier((low, high, flat_child))
    right = send(low, "phi", False)
    left = send(high, "phi", True)
    if len(pieces) > 2:
        translate_next(later_child)
    right, left, local = barrier((right, left, local))
    side = jnp.concatenate([right, left, jnp.zeros((8, rows + 6, 3, boxes), F32)], axis=2)

    lowered = parent_level(
        child_out,
        after,
        before,
        side,
        table_parent,
        sources_parent,
        kinds_parent,
        combine,
        polar_cos,
        polar_sin,
        phase,
    )
    lowered, later_child = barrier((lowered, flat_child))

    low = send(lowered[rows : rows + 3], "theta", True)
    high = send(lowered[rows + 3 : rows + 6], "theta", False)
    while len(local) < len(pieces):
        translate_next(later_child)
    local, lowered = barrier((local, lowered))
    here = lowered[:rows]
    here = here + jnp.pad(low, ((0, rows - 3), (0, 0), (0, 0))) + jnp.pad(high, ((rows - 3, 0), (0, 0), (0, 0)))
    low = send(here[:, columns : columns + 3], "phi", True)
    high = send(here[:, columns + 3 : columns + 5], "phi", False)
    here = here[:, :columns]
    here = here + jnp.pad(low, ((0, 0), (0, columns - 3), (0, 0))) + jnp.pad(high, ((0, 0), (columns - 2, 0), (0, 0)))
    here = here.reshape(samples, boxes)

    result = None
    for piece, part in zip(pieces, local):
        result = final_sum(flat_child.shape, part, here, phase_child, child_slot, piece, result)
    return result.reshape(child_out.shape)


def solution(mesh):
    placed = (
        P(None, "theta", "phi", None),
        P(),
        P(),
        P(),
        P(None, "theta", "phi", None),
        P(),
        P(),
        P(None, "theta", "phi", None),
    )
    return jax.shard_map(
        per_device,
        mesh=mesh,
        in_specs=placed,
        out_specs=P(None, "theta", "phi", None),
        check_vma=False,
    )
```

```python
import functools
import math

import jax
import jax.numpy as jnp
import numpy as np
from jax import lax
from jax.experimental import pallas as pl
from jax.experimental.pallas import tpu as pltpu
from jax.sharding import PartitionSpec as P

BAND1 = 180
WAVE = BAND1 / (2.0 * math.sqrt(3.0))
LANES = 128
MIB = 1 << 20
F32 = jnp.float32
BF16 = jnp.bfloat16


def round_up(count, step):
    return -(-count // step) * step


def stencil_entries(count_out, count_in, centered, out_rows):
    entries = []
    for row_out in out_rows:
        if centered:
            numerator = (2 * row_out + 1) * count_in - count_out
        else:
            numerator = 2 * row_out * count_in
        denominator = 2 * count_out
        base_index = numerator // denominator
        fraction = (numerator - base_index * denominator) / denominator
        for offset_a in range(-2, 4):
            weight = 1.0
            for offset_b in range(-2, 4):
                if offset_b != offset_a:
                    weight = weight * (fraction - offset_b) / (offset_a - offset_b)
            entries.append((row_out, base_index + offset_a, weight))
    return entries


def local_up(count_out, count_in, centered, rows_out, rows_in, below, shape):
    matrix = np.zeros(shape)
    for row_out, column, weight in stencil_entries(count_out, count_in, centered, range(rows_out)):
        assert -below <= column < rows_in + 3 or abs(weight) < 1e-12
        if column >= 0:
            matrix[row_out, column] += weight
        elif column >= -below:
            matrix[row_out, rows_in + 3 + below + column] += weight
    return matrix.astype(np.float32)


def split(x):
    high = x.astype(BF16)
    return high, (x - high.astype(F32)).astype(BF16)


def split_constant(matrix):
    high = matrix.astype(jnp.bfloat16)
    return high, (matrix - high.astype(np.float32)).astype(jnp.bfloat16)


def dot(a, b):
    return jnp.dot(a, b, preferred_element_type=F32)


def dot_transposed(a, b):
    return lax.dot_general(a, b, (((1,), (1,)), ((), ())), preferred_element_type=F32)


def segments(samples):
    full, rest = divmod(samples, 8 * LANES)
    found = [(0, full, 1, 8)] if full else []
    if rest:
        rows = -(-rest // LANES)
        packed = 4 if rows <= 2 else 2 if rows <= 4 else 1
        found.append((full, 1, packed, rows))
    return found


def translate_kernel(packed, rows, source_ref, kind_ref, child_ref, table_ref, *rest):
    out_ref, pattern, table = rest[-3:]
    groups, per = 4 // packed, 8 // packed
    tile = 16 * groups
    entries = source_ref.shape[0]
    step = pl.program_id(0)

    @pl.when(step == 0)
    def _():
        for row in range(rows):
            for part in range(2):
                turned = table_ref[part, row * LANES : (row + 1) * LANES].T
                for c in range(packed):
                    table[pl.ds(part * 8 + c * per + row, LANES, stride=16), :] = turned

    @pl.when(step < 2)
    def _():
        for i in range(2):
            c = 2 * step + i
            plane, sub = (c, 0) if packed == 1 else (c // packed, c % packed * per)
            for part in range(2):
                for row in range(rows):
                    at = pl.ds((part * groups + plane) * 8 + sub + row, LANES, stride=tile)
                    pattern[at, :] = child_ref[part, i, row * LANES : (row + 1) * LANES].T

    @pl.when(step >= 2)
    def _():
        half = LANES // 2

        def one_box(i, carry):
            box = (step - 2) * half + i
            total = [None] * (2 * groups)
            for entry in range(entries):
                x = pattern[pl.ds(pl.multiple_of(source_ref[entry, box] * tile, tile), tile), :]
                factor = table[pl.ds(pl.multiple_of(kind_ref[entry, box] * 16, 16), 16), :]
                real, imag = factor[:8], factor[8:]
                for g in range(groups):
                    xr, xi = x[g * 8 : g * 8 + 8], x[(groups + g) * 8 : (groups + g) * 8 + 8]
                    re = xr * real - xi * imag
                    im = xr * imag + xi * real
                    total[g] = re if entry == 0 else total[g] + re
                    total[groups + g] = im if entry == 0 else total[groups + g] + im
            for g in range(2 * groups):
                out_ref[0, pl.ds(pl.multiple_of(i * tile, tile) + g * 8, 8), :] = total[g]
            return carry

        lax.fori_loop(0, half, one_box, 0, unroll=2)


def child_translate(child, table, sources, kinds, segment, chunk, onto):
    first, count, packed, rows = segment
    tile = 64 // packed
    smem = pl.BlockSpec(memory_space=pltpu.SMEM)
    in_specs = [
        smem,
        smem,
        pl.BlockSpec((2, 2, 8 * LANES, LANES), lambda s: (0, jnp.minimum(s, 1), first + chunk, 0)),
        pl.BlockSpec((2, 8 * LANES, LANES), lambda s: (0, first + chunk, 0)),
    ]
    operands = [sources, kinds, child, table]
    aliases = {}
    if onto is not None:
        in_specs.append(pl.BlockSpec(memory_space=pl.ANY))
        operands.append(onto)
        aliases = {4: 0}
    work = rows * LANES * LANES
    return pl.pallas_call(
        functools.partial(translate_kernel, packed, rows),
        grid=(4,),
        in_specs=in_specs,
        out_specs=pl.BlockSpec((1, LANES // 2 * tile, LANES), lambda s: (chunk, jnp.maximum(s - 2, 0), 0)),
        out_shape=jax.ShapeDtypeStruct((count, LANES * tile, LANES), F32),
        input_output_aliases=aliases,
        scratch_shapes=[pltpu.VMEM((LANES * tile, LANES), F32), pltpu.VMEM((LANES * 16, LANES), F32)],
        compiler_params=pltpu.CompilerParams(vmem_limit_bytes=60 * MIB),
        cost_estimate=pl.CostEstimate(
            flops=work * sources.shape[0] * 32, bytes_accessed=work * 72, transcendentals=0
        ),
        name="child_translate",
    )(*operands)


def sum_kernel(packed, rows, parents, slot_ref, local_ref, lowered_ref, phase_ref, *rest):
    out_ref, lowered, total = rest[-3:]
    groups, per = 4 // packed, 8 // packed
    tile = 16 * groups
    step = pl.program_id(1)

    @pl.when(step == 0)
    def _():
        for row in range(rows):
            lowered[pl.ds(row, LANES, stride=8), :] = lowered_ref[row * LANES : (row + 1) * LANES].T

    @pl.when(step < 2)
    def _():
        half = LANES // 2

        def one_box(i, carry):
            slot = slot_ref[step * half + i]
            octant = slot // parents
            cosine, sine = phase_ref[octant][:per], phase_ref[8 + octant][:per]
            x = lowered[pl.ds(pl.multiple_of(slot % parents * 64, 64), 64), :]
            local = local_ref[0, pl.ds(pl.multiple_of(i * tile, tile), tile), :]
            for c in range(4):
                real, imag = x[c * 8 : c * 8 + per], x[(4 + c) * 8 : (4 + c) * 8 + per]
                at = c // packed * 8 + c % packed * per
                here = pl.multiple_of((step * half + i) * tile, tile)
                total[pl.ds(here + at, per), :] = local[at : at + per] + (real * cosine + imag * sine)
                at += groups * 8
                total[pl.ds(here + at, per), :] = local[at : at + per] + (imag * cosine - real * sine)
            return carry

        lax.fori_loop(0, half, one_box, 0, unroll=4)

    @pl.when(step >= 2)
    def _():
        for i in range(2):
            c = 2 * (step - 2) + i
            plane, sub = (c, 0) if packed == 1 else (c // packed, c % packed * per)
            for part in range(2):
                for row in range(rows):
                    at = pl.ds((part * groups + plane) * 8 + sub + row, LANES, stride=tile)
                    out_ref[part, i, row * LANES : (row + 1) * LANES] = total[at, :].T


def final_sum(shape, local, lowered, phase, slots, segment, onto):
    first, count, packed, rows = segment
    tile = 64 // packed
    in_specs = [
        pl.BlockSpec(memory_space=pltpu.SMEM),
        pl.BlockSpec((1, LANES // 2 * tile, LANES), lambda i, s: (i, jnp.minimum(s, 1), 0)),
        pl.BlockSpec((8 * LANES, LANES), lambda i, s: (first + i, 0)),
        pl.BlockSpec((16, 8, LANES), lambda i, s: (0, first + i, 0)),
    ]
    operands = [slots, local, lowered, phase]
    aliases = {}
    if onto is not None:
        in_specs.append(pl.BlockSpec(memory_space=pl.ANY))
        operands.append(onto)
        aliases = {4: 0}
    work = count * rows * LANES * LANES
    return pl.pallas_call(
        functools.partial(sum_kernel, packed, rows, LANES // 8),
        grid=(count, 4),
        in_specs=in_specs,
        out_specs=pl.BlockSpec((2, 2, 8 * LANES, LANES), lambda i, s: (0, jnp.maximum(s - 2, 0), first + i, 0)),
        out_shape=jax.ShapeDtypeStruct(shape, F32),
        input_output_aliases=aliases,
        scratch_shapes=[pltpu.VMEM((8 * LANES, LANES), F32), pltpu.VMEM((LANES * tile, LANES), F32)],
        compiler_params=pltpu.CompilerParams(vmem_limit_bytes=60 * MIB),
        cost_estimate=pl.CostEstimate(flops=work * 32, bytes_accessed=work * 72, transcendentals=0),
        name="final_sum",
    )(*operands)


def cos_sin(x):
    turns = jnp.floor(x * (2.0 / math.pi) + 0.5)
    rest = ((x - turns * 1.5703125) - turns * 4.837512969970703e-4) - turns * 7.54978995489188e-8
    square = rest * rest
    sine = rest + rest * square * (
        -1.6666654611e-1 + square * (8.3321608736e-3 + square * -1.9515295891e-4)
    )
    cosine = (1.0 - 0.5 * square) + square * square * (
        4.166664568298827e-2 + square * (-1.388731625493765e-3 + square * 2.443315711809948e-5)
    )
    quarter = turns.astype(jnp.int32)
    odd = (quarter & 1) == 1
    first, second = jnp.where(odd, sine, cosine), jnp.where(odd, cosine, sine)
    first = jnp.where(((quarter + 1) & 2) == 2, -first, first)
    second = jnp.where((quarter & 2) == 2, -second, second)
    return first, second


def tables_kernel(sizes, slot_ref, polar_up_ref, combine_ref, cos_ref, sin_ref, phase_ref, child_ref):
    rows, columns, rows_up, columns_up, parents, n_theta, n_phi = sizes
    polar_index, azimuth_index = lax.axis_index("theta"), lax.axis_index("phi")

    def iota(shape, axis):
        return lax.broadcasted_iota(jnp.int32, shape, axis)

    boxes = slot_ref.shape[1]
    slot = jnp.broadcast_to(slot_ref[...], (parents, boxes))
    same = (slot & (parents - 1)) == iota((parents, boxes), 0)
    octant = slot >> (parents.bit_length() - 1)
    east, north, upper = (2 * ((octant >> n) & 1) - 1 for n in range(3))
    blocks = []
    for z in range(2):
        for kind in range(2):
            for difference in range(2):
                chosen = same & ((east == north) if kind == 0 else (east != north))
                weight = (upper if z else 1) * (east if difference else 1)
                weight = jnp.where(chosen, weight, 0).astype(F32)
                blocks.append(weight)
    combine = jnp.concatenate(blocks, axis=0).astype(BF16)
    combine_ref[...] = jnp.concatenate([combine, combine], axis=1)

    p_pad, t_pad = cos_ref.shape
    q_pad = phase_ref.shape[2]
    polar = (iota((p_pad, LANES), 0) + polar_index * rows_up).astype(F32) + 0.5
    cosine, sine = cos_sin(polar * (math.pi / (rows_up * n_theta)))
    up_cos, up_sin = cos_sin(WAVE * cosine)
    cos_ref[...] = polar_up_ref[...] * up_cos[:, :t_pad]
    sin_ref[...] = polar_up_ref[...] * up_sin[:, :t_pad]
    azimuth = (iota((8, q_pad), 1) + azimuth_index * columns_up).astype(F32)
    east, north = cos_sin(azimuth * (2.0 * math.pi / (columns_up * n_phi)))
    flat = WAVE * sine
    valid = iota((p_pad, LANES), 0) < rows_up
    for lane in range(0, q_pad, LANES):
        lanes = slice(lane, lane + LANES)
        inside = valid & (iota((p_pad, LANES), 1) + lane < columns_up)
        for kind in range(2):
            turned = (east - north if kind else east + north)[:1, lanes]
            found = cos_sin(flat * turned)
            for i in range(2):
                phase_ref[2 * kind + i, :, lanes] = jnp.where(inside, found[i], 0.0)

    count = child_ref.shape[1]
    sample = iota((count, LANES), 0) * LANES + iota((count, LANES), 1)
    row = jnp.floor((sample.astype(F32) + 0.5) * (1.0 / columns))
    polar = row + (polar_index * rows).astype(F32) + 0.5
    azimuth = sample.astype(F32) - row * columns + (azimuth_index * columns).astype(F32)
    up, flat = cos_sin(polar * (math.pi / (rows * n_theta)))
    east, north = cos_sin(azimuth * (2.0 * math.pi / (columns * n_phi)))
    for octant in range(4):
        signs = [2 * ((octant >> n) & 1) - 1 for n in range(3)]
        found = cos_sin(WAVE * (flat * east * signs[0] + flat * north * signs[1] + up * signs[2]))
        child_ref[octant] = found[0]
        child_ref[7 - octant] = found[0]
        child_ref[8 + octant] = found[1]
        child_ref[15 - octant] = -found[1]


def tables(slots, sizes, p_pad, t_pad, q_pad, polar_up):
    rows, columns, rows_up, columns_up, parents, n_theta, n_phi = sizes
    boxes = slots.shape[0]
    assert parents & (parents - 1) == 0
    return pl.pallas_call(
        functools.partial(tables_kernel, sizes),
        out_shape=[
            jax.ShapeDtypeStruct((8 * parents, 2 * boxes), BF16),
            jax.ShapeDtypeStruct((p_pad, t_pad), F32),
            jax.ShapeDtypeStruct((p_pad, t_pad), F32),
            jax.ShapeDtypeStruct((4, p_pad, q_pad), F32),
            jax.ShapeDtypeStruct((16, -(-rows * columns // LANES), LANES), F32),
        ],
        compiler_params=pltpu.CompilerParams(vmem_limit_bytes=60 * MIB),
        name="tables",
    )(slots.reshape(1, boxes), polar_up)


def parent_kernel(
    sizes,
    source_ref,
    kind_ref,
    child_ref,
    next_ref,
    previous_ref,
    side_ref,
    table_ref,
    combine_ref,
    polar_cos_ref,
    polar_sin_ref,
    azimuth_up_ref,
    polar_down_ref,
    azimuth_down_ref,
    phase_ref,
    out_ref,
    wide,
    rows_done,
    table_by_kind,
    parent_out,
    in_high,
    in_low,
    lowered,
):
    (rows, columns, rows_up, columns_up, parents, entries, table_steps, table_rows) = sizes
    t_pad, f_pad = wide.shape[1] // 128, wide.shape[2]
    p_pad, q_pad = phase_ref.shape[1], phase_ref.shape[2]
    row_tiles, lane_tiles = p_pad // 8, q_pad // LANES
    step = pl.program_id(0)
    half = 4 * parents
    table_first = jnp.minimum(step, table_steps - 1) * table_rows

    @pl.when(step == 0)
    def _():
        for part in range(2):
            for t in range(rows + 6, t_pad):
                wide[part, pl.ds(t, 128, stride=t_pad), :] = jnp.zeros((128, f_pad), F32)
        for part in range(2):
            for p in range(rows_up, p_pad):
                for lane_tile in range(lane_tiles):
                    at = pl.ds(part * 8 + p % 8, 128, stride=16)
                    table_by_kind[lane_tile * row_tiles + p // 8, at, :] = jnp.zeros((128, LANES), F32)

    combine = combine_ref[...]

    def samples(part, main_ref, r, t):
        x = jnp.concatenate(
            [main_ref[part, 0, r], side_ref[part, 0, t], jnp.zeros((f_pad - columns - 8, LANES), F32)], axis=0
        )
        high, low = split(x)
        return jnp.concatenate([high, low], axis=1)

    def turn(pieces):
        for part in range(2):
            for i in range(0, len(pieces), 2):
                both = jnp.concatenate([samples(part, *piece) for piece in pieces[i : i + 2]], axis=0)
                turned = dot_transposed(combine, both)
                for j, piece in enumerate(pieces[i : i + 2]):
                    at = pl.ds(piece[2], 128, stride=t_pad)
                    wide[part, at, :] = turned[:, j * f_pad : (j + 1) * f_pad]

    per_turn = next(n for n in (4, 3, 2, 1) if rows % n == 0)

    turns = rows // per_turn
    table_per_turn = -(-table_rows // turns)

    def main_rows(i, carry):
        turn([(child_ref, per_turn * i + r, per_turn * i + r) for r in range(per_turn)])
        for j in range(table_per_turn):
            r = jnp.minimum(i * table_per_turn + j, table_rows - 1)
            for part in range(2):
                x = table_ref[part, r]
                if q_pad > columns_up:
                    x = jnp.concatenate([x, jnp.zeros((q_pad - columns_up, LANES), F32)], axis=0)
                for lane in range(0, q_pad, LANES):
                    turned = x[lane : lane + LANES].T
                    p = table_first + r
                    at = pl.ds(part * 8 + p % 8, 128, stride=16)
                    table_by_kind[lane // LANES * row_tiles + p // 8, at, :] = turned
        return carry

    lax.fori_loop(0, turns, main_rows, 0)
    turn([(next_ref, r, rows + r) for r in range(3)] + [(previous_ref, r, rows + 3 + r) for r in range(3)])

    polar = []
    for sign in (-1.0, 1.0):
        both = jnp.concatenate([polar_cos_ref[...], sign * polar_sin_ref[...]], axis=1)
        high, low = split(both)
        polar.append(jnp.concatenate([high, high, low], axis=1))
    azimuth = azimuth_up_ref[...]
    per = 4
    for target in range(2):
        for difference in range(2):
            part = target if difference == 0 else 1 - target

            def one_kind(kind, carry, part=part, difference=difference):
                first = (kind * 2 + difference) * parents
                for pair in range(parents // 2):
                    stacked = []
                    for source, offset in ((part, 0), (1 - part, half)):
                        at = (offset + first + 2 * pair) * t_pad
                        stacked.append(
                            jnp.concatenate(
                                [wide[source, pl.ds(pl.multiple_of(at + i * t_pad, 8), t_pad), :] for i in range(2)],
                                axis=1,
                            )
                        )
                    high, low = split(jnp.concatenate(stacked, axis=0))
                    result = dot(polar[part], jnp.concatenate([high, low, high], axis=0))
                    high, low = split(result)
                    for i in range(2):
                        lanes = slice(i * f_pad, (i + 1) * f_pad)
                        rows_done[kind * 2 + difference, pl.ds((2 * pair + i) * p_pad, p_pad), :] = jnp.concatenate(
                            [high[:, lanes], low[:, lanes], high[:, lanes]], axis=1
                        )
                return carry

            lax.fori_loop(0, 2, one_kind, 0)

        def one_group(group, carry, target=target):
            at = pl.ds(pl.multiple_of(group * per * p_pad, 16), per * p_pad)
            y = dot(jnp.concatenate([rows_done[k, at, :] for k in range(4)], axis=0), azimuth)
            for i in range(per):
                terms = [y[(k * per + i) * p_pad : (k * per + i + 1) * p_pad] * phase_ref[k] for k in range(4)]
                if target == 0:
                    value = (terms[0] - terms[1]) + (terms[2] - terms[3])
                else:
                    value = (terms[0] + terms[1]) + (terms[2] + terms[3])
                at = pl.ds(pl.multiple_of((group * per + i) * 64 + target * 32 + step * 8, 8), 8)
                for lane_tile in range(lane_tiles):
                    lanes = slice(lane_tile * LANES, (lane_tile + 1) * LANES)
                    for row_tile in range(row_tiles):
                        tile = value[row_tile * 8 : row_tile * 8 + 8, lanes]
                        parent_out[lane_tile * row_tiles + row_tile, at, :] = tile
            return carry

        lax.fori_loop(0, parents // per, one_group, 0)

    @pl.when(step == 3)
    def _():
        def one_tile(tile, carry):
            box = tile // (p_pad // 16)
            row_pair = tile % (p_pad // 16)
            sources = [pl.ds(pl.multiple_of(source_ref[box, e] * 64, 64), 64) for e in range(entries)]
            kinds = [pl.ds(pl.multiple_of(kind_ref[box, e] * 16, 16), 16) for e in range(entries)]
            for lane_tile in range(lane_tiles):
                halves = []
                for i in range(2):
                    where = lane_tile * row_tiles + 2 * row_pair + i
                    total = [None] * 8
                    for e in range(entries):
                        x = parent_out[where, sources[e], :]
                        factor = table_by_kind[where, kinds[e], :]
                        real, imag = factor[:8], factor[8:]
                        for c in range(4):
                            xr, xi = x[c * 8 : c * 8 + 8], x[(4 + c) * 8 : (4 + c) * 8 + 8]
                            re = xr * real - xi * imag
                            im = xr * imag + xi * real
                            total[c] = re if e == 0 else total[c] + re
                            total[4 + c] = im if e == 0 else total[4 + c] + im
                    halves.append(total)
                for c in range(8):
                    high, low = split(jnp.concatenate([halves[0][c], halves[1][c]], axis=0))
                    at = pl.ds(pl.multiple_of((c * parents + box) * p_pad + row_pair * 16, 16), 16)
                    lanes = slice(lane_tile * LANES, (lane_tile + 1) * LANES)
                    in_high[at, lanes] = high
                    in_low[at, lanes] = low
            return carry

        lax.fori_loop(0, parents * (p_pad // 16), one_tile, 0)

        down = azimuth_down_ref[...]
        down_high = down[:, :f_pad]
        high, low = split(polar_down_ref[...])
        polar_back = jnp.concatenate([high, high, low], axis=1)
        per = parents

        def one_group(group, carry):
            at = pl.ds(pl.multiple_of(group * per * p_pad, 16), per * p_pad)
            high = in_high[at, :]
            low = in_low[at, :]
            both = dot(high, down)
            y = both[:, :f_pad] + both[:, f_pad:] + dot(low, down_high)
            for i in range(0, per, 2):
                x = jnp.concatenate([y[i * p_pad : (i + 1) * p_pad], y[(i + 1) * p_pad : (i + 2) * p_pad]], axis=1)
                high, low = split(x)
                z = dot(polar_back, jnp.concatenate([high, low, high], axis=0))
                for j in range(2):
                    lowered[pl.ds(pl.multiple_of(((i + j) * 8 + group) * t_pad, 8), t_pad), :] = z[
                        :, j * f_pad : (j + 1) * f_pad
                    ]
            return carry

        lax.fori_loop(0, 8 * parents // per, one_group, 0)

        per_turn = next(n for n in (6, 5, 3, 2, 1) if (rows + 6) % n == 0)

        def some_rows(i, carry):
            for r in range(per_turn):
                turned = lowered[pl.ds(i * per_turn + r, 8 * parents, stride=t_pad), :].T
                out_ref[i * per_turn + r] = turned[: columns + 8]
            return carry

        lax.fori_loop(0, (rows + 6) // per_turn, some_rows, 0)


def parent_level(child_out, after, before, side, table, sources, kinds, combine, polar_cos, polar_sin, phase):
    _, rows, columns, boxes = child_out.shape
    _, rows_up, columns_up, translators = table.shape
    assert boxes == LANES and translators == LANES
    parents, entries = sources.shape
    t_pad, p_pad = polar_cos.shape[1], polar_cos.shape[0]
    f_pad, q_pad = round_up(columns + 8, LANES), round_up(columns_up, LANES)
    assert f_pad == LANES
    table_steps = next(s for s in (4, 2, 1) if rows_up % s == 0)
    table_rows = rows_up // table_steps
    n_theta, n_phi = lax.axis_size("theta"), lax.axis_size("phi")
    polar_up = local_up(rows_up * n_theta, rows * n_theta, True, rows_up, rows, 3, (p_pad, t_pad))
    azimuth_up = local_up(columns_up * n_phi, columns * n_phi, False, columns_up, columns, 2, (q_pad, f_pad))
    high, low = split_constant(np.ascontiguousarray(azimuth_up.T))
    azimuth_three = jnp.asarray(np.concatenate([high, high, low], axis=0))
    high, low = split_constant(azimuth_up)
    azimuth_down = jnp.asarray(np.concatenate([high, low], axis=1))
    polar_down = jnp.asarray(np.ascontiguousarray(polar_up.T))

    def whole(array):
        return pl.BlockSpec(array.shape, lambda g: (0,) * array.ndim)

    def channel(shape):
        return pl.BlockSpec((2, 1) + shape, lambda g: (0, g, 0, 0, 0))

    smem = pl.BlockSpec(memory_space=pltpu.SMEM)
    constants = [combine, polar_cos, polar_sin, azimuth_three, polar_down, azimuth_down, phase]
    return pl.pallas_call(
        functools.partial(
            parent_kernel, (rows, columns, rows_up, columns_up, parents, entries, table_steps, table_rows)
        ),
        grid=(4,),
        in_specs=[
            smem,
            smem,
            channel((rows, columns, boxes)),
            channel((3, columns, boxes)),
            channel((3, columns, boxes)),
            channel((rows + 6, 8, boxes)),
            pl.BlockSpec(
                (2, table_rows, columns_up, translators), lambda g: (0, jnp.minimum(g, table_steps - 1), 0, 0)
            ),
        ]
        + [whole(c) for c in constants],
        out_specs=pl.BlockSpec((rows + 6, columns + 8, 8 * parents), lambda g: (0, 0, 0)),
        out_shape=jax.ShapeDtypeStruct((rows + 6, columns + 8, 8 * parents), F32),
        scratch_shapes=[
            pltpu.VMEM((2, 128 * t_pad, f_pad), F32),
            pltpu.VMEM((4, parents * p_pad, 3 * f_pad), BF16),
            pltpu.VMEM((q_pad // LANES * (p_pad // 8), translators * 16, LANES), F32),
            pltpu.VMEM((q_pad // LANES * (p_pad // 8), parents * 64, LANES), F32),
            pltpu.VMEM((8 * parents * p_pad, q_pad), BF16),
            pltpu.VMEM((8 * parents * p_pad, q_pad), BF16),
            pltpu.VMEM((8 * parents * t_pad, f_pad), F32),
        ],
        compiler_params=pltpu.CompilerParams(vmem_limit_bytes=60 * MIB),
        cost_estimate=pl.CostEstimate(
            flops=20_000_000_000, bytes_accessed=child_out.size * 8, transcendentals=0
        ),
        name="parent_level",
    )(
        sources,
        kinds,
        child_out.reshape((2, 4) + child_out.shape[1:]),
        after.reshape((2, 4) + after.shape[1:]),
        before.reshape((2, 4) + before.shape[1:]),
        side.reshape((2, 4) + side.shape[1:]),
        table,
        *constants,
    )


def chain(count, periodic):
    pairs = [(i, i + 1) for i in range(count - 1)]
    return pairs + [(count - 1, 0)] if periodic else pairs


def send(block, axis, up):
    pairs = chain(lax.axis_size(axis), axis == "phi")
    return lax.ppermute(block, axis, pairs if up else [(b, a) for a, b in pairs])


def per_device(
    child_out,
    child_slot,
    sources_child,
    kinds_child,
    table_child,
    sources_parent,
    kinds_parent,
    table_parent,
):
    _, rows, columns, boxes = child_out.shape
    _, rows_up, columns_up, _ = table_parent.shape
    parents = boxes // 8
    n_theta, n_phi = lax.axis_size("theta"), lax.axis_size("phi")
    t_pad, p_pad = round_up(rows + 6, 16), round_up(rows_up, 16)
    q_pad = round_up(columns_up, LANES)
    barrier = lax.optimization_barrier

    polar_up = local_up(rows_up * n_theta, rows * n_theta, True, rows_up, rows, 3, (p_pad, t_pad))
    sizes = (rows, columns, rows_up, columns_up, parents, n_theta, n_phi)
    combine, polar_cos, polar_sin, phase, phase_child = tables(
        child_slot, sizes, p_pad, t_pad, q_pad, jnp.asarray(polar_up)
    )

    samples = rows * columns
    flat_child = child_out.reshape(2, 4, samples, boxes)
    flat_table = table_child.reshape(2, samples, table_child.shape[3])
    pieces = segments(samples)
    local = [None] * len(pieces)
    chunks = [(n, i) for n, piece in enumerate(pieces) for i in range(piece[1])]

    def translate_next(child):
        if chunks:
            n, i = chunks.pop(0)
            local[n] = child_translate(
                child, flat_table, sources_child.T, kinds_child.T, pieces[n], i, local[n]
            )

    after = send(child_out[:, :3], "theta", False)
    before = send(child_out[:, rows - 3 :], "theta", True)
    translate_next(flat_child)
    after, before, local = barrier((after, before, local))

    low, high = (
        jnp.concatenate([edge[:, :, at] for edge in (child_out, after, before)], axis=1)
        for at in (slice(0, 3), slice(columns - 2, columns))
    )
    low, high, later_child = barrier((low, high, flat_child))
    right = send(low, "phi", False)
    left = send(high, "phi", True)
    if len(chunks) > 1:
        translate_next(later_child)
    right, left, local = barrier((right, left, local))
    side = jnp.concatenate([right, left, jnp.zeros((8, rows + 6, 3, boxes), F32)], axis=2)

    lowered = parent_level(
        child_out,
        after,
        before,
        side,
        table_parent,
        sources_parent,
        kinds_parent,
        combine,
        polar_cos,
        polar_sin,
        phase,
    )
    lowered, later_child = barrier((lowered, flat_child))

    low = send(lowered[rows : rows + 3], "theta", True)
    high = send(lowered[rows + 3 : rows + 6], "theta", False)
    while chunks:
        translate_next(later_child)
    local, lowered = barrier((local, lowered))
    here = lowered[:rows]
    here = here + jnp.pad(low, ((0, rows - 3), (0, 0), (0, 0))) + jnp.pad(high, ((rows - 3, 0), (0, 0), (0, 0)))
    low = send(here[:, columns : columns + 3], "phi", True)
    high = send(here[:, columns + 3 : columns + 5], "phi", False)
    here = here[:, :columns]
    here = here + jnp.pad(low, ((0, 0), (0, columns - 3), (0, 0))) + jnp.pad(high, ((0, 0), (columns - 2, 0), (0, 0)))
    here = here.reshape(samples, boxes)

    result = None
    for piece, part in zip(pieces, local):
        result = final_sum(flat_child.shape, part, here, phase_child, child_slot, piece, result)
    return result.reshape(child_out.shape)


def solution(mesh):
    placed = (
        P(None, "theta", "phi", None),
        P(),
        P(),
        P(),
        P(None, "theta", "phi", None),
        P(),
        P(),
        P(None, "theta", "phi", None),
    )
    return jax.shard_map(
        per_device,
        mesh=mesh,
        in_specs=placed,
        out_specs=P(None, "theta", "phi", None),
        check_vma=False,
    )
```

```python
import functools
import math

import jax
import jax.numpy as jnp
import numpy as np
from jax import lax
from jax.experimental import pallas as pl
from jax.experimental.layout import Layout, with_layout_constraint
from jax.experimental.pallas import tpu as pltpu
from jax.sharding import PartitionSpec as P

BAND1 = 180
WAVE = BAND1 / (2.0 * math.sqrt(3.0))
LANES = 128
MIB = 1 << 20
F32 = jnp.float32
BF16 = jnp.bfloat16


def round_up(count, step):
    return -(-count // step) * step


def stencil_entries(count_out, count_in, centered, out_rows):
    entries = []
    for row_out in out_rows:
        if centered:
            numerator = (2 * row_out + 1) * count_in - count_out
        else:
            numerator = 2 * row_out * count_in
        denominator = 2 * count_out
        base_index = numerator // denominator
        fraction = (numerator - base_index * denominator) / denominator
        for offset_a in range(-2, 4):
            weight = 1.0
            for offset_b in range(-2, 4):
                if offset_b != offset_a:
                    weight = weight * (fraction - offset_b) / (offset_a - offset_b)
            entries.append((row_out, base_index + offset_a, weight))
    return entries


def local_up(count_out, count_in, centered, rows_out, rows_in, below, shape):
    matrix = np.zeros(shape)
    for row_out, column, weight in stencil_entries(count_out, count_in, centered, range(rows_out)):
        assert -below <= column < rows_in + 3 or abs(weight) < 1e-12
        if column >= 0:
            matrix[row_out, column] += weight
        elif column >= -below:
            matrix[row_out, rows_in + 3 + below + column] += weight
    return matrix.astype(np.float32)


def split(x):
    high = x.astype(BF16)
    return high, (x - high.astype(F32)).astype(BF16)


def split_constant(matrix):
    high = matrix.astype(jnp.bfloat16)
    return high, (matrix - high.astype(np.float32)).astype(jnp.bfloat16)


def dot(a, b):
    return jnp.dot(a, b, preferred_element_type=F32)


def dot_transposed(a, b):
    return lax.dot_general(a, b, (((1,), (1,)), ((), ())), preferred_element_type=F32)


def segments(samples):
    full, rest = divmod(samples, 8 * LANES)
    found = [(0, full, 1, 8)] if full else []
    if rest:
        rows = -(-rest // LANES)
        packed = 4 if rows <= 2 else 2 if rows <= 4 else 1
        found.append((full, 1, packed, rows))
    return found


def translate_kernel(packed, rows, source_ref, kind_ref, child_ref, table_ref, *rest):
    out_ref, pattern, table = rest[-3:]
    groups, per = 4 // packed, 8 // packed
    tile = 16 * groups
    pitch = tile + 8
    entries = source_ref.shape[0]
    step = pl.program_id(0)

    @pl.when(step == 0)
    def _():
        for row in range(rows):
            for part in range(2):
                turned = table_ref[part, row * LANES : (row + 1) * LANES].T
                for c in range(packed):
                    table[part, pl.ds(c * per + row, LANES, stride=8), :] = turned

    @pl.when(step < 2)
    def _():
        for i in range(2):
            c = 2 * step + i
            plane, sub = (c, 0) if packed == 1 else (c // packed, c % packed * per)
            for part in range(2):
                for row in range(rows):
                    at = pl.ds((part * groups + plane) * 8 + sub + row, LANES, stride=pitch)
                    pattern[at, :] = child_ref[part, i, row * LANES : (row + 1) * LANES].T

    @pl.when(step >= 2)
    def _():
        half = LANES // 2

        def one_box(i, carry):
            box = (step - 2) * half + i
            total = [None] * (2 * groups)
            for entry in range(entries):
                x = pattern[pl.ds(pl.multiple_of(source_ref[entry, box] * pitch, 8), tile), :]
                kind = pl.ds(pl.multiple_of(kind_ref[entry, box] * 8, 8), 8)
                real, imag = table[0, kind, :], table[1, kind, :]
                for g in range(groups):
                    xr, xi = x[g * 8 : g * 8 + 8], x[(groups + g) * 8 : (groups + g) * 8 + 8]
                    re = xr * real - xi * imag
                    im = xr * imag + xi * real
                    total[g] = re if entry == 0 else total[g] + re
                    total[groups + g] = im if entry == 0 else total[groups + g] + im
            for g in range(2 * groups):
                out_ref[0, pl.ds(pl.multiple_of(i * tile, tile) + g * 8, 8), :] = total[g]
            return carry

        lax.fori_loop(0, half, one_box, 0, unroll=2)


def child_translate(child, table, sources, kinds, segment, chunk, onto):
    first, count, packed, rows = segment
    tile = 64 // packed
    smem = pl.BlockSpec(memory_space=pltpu.SMEM)
    in_specs = [
        smem,
        smem,
        pl.BlockSpec((2, 2, 8 * LANES, LANES), lambda s: (0, jnp.minimum(s, 1), first + chunk, 0)),
        pl.BlockSpec((2, 8 * LANES, LANES), lambda s: (0, first + chunk, 0)),
    ]
    operands = [sources, kinds, child, table]
    aliases = {}
    if onto is not None:
        in_specs.append(pl.BlockSpec(memory_space=pl.ANY))
        operands.append(onto)
        aliases = {4: 0}
    work = rows * LANES * LANES
    return pl.pallas_call(
        functools.partial(translate_kernel, packed, rows),
        grid=(4,),
        in_specs=in_specs,
        out_specs=pl.BlockSpec((1, LANES // 2 * tile, LANES), lambda s: (chunk, jnp.maximum(s - 2, 0), 0)),
        out_shape=jax.ShapeDtypeStruct((count, LANES * tile, LANES), F32),
        input_output_aliases=aliases,
        scratch_shapes=[pltpu.VMEM((LANES * (tile + 8), LANES), F32), pltpu.VMEM((2, LANES * 8, LANES), F32)],
        compiler_params=pltpu.CompilerParams(vmem_limit_bytes=60 * MIB),
        cost_estimate=pl.CostEstimate(
            flops=work * sources.shape[0] * 32, bytes_accessed=work * 72, transcendentals=0
        ),
        name="child_translate",
    )(*operands)


def sum_kernel(packed, rows, parents, slot_ref, local_ref, lowered_ref, phase_ref, *rest):
    out_ref, lowered, total = rest[-3:]
    groups, per = 4 // packed, 8 // packed
    tile = 16 * groups
    pitch = tile + 8
    step = pl.program_id(1)

    @pl.when(step == 0)
    def _():
        for row in range(rows):
            lowered[pl.ds(row, LANES, stride=8), :] = lowered_ref[row * LANES : (row + 1) * LANES].T

    @pl.when(step < 2)
    def _():
        half = LANES // 2

        def one_box(i, carry):
            slot = slot_ref[step * half + i]
            octant = slot // parents
            cosine, sine = phase_ref[octant][:per], phase_ref[8 + octant][:per]
            x = lowered[pl.ds(pl.multiple_of(slot % parents * 64, 64), 64), :]
            local = local_ref[0, pl.ds(pl.multiple_of(i * tile, tile), tile), :]
            for c in range(4):
                real, imag = x[c * 8 : c * 8 + per], x[(4 + c) * 8 : (4 + c) * 8 + per]
                at = c // packed * 8 + c % packed * per
                here = pl.multiple_of((step * half + i) * pitch, 8)
                total[pl.ds(here + at, per), :] = local[at : at + per] + (real * cosine + imag * sine)
                at += groups * 8
                total[pl.ds(here + at, per), :] = local[at : at + per] + (imag * cosine - real * sine)
            return carry

        lax.fori_loop(0, half, one_box, 0, unroll=4)

    @pl.when(step >= 2)
    def _():
        for i in range(2):
            c = 2 * (step - 2) + i
            plane, sub = (c, 0) if packed == 1 else (c // packed, c % packed * per)
            for part in range(2):
                for row in range(rows):
                    at = pl.ds((part * groups + plane) * 8 + sub + row, LANES, stride=pitch)
                    out_ref[part, i, row * LANES : (row + 1) * LANES] = total[at, :].T


def final_sum(shape, local, lowered, phase, slots, segment, onto):
    first, count, packed, rows = segment
    tile = 64 // packed
    in_specs = [
        pl.BlockSpec(memory_space=pltpu.SMEM),
        pl.BlockSpec((1, LANES // 2 * tile, LANES), lambda i, s: (i, jnp.minimum(s, 1), 0)),
        pl.BlockSpec((8 * LANES, LANES), lambda i, s: (first + i, 0)),
        pl.BlockSpec((16, 8, LANES), lambda i, s: (0, first + i, 0)),
    ]
    operands = [slots, local, lowered, phase]
    aliases = {}
    if onto is not None:
        in_specs.append(pl.BlockSpec(memory_space=pl.ANY))
        operands.append(onto)
        aliases = {4: 0}
    work = count * rows * LANES * LANES
    return pl.pallas_call(
        functools.partial(sum_kernel, packed, rows, LANES // 8),
        grid=(count, 4),
        in_specs=in_specs,
        out_specs=pl.BlockSpec((2, 2, 8 * LANES, LANES), lambda i, s: (0, jnp.maximum(s - 2, 0), first + i, 0)),
        out_shape=jax.ShapeDtypeStruct(shape, F32),
        input_output_aliases=aliases,
        scratch_shapes=[pltpu.VMEM((8 * LANES, LANES), F32), pltpu.VMEM((LANES * (tile + 8), LANES), F32)],
        compiler_params=pltpu.CompilerParams(vmem_limit_bytes=60 * MIB),
        cost_estimate=pl.CostEstimate(flops=work * 32, bytes_accessed=work * 72, transcendentals=0),
        name="final_sum",
    )(*operands)


def cos_sin(x):
    turns = jnp.floor(x * (2.0 / math.pi) + 0.5)
    rest = ((x - turns * 1.5703125) - turns * 4.837512969970703e-4) - turns * 7.54978995489188e-8
    square = rest * rest
    sine = rest + rest * square * (
        -1.6666654611e-1 + square * (8.3321608736e-3 + square * -1.9515295891e-4)
    )
    cosine = (1.0 - 0.5 * square) + square * square * (
        4.166664568298827e-2 + square * (-1.388731625493765e-3 + square * 2.443315711809948e-5)
    )
    quarter = turns.astype(jnp.int32)
    odd = (quarter & 1) == 1
    first, second = jnp.where(odd, sine, cosine), jnp.where(odd, cosine, sine)
    first = jnp.where(((quarter + 1) & 2) == 2, -first, first)
    second = jnp.where((quarter & 2) == 2, -second, second)
    return first, second


def tables_kernel(sizes, slot_ref, polar_up_ref, combine_ref, cos_ref, sin_ref, phase_ref, child_ref):
    rows, columns, rows_up, columns_up, parents, n_theta, n_phi = sizes
    polar_index, azimuth_index = lax.axis_index("theta"), lax.axis_index("phi")

    def iota(shape, axis):
        return lax.broadcasted_iota(jnp.int32, shape, axis)

    boxes = slot_ref.shape[1]
    slot = jnp.broadcast_to(slot_ref[...], (parents, boxes))
    same = (slot & (parents - 1)) == iota((parents, boxes), 0)
    octant = slot >> (parents.bit_length() - 1)
    east, north, upper = (2 * ((octant >> n) & 1) - 1 for n in range(3))
    blocks = []
    for z in range(2):
        for kind in range(2):
            for difference in range(2):
                chosen = same & ((east == north) if kind == 0 else (east != north))
                weight = (upper if z else 1) * (east if difference else 1)
                weight = jnp.where(chosen, weight, 0).astype(F32)
                blocks.append(weight)
    combine = jnp.concatenate(blocks, axis=0).astype(BF16)
    combine_ref[...] = jnp.concatenate([combine, combine], axis=1)

    p_pad, t_pad = cos_ref.shape
    q_pad = phase_ref.shape[2]
    polar = (iota((p_pad, LANES), 0) + polar_index * rows_up).astype(F32) + 0.5
    cosine, sine = cos_sin(polar * (math.pi / (rows_up * n_theta)))
    up_cos, up_sin = cos_sin(WAVE * cosine)
    cos_ref[...] = polar_up_ref[...] * up_cos[:, :t_pad]
    sin_ref[...] = polar_up_ref[...] * up_sin[:, :t_pad]
    azimuth = (iota((8, q_pad), 1) + azimuth_index * columns_up).astype(F32)
    east, north = cos_sin(azimuth * (2.0 * math.pi / (columns_up * n_phi)))
    flat = WAVE * sine
    valid = iota((p_pad, LANES), 0) < rows_up
    for lane in range(0, q_pad, LANES):
        lanes = slice(lane, lane + LANES)
        inside = valid & (iota((p_pad, LANES), 1) + lane < columns_up)
        for kind in range(2):
            turned = (east - north if kind else east + north)[:1, lanes]
            found = cos_sin(flat * turned)
            for i in range(2):
                phase_ref[2 * kind + i, :, lanes] = jnp.where(inside, found[i], 0.0)

    count = child_ref.shape[1]
    sample = iota((count, LANES), 0) * LANES + iota((count, LANES), 1)
    row = jnp.floor((sample.astype(F32) + 0.5) * (1.0 / columns))
    polar = row + (polar_index * rows).astype(F32) + 0.5
    azimuth = sample.astype(F32) - row * columns + (azimuth_index * columns).astype(F32)
    up, flat = cos_sin(polar * (math.pi / (rows * n_theta)))
    east, north = cos_sin(azimuth * (2.0 * math.pi / (columns * n_phi)))
    for octant in range(4):
        signs = [2 * ((octant >> n) & 1) - 1 for n in range(3)]
        found = cos_sin(WAVE * (flat * east * signs[0] + flat * north * signs[1] + up * signs[2]))
        child_ref[octant] = found[0]
        child_ref[7 - octant] = found[0]
        child_ref[8 + octant] = found[1]
        child_ref[15 - octant] = -found[1]


def tables(slots, sizes, p_pad, t_pad, q_pad, polar_up):
    rows, columns, rows_up, columns_up, parents, n_theta, n_phi = sizes
    boxes = slots.shape[0]
    assert parents & (parents - 1) == 0
    return pl.pallas_call(
        functools.partial(tables_kernel, sizes),
        out_shape=[
            jax.ShapeDtypeStruct((8 * parents, 2 * boxes), BF16),
            jax.ShapeDtypeStruct((p_pad, t_pad), F32),
            jax.ShapeDtypeStruct((p_pad, t_pad), F32),
            jax.ShapeDtypeStruct((4, p_pad, q_pad), F32),
            jax.ShapeDtypeStruct((16, -(-rows * columns // LANES), LANES), F32),
        ],
        compiler_params=pltpu.CompilerParams(vmem_limit_bytes=60 * MIB),
        name="tables",
    )(slots.reshape(1, boxes), polar_up)


def parent_kernel(
    sizes,
    source_ref,
    kind_ref,
    child_ref,
    next_ref,
    previous_ref,
    side_ref,
    table_ref,
    combine_ref,
    polar_cos_ref,
    polar_sin_ref,
    azimuth_up_ref,
    polar_down_ref,
    azimuth_down_ref,
    phase_ref,
    out_ref,
    wide,
    rows_done,
    table_by_kind,
    parent_out,
    in_high,
    in_low,
    lowered,
):
    (rows, columns, rows_up, columns_up, parents, entries, table_steps, table_rows) = sizes
    pitch, f_pad = wide.shape[1] // 128, wide.shape[2]
    t_pad = pitch - 8
    p_pad, q_pad = phase_ref.shape[1], phase_ref.shape[2]
    row_tiles, lane_tiles = p_pad // 8, q_pad // LANES
    step = pl.program_id(0)
    half = 4 * parents
    table_first = jnp.minimum(step, table_steps - 1) * table_rows

    @pl.when(step == 0)
    def _():
        for part in range(2):
            for t in range(rows + 6, t_pad):
                wide[part, pl.ds(t, 128, stride=pitch), :] = jnp.zeros((128, f_pad), F32)
        for part in range(2):
            for p in range(rows_up, p_pad):
                for lane_tile in range(lane_tiles):
                    at = pl.ds(p % 8, 128, stride=8)
                    table_by_kind[lane_tile * row_tiles + p // 8, part, at, :] = jnp.zeros((128, LANES), F32)

    combine = combine_ref[...]

    def samples(part, main_ref, r, t):
        x = jnp.concatenate(
            [main_ref[part, 0, r], side_ref[part, 0, t], jnp.zeros((f_pad - columns - 8, LANES), F32)], axis=0
        )
        high, low = split(x)
        return jnp.concatenate([high, low], axis=1)

    def turn(pieces):
        for part in range(2):
            for i in range(0, len(pieces), 2):
                both = jnp.concatenate([samples(part, *piece) for piece in pieces[i : i + 2]], axis=0)
                turned = dot_transposed(combine, both)
                for j, piece in enumerate(pieces[i : i + 2]):
                    at = pl.ds(piece[2], 128, stride=pitch)
                    wide[part, at, :] = turned[:, j * f_pad : (j + 1) * f_pad]

    per_turn = next(n for n in (4, 3, 2, 1) if rows % n == 0)

    turns = rows // per_turn
    table_per_turn = -(-table_rows // turns)

    def main_rows(i, carry):
        turn([(child_ref, per_turn * i + r, per_turn * i + r) for r in range(per_turn)])
        for j in range(table_per_turn):
            r = jnp.minimum(i * table_per_turn + j, table_rows - 1)
            for part in range(2):
                x = table_ref[part, r]
                if q_pad > columns_up:
                    x = jnp.concatenate([x, jnp.zeros((q_pad - columns_up, LANES), F32)], axis=0)
                for lane in range(0, q_pad, LANES):
                    turned = x[lane : lane + LANES].T
                    p = table_first + r
                    at = pl.ds(p % 8, 128, stride=8)
                    table_by_kind[lane // LANES * row_tiles + p // 8, part, at, :] = turned
        return carry

    lax.fori_loop(0, turns, main_rows, 0)
    turn([(next_ref, r, rows + r) for r in range(3)] + [(previous_ref, r, rows + 3 + r) for r in range(3)])

    polar = []
    for sign in (-1.0, 1.0):
        both = jnp.concatenate([polar_cos_ref[...], sign * polar_sin_ref[...]], axis=1)
        high, low = split(both)
        polar.append(jnp.concatenate([high, high, low], axis=1))
    azimuth = azimuth_up_ref[...]
    per = 4
    for target in range(2):
        for difference in range(2):
            part = target if difference == 0 else 1 - target

            def one_kind(kind, carry, part=part, difference=difference):
                first = (kind * 2 + difference) * parents
                for pair in range(parents // 2):
                    stacked = []
                    for source, offset in ((part, 0), (1 - part, half)):
                        at = (offset + first + 2 * pair) * pitch
                        stacked.append(
                            jnp.concatenate(
                                [wide[source, pl.ds(pl.multiple_of(at + i * pitch, 8), t_pad), :] for i in range(2)],
                                axis=1,
                            )
                        )
                    high, low = split(jnp.concatenate(stacked, axis=0))
                    result = dot(polar[part], jnp.concatenate([high, low, high], axis=0))
                    high, low = split(result)
                    for i in range(2):
                        lanes = slice(i * f_pad, (i + 1) * f_pad)
                        rows_done[kind * 2 + difference, pl.ds((2 * pair + i) * p_pad, p_pad), :] = jnp.concatenate(
                            [high[:, lanes], low[:, lanes], high[:, lanes]], axis=1
                        )
                return carry

            lax.fori_loop(0, 2, one_kind, 0)

        def one_group(group, carry, target=target):
            at = pl.ds(pl.multiple_of(group * per * p_pad, 16), per * p_pad)
            y = dot(jnp.concatenate([rows_done[k, at, :] for k in range(4)], axis=0), azimuth)
            for i in range(per):
                terms = [y[(k * per + i) * p_pad : (k * per + i + 1) * p_pad] * phase_ref[k] for k in range(4)]
                if target == 0:
                    value = (terms[0] - terms[1]) + (terms[2] - terms[3])
                else:
                    value = (terms[0] + terms[1]) + (terms[2] + terms[3])
                at = pl.ds(pl.multiple_of((group * per + i) * 64 + target * 32 + step * 8, 8), 8)
                for lane_tile in range(lane_tiles):
                    lanes = slice(lane_tile * LANES, (lane_tile + 1) * LANES)
                    for row_tile in range(row_tiles):
                        tile = value[row_tile * 8 : row_tile * 8 + 8, lanes]
                        parent_out[lane_tile * row_tiles + row_tile, at, :] = tile
            return carry

        lax.fori_loop(0, parents // per, one_group, 0)

    @pl.when(step == 3)
    def _():
        def one_tile(tile, carry):
            box = tile // (p_pad // 16)
            row_pair = tile % (p_pad // 16)
            sources = [pl.ds(pl.multiple_of(source_ref[box, e] * 64, 64), 64) for e in range(entries)]
            kinds = [pl.ds(pl.multiple_of(kind_ref[box, e] * 8, 8), 8) for e in range(entries)]
            for lane_tile in range(lane_tiles):
                halves = []
                for i in range(2):
                    where = lane_tile * row_tiles + 2 * row_pair + i
                    total = [None] * 8
                    for e in range(entries):
                        x = parent_out[where, sources[e], :]
                        real, imag = (table_by_kind[where, part, kinds[e], :] for part in range(2))
                        for c in range(4):
                            xr, xi = x[c * 8 : c * 8 + 8], x[(4 + c) * 8 : (4 + c) * 8 + 8]
                            re = xr * real - xi * imag
                            im = xr * imag + xi * real
                            total[c] = re if e == 0 else total[c] + re
                            total[4 + c] = im if e == 0 else total[4 + c] + im
                    halves.append(total)
                for c in range(8):
                    high, low = split(jnp.concatenate([halves[0][c], halves[1][c]], axis=0))
                    at = pl.ds(pl.multiple_of((c * parents + box) * p_pad + row_pair * 16, 16), 16)
                    lanes = slice(lane_tile * LANES, (lane_tile + 1) * LANES)
                    in_high[at, lanes] = high
                    in_low[at, lanes] = low
            return carry

        lax.fori_loop(0, parents * (p_pad // 16), one_tile, 0)

        down = azimuth_down_ref[...]
        down_high = down[:, :f_pad]
        high, low = split(polar_down_ref[...])
        polar_back = jnp.concatenate([high, high, low], axis=1)
        per = parents

        def one_group(group, carry):
            at = pl.ds(pl.multiple_of(group * per * p_pad, 16), per * p_pad)
            high = in_high[at, :]
            low = in_low[at, :]
            both = dot(high, down)
            y = both[:, :f_pad] + both[:, f_pad:] + dot(low, down_high)
            for i in range(0, per, 2):
                x = jnp.concatenate([y[i * p_pad : (i + 1) * p_pad], y[(i + 1) * p_pad : (i + 2) * p_pad]], axis=1)
                high, low = split(x)
                z = dot(polar_back, jnp.concatenate([high, low, high], axis=0))
                for j in range(2):
                    lowered[pl.ds(pl.multiple_of(((i + j) * 8 + group) * pitch, 8), t_pad), :] = z[
                        :, j * f_pad : (j + 1) * f_pad
                    ]
            return carry

        lax.fori_loop(0, 8 * parents // per, one_group, 0)

        per_turn = next(n for n in (6, 5, 3, 2, 1) if (rows + 6) % n == 0)

        def some_rows(i, carry):
            for r in range(per_turn):
                turned = lowered[pl.ds(i * per_turn + r, 8 * parents, stride=pitch), :].T
                out_ref[i * per_turn + r] = turned[: columns + 8]
            return carry

        lax.fori_loop(0, (rows + 6) // per_turn, some_rows, 0)


def parent_level(child_out, after, before, side, table, sources, kinds, combine, polar_cos, polar_sin, phase):
    _, rows, columns, boxes = child_out.shape
    _, rows_up, columns_up, translators = table.shape
    assert boxes == LANES and translators == LANES
    parents, entries = sources.shape
    t_pad, p_pad = polar_cos.shape[1], polar_cos.shape[0]
    f_pad, q_pad = round_up(columns + 8, LANES), round_up(columns_up, LANES)
    assert f_pad == LANES
    table_steps = next(s for s in (4, 2, 1) if rows_up % s == 0)
    table_rows = rows_up // table_steps
    n_theta, n_phi = lax.axis_size("theta"), lax.axis_size("phi")
    polar_up = local_up(rows_up * n_theta, rows * n_theta, True, rows_up, rows, 3, (p_pad, t_pad))
    azimuth_up = local_up(columns_up * n_phi, columns * n_phi, False, columns_up, columns, 2, (q_pad, f_pad))
    high, low = split_constant(np.ascontiguousarray(azimuth_up.T))
    azimuth_three = jnp.asarray(np.concatenate([high, high, low], axis=0))
    high, low = split_constant(azimuth_up)
    azimuth_down = jnp.asarray(np.concatenate([high, low], axis=1))
    polar_down = jnp.asarray(np.ascontiguousarray(polar_up.T))

    def whole(array):
        return pl.BlockSpec(array.shape, lambda g: (0,) * array.ndim)

    def channel(shape):
        return pl.BlockSpec((2, 1) + shape, lambda g: (0, g, 0, 0, 0))

    smem = pl.BlockSpec(memory_space=pltpu.SMEM)
    constants = [combine, polar_cos, polar_sin, azimuth_three, polar_down, azimuth_down, phase]
    return pl.pallas_call(
        functools.partial(
            parent_kernel, (rows, columns, rows_up, columns_up, parents, entries, table_steps, table_rows)
        ),
        grid=(4,),
        in_specs=[
            smem,
            smem,
            channel((rows, columns, boxes)),
            channel((3, columns, boxes)),
            channel((3, columns, boxes)),
            channel((rows + 6, 8, boxes)),
            pl.BlockSpec(
                (2, table_rows, columns_up, translators), lambda g: (0, jnp.minimum(g, table_steps - 1), 0, 0)
            ),
        ]
        + [whole(c) for c in constants],
        out_specs=pl.BlockSpec((rows + 6, columns + 8, 8 * parents), lambda g: (0, 0, 0)),
        out_shape=jax.ShapeDtypeStruct((rows + 6, columns + 8, 8 * parents), F32),
        scratch_shapes=[
            pltpu.VMEM((2, 128 * (t_pad + 8), f_pad), F32),
            pltpu.VMEM((4, parents * p_pad, 3 * f_pad), BF16),
            pltpu.VMEM((q_pad // LANES * (p_pad // 8), 2, translators * 8, LANES), F32),
            pltpu.VMEM((q_pad // LANES * (p_pad // 8), parents * 64, LANES), F32),
            pltpu.VMEM((8 * parents * p_pad, q_pad), BF16),
            pltpu.VMEM((8 * parents * p_pad, q_pad), BF16),
            pltpu.VMEM((8 * parents * (t_pad + 8), f_pad), F32),
        ],
        compiler_params=pltpu.CompilerParams(vmem_limit_bytes=60 * MIB),
        cost_estimate=pl.CostEstimate(
            flops=20_000_000_000, bytes_accessed=child_out.size * 8, transcendentals=0
        ),
        name="parent_level",
    )(
        sources,
        kinds,
        child_out.reshape((2, 4) + child_out.shape[1:]),
        after.reshape((2, 4) + after.shape[1:]),
        before.reshape((2, 4) + before.shape[1:]),
        side.reshape((2, 4) + side.shape[1:]),
        table,
        *constants,
    )


def chain(count, periodic):
    pairs = [(i, i + 1) for i in range(count - 1)]
    return pairs + [(count - 1, 0)] if periodic else pairs


def send(block, axis, up):
    pairs = chain(lax.axis_size(axis), axis == "phi")
    return lax.ppermute(block, axis, pairs if up else [(b, a) for a, b in pairs])


def plain(array):
    return with_layout_constraint(array, Layout(major_to_minor=tuple(range(array.ndim))))


def per_device(
    child_out,
    child_slot,
    sources_child,
    kinds_child,
    table_child,
    sources_parent,
    kinds_parent,
    table_parent,
):
    _, rows, columns, boxes = child_out.shape
    _, rows_up, columns_up, _ = table_parent.shape
    parents = boxes // 8
    n_theta, n_phi = lax.axis_size("theta"), lax.axis_size("phi")
    t_pad, p_pad = round_up(rows + 6, 16), round_up(rows_up, 16)
    q_pad = round_up(columns_up, LANES)
    barrier = lax.optimization_barrier

    polar_up = local_up(rows_up * n_theta, rows * n_theta, True, rows_up, rows, 3, (p_pad, t_pad))
    sizes = (rows, columns, rows_up, columns_up, parents, n_theta, n_phi)
    combine, polar_cos, polar_sin, phase, phase_child = tables(
        child_slot, sizes, p_pad, t_pad, q_pad, jnp.asarray(polar_up)
    )

    samples = rows * columns
    flat_child = child_out.reshape(2, 4, samples, boxes)
    flat_table = table_child.reshape(2, samples, table_child.shape[3])
    pieces = segments(samples)
    local = [None] * len(pieces)
    chunks = [(n, i) for n, piece in enumerate(pieces) for i in range(piece[1])]

    def translate_next(child):
        if chunks:
            n, i = chunks.pop(0)
            local[n] = child_translate(
                child, flat_table, sources_child.T, kinds_child.T, pieces[n], i, local[n]
            )

    after = plain(send(plain(child_out[:, :3]), "theta", False))
    before = plain(send(plain(child_out[:, rows - 3 :]), "theta", True))
    translate_next(flat_child)
    after, before, local = barrier((after, before, local))

    low, high = (
        jnp.concatenate([edge[:, :, at] for edge in (child_out, after, before)], axis=1)
        for at in (slice(0, 3), slice(columns - 2, columns))
    )
    low, high, later_child = barrier((low, high, flat_child))
    right = send(low, "phi", False)
    left = send(high, "phi", True)
    if len(chunks) > 1:
        translate_next(later_child)
    right, left, local = barrier((right, left, local))
    side = jnp.concatenate([right, left, jnp.zeros((8, rows + 6, 3, boxes), F32)], axis=2)

    lowered = parent_level(
        child_out,
        after,
        before,
        side,
        table_parent,
        sources_parent,
        kinds_parent,
        combine,
        polar_cos,
        polar_sin,
        phase,
    )
    lowered, later_child = barrier((lowered, flat_child))

    low = send(lowered[rows : rows + 3], "theta", True)
    high = send(lowered[rows + 3 : rows + 6], "theta", False)
    while chunks:
        translate_next(later_child)
    local, lowered = barrier((local, lowered))
    here = lowered[:rows]
    here = here + jnp.pad(low, ((0, rows - 3), (0, 0), (0, 0))) + jnp.pad(high, ((rows - 3, 0), (0, 0), (0, 0)))
    low = send(here[:, columns : columns + 3], "phi", True)
    high = send(here[:, columns + 3 : columns + 5], "phi", False)
    here = here[:, :columns]
    here = here + jnp.pad(low, ((0, 0), (0, columns - 3), (0, 0))) + jnp.pad(high, ((0, 0), (columns - 2, 0), (0, 0)))
    here = here.reshape(samples, boxes)

    result = None
    for piece, part in zip(pieces, local):
        result = final_sum(flat_child.shape, part, here, phase_child, child_slot, piece, result)
    return result.reshape(child_out.shape)


def solution(mesh):
    placed = (
        P(None, "theta", "phi", None),
        P(),
        P(),
        P(),
        P(None, "theta", "phi", None),
        P(),
        P(),
        P(None, "theta", "phi", None),
    )
    return jax.shard_map(
        per_device,
        mesh=mesh,
        in_specs=placed,
        out_specs=P(None, "theta", "phi", None),
        check_vma=False,
    )
```

```python
import functools
import math

import jax
import jax.numpy as jnp
import numpy as np
from jax import lax
from jax.experimental import pallas as pl
from jax.experimental.layout import Layout, with_layout_constraint
from jax.experimental.pallas import tpu as pltpu
from jax.sharding import PartitionSpec as P

BAND1 = 180
WAVE = BAND1 / (2.0 * math.sqrt(3.0))
LANES = 128
MIB = 1 << 20
F32 = jnp.float32
BF16 = jnp.bfloat16


def round_up(count, step):
    return -(-count // step) * step


def stencil_entries(count_out, count_in, centered, out_rows):
    entries = []
    for row_out in out_rows:
        if centered:
            numerator = (2 * row_out + 1) * count_in - count_out
        else:
            numerator = 2 * row_out * count_in
        denominator = 2 * count_out
        base_index = numerator // denominator
        fraction = (numerator - base_index * denominator) / denominator
        for offset_a in range(-2, 4):
            weight = 1.0
            for offset_b in range(-2, 4):
                if offset_b != offset_a:
                    weight = weight * (fraction - offset_b) / (offset_a - offset_b)
            entries.append((row_out, base_index + offset_a, weight))
    return entries


def local_up(count_out, count_in, centered, rows_out, rows_in, below, shape):
    matrix = np.zeros(shape)
    for row_out, column, weight in stencil_entries(count_out, count_in, centered, range(rows_out)):
        assert -below <= column < rows_in + 3 or abs(weight) < 1e-12
        if column >= 0:
            matrix[row_out, column] += weight
        elif column >= -below:
            matrix[row_out, rows_in + 3 + below + column] += weight
    return matrix.astype(np.float32)


def split(x):
    high = x.astype(BF16)
    return high, (x - high.astype(F32)).astype(BF16)


def split_constant(matrix):
    high = matrix.astype(jnp.bfloat16)
    return high, (matrix - high.astype(np.float32)).astype(jnp.bfloat16)


def dot(a, b):
    return jnp.dot(a, b, preferred_element_type=F32)


def dot_transposed(a, b):
    return lax.dot_general(a, b, (((1,), (1,)), ((), ())), preferred_element_type=F32)


def segments(samples):
    full, rest = divmod(samples, 8 * LANES)
    found = [(0, full, 1, 8)] if full else []
    if rest:
        rows = -(-rest // LANES)
        packed = 4 if rows <= 2 else 2 if rows <= 4 else 1
        found.append((full, 1, packed, rows))
    return found


def translate_kernel(packed, rows, source_ref, kind_ref, child_ref, table_ref, *rest):
    out_ref, pattern, table = rest[-3:]
    groups, per = 4 // packed, 8 // packed
    tile = 16 * groups
    pitch = tile + 8
    entries = source_ref.shape[0]
    step = pl.program_id(0)

    @pl.when(step == 0)
    def _():
        for row in range(rows):
            for part in range(2):
                turned = table_ref[part, row * LANES : (row + 1) * LANES].T
                for c in range(packed):
                    table[part, pl.ds(c * per + row, LANES, stride=8), :] = turned

    @pl.when(step < 2)
    def _():
        for i in range(2):
            c = 2 * step + i
            plane, sub = (c, 0) if packed == 1 else (c // packed, c % packed * per)
            for part in range(2):
                for row in range(rows):
                    at = pl.ds((part * groups + plane) * 8 + sub + row, LANES, stride=pitch)
                    pattern[at, :] = child_ref[part, i, row * LANES : (row + 1) * LANES].T

    @pl.when(step >= 2)
    def _():
        half = LANES // 2

        def one_box(i, carry):
            box = (step - 2) * half + i
            total = [None] * (2 * groups)
            for entry in range(entries):
                x = pattern[pl.ds(pl.multiple_of(source_ref[entry, box] * pitch, 8), tile), :]
                kind = pl.ds(pl.multiple_of(kind_ref[entry, box] * 8, 8), 8)
                real, imag = table[0, kind, :], table[1, kind, :]
                for g in range(groups):
                    xr, xi = x[g * 8 : g * 8 + 8], x[(groups + g) * 8 : (groups + g) * 8 + 8]
                    re = xr * real - xi * imag
                    im = xr * imag + xi * real
                    total[g] = re if entry == 0 else total[g] + re
                    total[groups + g] = im if entry == 0 else total[groups + g] + im
            for g in range(2 * groups):
                out_ref[0, pl.ds(pl.multiple_of(i * tile, tile) + g * 8, 8), :] = total[g]
            return carry

        lax.fori_loop(0, half, one_box, 0, unroll=2)


def child_translate(child, table, sources, kinds, segment, chunk, onto):
    first, count, packed, rows = segment
    tile = 64 // packed
    smem = pl.BlockSpec(memory_space=pltpu.SMEM)
    in_specs = [
        smem,
        smem,
        pl.BlockSpec((2, 2, 8 * LANES, LANES), lambda s: (0, jnp.minimum(s, 1), first + chunk, 0)),
        pl.BlockSpec((2, 8 * LANES, LANES), lambda s: (0, first + chunk, 0)),
    ]
    operands = [sources, kinds, child, table]
    aliases = {}
    if onto is not None:
        in_specs.append(pl.BlockSpec(memory_space=pl.ANY))
        operands.append(onto)
        aliases = {4: 0}
    work = rows * LANES * LANES
    return pl.pallas_call(
        functools.partial(translate_kernel, packed, rows),
        grid=(4,),
        in_specs=in_specs,
        out_specs=pl.BlockSpec((1, LANES // 2 * tile, LANES), lambda s: (chunk, jnp.maximum(s - 2, 0), 0)),
        out_shape=jax.ShapeDtypeStruct((count, LANES * tile, LANES), F32),
        input_output_aliases=aliases,
        scratch_shapes=[pltpu.VMEM((LANES * (tile + 8), LANES), F32), pltpu.VMEM((2, LANES * 8, LANES), F32)],
        compiler_params=pltpu.CompilerParams(vmem_limit_bytes=60 * MIB),
        cost_estimate=pl.CostEstimate(
            flops=work * sources.shape[0] * 32, bytes_accessed=work * 72, transcendentals=0
        ),
        name="child_translate",
    )(*operands)


def sum_kernel(packed, rows, parents, slot_ref, local_ref, lowered_ref, phase_ref, *rest):
    out_ref, lowered, total, phase = rest[-4:]
    groups, per = 4 // packed, 8 // packed
    tile = 16 * groups
    pitch = tile + 8
    step = pl.program_id(1)

    @pl.when(step == 0)
    def _():
        for row in range(rows):
            lowered[pl.ds(row, LANES, stride=per), :] = lowered_ref[row * LANES : (row + 1) * LANES].T
        for octant in range(8):
            for part in range(2):
                phase[2 * octant + part] = jnp.concatenate([phase_ref[8 * part + octant, :per]] * packed, axis=0)

    @pl.when(step < 2)
    def _():
        half = LANES // 2

        def one_box(i, carry):
            slot = slot_ref[step * half + i]
            octant = slot // parents
            cosine, sine = phase[2 * octant], phase[2 * octant + 1]
            x = lowered[pl.ds(pl.multiple_of(slot % parents * tile, tile), tile), :]
            local = local_ref[0, pl.ds(pl.multiple_of(i * tile, tile), tile), :]
            here = pl.multiple_of((step * half + i) * pitch, 8)
            for g in range(groups):
                at, to = slice(g * 8, g * 8 + 8), slice((groups + g) * 8, (groups + g) * 8 + 8)
                real, imag = x[at], x[to]
                total[pl.ds(here + g * 8, 8), :] = local[at] + (real * cosine + imag * sine)
                total[pl.ds(here + (groups + g) * 8, 8), :] = local[to] + (imag * cosine - real * sine)
            return carry

        lax.fori_loop(0, half, one_box, 0, unroll=4)

    @pl.when(step >= 2)
    def _():
        for i in range(2):
            c = 2 * (step - 2) + i
            plane, sub = (c, 0) if packed == 1 else (c // packed, c % packed * per)
            for part in range(2):
                for row in range(rows):
                    at = pl.ds((part * groups + plane) * 8 + sub + row, LANES, stride=pitch)
                    out_ref[part, i, row * LANES : (row + 1) * LANES] = total[at, :].T


def final_sum(shape, local, lowered, phase, slots, segment, onto):
    first, count, packed, rows = segment
    tile = 64 // packed
    in_specs = [
        pl.BlockSpec(memory_space=pltpu.SMEM),
        pl.BlockSpec((1, LANES // 2 * tile, LANES), lambda i, s: (i, jnp.minimum(s, 1), 0)),
        pl.BlockSpec((8 * LANES, LANES), lambda i, s: (first + i, 0)),
        pl.BlockSpec((16, 8, LANES), lambda i, s: (0, first + i, 0)),
    ]
    operands = [slots, local, lowered, phase]
    aliases = {}
    if onto is not None:
        in_specs.append(pl.BlockSpec(memory_space=pl.ANY))
        operands.append(onto)
        aliases = {4: 0}
    work = count * rows * LANES * LANES
    return pl.pallas_call(
        functools.partial(sum_kernel, packed, rows, LANES // 8),
        grid=(count, 4),
        in_specs=in_specs,
        out_specs=pl.BlockSpec((2, 2, 8 * LANES, LANES), lambda i, s: (0, jnp.maximum(s - 2, 0), first + i, 0)),
        out_shape=jax.ShapeDtypeStruct(shape, F32),
        input_output_aliases=aliases,
        scratch_shapes=[
            pltpu.VMEM((LANES * (8 // packed), LANES), F32),
            pltpu.VMEM((LANES * (tile + 8), LANES), F32),
            pltpu.VMEM((16, 8, LANES), F32),
        ],
        compiler_params=pltpu.CompilerParams(vmem_limit_bytes=60 * MIB),
        cost_estimate=pl.CostEstimate(flops=work * 32, bytes_accessed=work * 72, transcendentals=0),
        name="final_sum",
    )(*operands)


def cos_sin(x):
    turns = jnp.floor(x * (2.0 / math.pi) + 0.5)
    rest = ((x - turns * 1.5703125) - turns * 4.837512969970703e-4) - turns * 7.54978995489188e-8
    square = rest * rest
    sine = rest + rest * square * (
        -1.6666654611e-1 + square * (8.3321608736e-3 + square * -1.9515295891e-4)
    )
    cosine = (1.0 - 0.5 * square) + square * square * (
        4.166664568298827e-2 + square * (-1.388731625493765e-3 + square * 2.443315711809948e-5)
    )
    quarter = turns.astype(jnp.int32)
    odd = (quarter & 1) == 1
    first, second = jnp.where(odd, sine, cosine), jnp.where(odd, cosine, sine)
    first = jnp.where(((quarter + 1) & 2) == 2, -first, first)
    second = jnp.where((quarter & 2) == 2, -second, second)
    return first, second


def tables_kernel(sizes, slot_ref, polar_up_ref, combine_ref, cos_ref, sin_ref, phase_ref, child_ref):
    rows, columns, rows_up, columns_up, parents, n_theta, n_phi = sizes
    polar_index, azimuth_index = lax.axis_index("theta"), lax.axis_index("phi")

    def iota(shape, axis):
        return lax.broadcasted_iota(jnp.int32, shape, axis)

    boxes = slot_ref.shape[1]
    slot = jnp.broadcast_to(slot_ref[...], (parents, boxes))
    same = (slot & (parents - 1)) == iota((parents, boxes), 0)
    octant = slot >> (parents.bit_length() - 1)
    east, north, upper = (2 * ((octant >> n) & 1) - 1 for n in range(3))
    blocks = []
    for z in range(2):
        for kind in range(2):
            for difference in range(2):
                chosen = same & ((east == north) if kind == 0 else (east != north))
                weight = (upper if z else 1) * (east if difference else 1)
                weight = jnp.where(chosen, weight, 0).astype(F32)
                blocks.append(weight)
    combine = jnp.concatenate(blocks, axis=0).astype(BF16)
    combine_ref[...] = jnp.concatenate([combine, combine], axis=1)

    p_pad, t_pad = cos_ref.shape
    q_pad = phase_ref.shape[2]
    polar = (iota((p_pad, LANES), 0) + polar_index * rows_up).astype(F32) + 0.5
    cosine, sine = cos_sin(polar * (math.pi / (rows_up * n_theta)))
    up_cos, up_sin = cos_sin(WAVE * cosine)
    cos_ref[...] = polar_up_ref[...] * up_cos[:, :t_pad]
    sin_ref[...] = polar_up_ref[...] * up_sin[:, :t_pad]
    azimuth = (iota((8, q_pad), 1) + azimuth_index * columns_up).astype(F32)
    east, north = cos_sin(azimuth * (2.0 * math.pi / (columns_up * n_phi)))
    flat = WAVE * sine
    valid = iota((p_pad, LANES), 0) < rows_up
    for lane in range(0, q_pad, LANES):
        lanes = slice(lane, lane + LANES)
        inside = valid & (iota((p_pad, LANES), 1) + lane < columns_up)
        for kind in range(2):
            turned = (east - north if kind else east + north)[:1, lanes]
            found = cos_sin(flat * turned)
            for i in range(2):
                phase_ref[2 * kind + i, :, lanes] = jnp.where(inside, found[i], 0.0)

    count = child_ref.shape[1]
    sample = iota((count, LANES), 0) * LANES + iota((count, LANES), 1)
    row = jnp.floor((sample.astype(F32) + 0.5) * (1.0 / columns))
    polar = row + (polar_index * rows).astype(F32) + 0.5
    azimuth = sample.astype(F32) - row * columns + (azimuth_index * columns).astype(F32)
    up, flat = cos_sin(polar * (math.pi / (rows * n_theta)))
    east, north = cos_sin(azimuth * (2.0 * math.pi / (columns * n_phi)))
    for octant in range(4):
        signs = [2 * ((octant >> n) & 1) - 1 for n in range(3)]
        found = cos_sin(WAVE * (flat * east * signs[0] + flat * north * signs[1] + up * signs[2]))
        child_ref[octant] = found[0]
        child_ref[7 - octant] = found[0]
        child_ref[8 + octant] = found[1]
        child_ref[15 - octant] = -found[1]


def tables(slots, sizes, p_pad, t_pad, q_pad, polar_up):
    rows, columns, rows_up, columns_up, parents, n_theta, n_phi = sizes
    boxes = slots.shape[0]
    assert parents & (parents - 1) == 0
    return pl.pallas_call(
        functools.partial(tables_kernel, sizes),
        out_shape=[
            jax.ShapeDtypeStruct((8 * parents, 2 * boxes), BF16),
            jax.ShapeDtypeStruct((p_pad, t_pad), F32),
            jax.ShapeDtypeStruct((p_pad, t_pad), F32),
            jax.ShapeDtypeStruct((4, p_pad, q_pad), F32),
            jax.ShapeDtypeStruct((16, -(-rows * columns // LANES), LANES), F32),
        ],
        compiler_params=pltpu.CompilerParams(vmem_limit_bytes=60 * MIB),
        name="tables",
    )(slots.reshape(1, boxes), polar_up)


def parent_kernel(
    sizes,
    source_ref,
    kind_ref,
    child_ref,
    next_ref,
    previous_ref,
    side_ref,
    table_ref,
    combine_ref,
    polar_cos_ref,
    polar_sin_ref,
    azimuth_up_ref,
    polar_down_ref,
    azimuth_down_ref,
    phase_ref,
    out_ref,
    wide_even,
    wide_odd,
    rows_done,
    table_by_kind,
    parent_out,
    in_high,
    in_low,
    lowered,
):
    (rows, columns, rows_up, columns_up, parents, entries, table_steps, table_rows) = sizes
    pitch, f_pad = wide_even.shape[1] // 128, wide_even.shape[2]
    t_pad = pitch - 8
    p_pad, q_pad = phase_ref.shape[1], phase_ref.shape[2]
    row_tiles, lane_tiles = p_pad // 8, q_pad // LANES
    step = pl.program_id(0)
    half = 4 * parents
    table_first = jnp.minimum(step, table_steps - 1) * table_rows

    @pl.when(step == 0)
    def _():
        for part in range(2):
            for t in range(rows + 6, t_pad):
                for wide in (wide_even, wide_odd):
                    wide[part, pl.ds(t, 128, stride=pitch), :] = jnp.zeros((128, f_pad), F32)
        for part in range(2):
            for p in range(rows_up, p_pad):
                for lane_tile in range(lane_tiles):
                    at = pl.ds(p % 8, 128, stride=8)
                    table_by_kind[lane_tile * row_tiles + p // 8, part, at, :] = jnp.zeros((128, LANES), F32)

    combine = combine_ref[...]

    def samples(part, main_ref, r, t):
        x = jnp.concatenate(
            [main_ref[part, 0, r], side_ref[part, 0, t], jnp.zeros((f_pad - columns - 8, LANES), F32)], axis=0
        )
        high, low = split(x)
        return jnp.concatenate([high, low], axis=1)

    def turn(rows_here, wide):
        pieces = [(part,) + row for row in rows_here for part in range(2)]
        for i in range(0, len(pieces), 2):
            both = jnp.concatenate([samples(*piece) for piece in pieces[i : i + 2]], axis=0)
            turned = dot_transposed(combine, both)
            for j, piece in enumerate(pieces[i : i + 2]):
                at = pl.ds(piece[3], 128, stride=pitch)
                wide[piece[0], at, :] = turned[:, j * f_pad : (j + 1) * f_pad]

    def turn_table(r):
        p = table_first + r
        at = pl.ds(p % 8, 128, stride=8)
        for part in range(2):
            x = table_ref[part, r]
            if q_pad > columns_up:
                x = jnp.concatenate([x, jnp.zeros((q_pad - columns_up, LANES), F32)], axis=0)
            for lane_tile in range(lane_tiles):
                turned = x[lane_tile * LANES : (lane_tile + 1) * LANES].T
                table_by_kind[lane_tile * row_tiles + p // 8, part, at, :] = turned

    def shares(count):
        pairs = -(-count // 2)
        sizes_here = [(pairs + 3 - i) // 4 for i in range(4)]
        return [(2 * sum(sizes_here[:i]), sizes_here[i]) for i in range(4)]

    per = 4

    def channel(read, write):
        if write is not None:
            turn(
                [(next_ref, r, rows + r) for r in range(3)] + [(previous_ref, r, rows + 3 + r) for r in range(3)],
                write,
            )
        if read is not None:
            polar = []
            for sign in (-1.0, 1.0):
                high, low = split(jnp.concatenate([polar_cos_ref[...], sign * polar_sin_ref[...]], axis=1))
                polar.append(jnp.concatenate([high, high, low], axis=1))
        for target in range(2):
            for difference in range(2):
                part = target if difference == 0 else 1 - target
                loop = 2 * target + difference

                def one_kind(kind, carry, part=part, difference=difference, loop=loop):
                    if write is not None:
                        first, count = shares(rows)[loop]
                        here = [jnp.minimum(first + kind * count + j, rows - 1) for j in range(count)]
                        turn([(child_ref, r, r) for r in here], write)
                        first, count = shares(table_rows)[loop]
                        for j in range(count):
                            turn_table(jnp.minimum(first + kind * count + j, table_rows - 1))
                    if read is not None:
                        first = (kind * 2 + difference) * parents
                        for pair in range(parents // 2):
                            stacked = []
                            for source, offset in ((part, 0), (1 - part, half)):
                                at = (offset + first + 2 * pair) * pitch
                                both = [
                                    read[source, pl.ds(pl.multiple_of(at + i * pitch, 8), t_pad), :] for i in range(2)
                                ]
                                stacked.append(jnp.concatenate(both, axis=1))
                            high, low = split(jnp.concatenate(stacked, axis=0))
                            result = dot(polar[part], jnp.concatenate([high, low, high], axis=0))
                            high, low = split(result)
                            for i in range(2):
                                lanes = slice(i * f_pad, (i + 1) * f_pad)
                                rows_done[kind * 2 + difference, pl.ds((2 * pair + i) * p_pad, p_pad), :] = (
                                    jnp.concatenate([high[:, lanes], low[:, lanes], high[:, lanes]], axis=1)
                                )
                    return carry

                lax.fori_loop(0, 2, one_kind, 0)

            if read is None:
                continue

            def one_group(group, carry, target=target):
                at = pl.ds(pl.multiple_of(group * per * p_pad, 16), per * p_pad)
                y = dot(jnp.concatenate([rows_done[k, at, :] for k in range(4)], axis=0), azimuth_up_ref[...])
                for i in range(per):
                    terms = [y[(k * per + i) * p_pad : (k * per + i + 1) * p_pad] * phase_ref[k] for k in range(4)]
                    if target == 0:
                        value = (terms[0] - terms[1]) + (terms[2] - terms[3])
                    else:
                        value = (terms[0] + terms[1]) + (terms[2] + terms[3])
                    at = pl.ds(pl.multiple_of((group * per + i) * 64 + target * 32 + (step - 1) * 8, 8), 8)
                    for lane_tile in range(lane_tiles):
                        lanes = slice(lane_tile * LANES, (lane_tile + 1) * LANES)
                        for row_tile in range(row_tiles):
                            tile = value[row_tile * 8 : row_tile * 8 + 8, lanes]
                            parent_out[lane_tile * row_tiles + row_tile, at, :] = tile
                return carry

            lax.fori_loop(0, parents // per, one_group, 0)

    pl.when(step == 0)(lambda: channel(None, wide_even))
    pl.when((step == 1) | (step == 3))(lambda: channel(wide_even, wide_odd))
    pl.when(step == 2)(lambda: channel(wide_odd, wide_even))
    pl.when(step == 4)(lambda: channel(wide_odd, None))

    @pl.when(step == 4)
    def _():
        def one_tile(tile, carry):
            box = tile // (p_pad // 16)
            row_pair = tile % (p_pad // 16)
            sources = [pl.ds(pl.multiple_of(source_ref[box, e] * 64, 64), 64) for e in range(entries)]
            kinds = [pl.ds(pl.multiple_of(kind_ref[box, e] * 8, 8), 8) for e in range(entries)]
            for lane_tile in range(lane_tiles):
                halves = []
                for i in range(2):
                    where = lane_tile * row_tiles + 2 * row_pair + i
                    total = [None] * 8
                    for e in range(entries):
                        x = parent_out[where, sources[e], :]
                        real, imag = (table_by_kind[where, part, kinds[e], :] for part in range(2))
                        for c in range(4):
                            xr, xi = x[c * 8 : c * 8 + 8], x[(4 + c) * 8 : (4 + c) * 8 + 8]
                            re = xr * real - xi * imag
                            im = xr * imag + xi * real
                            total[c] = re if e == 0 else total[c] + re
                            total[4 + c] = im if e == 0 else total[4 + c] + im
                    halves.append(total)
                for c in range(8):
                    high, low = split(jnp.concatenate([halves[0][c], halves[1][c]], axis=0))
                    at = pl.ds(pl.multiple_of((c * parents + box) * p_pad + row_pair * 16, 16), 16)
                    lanes = slice(lane_tile * LANES, (lane_tile + 1) * LANES)
                    in_high[at, lanes] = high
                    in_low[at, lanes] = low
            return carry

        lax.fori_loop(0, parents * (p_pad // 16), one_tile, 0)

        down = azimuth_down_ref[...]
        down_high = down[:, :f_pad]
        high, low = split(polar_down_ref[...])
        polar_back = jnp.concatenate([high, high, low], axis=1)
        per = parents

        def one_group(group, carry):
            at = pl.ds(pl.multiple_of(group * per * p_pad, 16), per * p_pad)
            high = in_high[at, :]
            low = in_low[at, :]
            both = dot(high, down)
            y = both[:, :f_pad] + both[:, f_pad:] + dot(low, down_high)
            for i in range(0, per, 2):
                x = jnp.concatenate([y[i * p_pad : (i + 1) * p_pad], y[(i + 1) * p_pad : (i + 2) * p_pad]], axis=1)
                high, low = split(x)
                z = dot(polar_back, jnp.concatenate([high, low, high], axis=0))
                for j in range(2):
                    lowered[pl.ds(pl.multiple_of(((i + j) * 8 + group) * pitch, 8), t_pad), :] = z[
                        :, j * f_pad : (j + 1) * f_pad
                    ]
            return carry

        lax.fori_loop(0, 8 * parents // per, one_group, 0)

        per_turn = next(n for n in (6, 5, 3, 2, 1) if (rows + 6) % n == 0)

        def some_rows(i, carry):
            for r in range(per_turn):
                turned = lowered[pl.ds(i * per_turn + r, 8 * parents, stride=pitch), :].T
                out_ref[i * per_turn + r] = turned[: columns + 8]
            return carry

        lax.fori_loop(0, (rows + 6) // per_turn, some_rows, 0)


def parent_level(child_out, after, before, side, table, sources, kinds, combine, polar_cos, polar_sin, phase):
    _, rows, columns, boxes = child_out.shape
    _, rows_up, columns_up, translators = table.shape
    assert boxes == LANES and translators == LANES
    parents, entries = sources.shape
    t_pad, p_pad = polar_cos.shape[1], polar_cos.shape[0]
    f_pad, q_pad = round_up(columns + 8, LANES), round_up(columns_up, LANES)
    assert f_pad == LANES
    table_steps = next(s for s in (4, 2, 1) if rows_up % s == 0)
    table_rows = rows_up // table_steps
    n_theta, n_phi = lax.axis_size("theta"), lax.axis_size("phi")
    polar_up = local_up(rows_up * n_theta, rows * n_theta, True, rows_up, rows, 3, (p_pad, t_pad))
    azimuth_up = local_up(columns_up * n_phi, columns * n_phi, False, columns_up, columns, 2, (q_pad, f_pad))
    high, low = split_constant(np.ascontiguousarray(azimuth_up.T))
    azimuth_three = jnp.asarray(np.concatenate([high, high, low], axis=0))
    high, low = split_constant(azimuth_up)
    azimuth_down = jnp.asarray(np.concatenate([high, low], axis=1))
    polar_down = jnp.asarray(np.ascontiguousarray(polar_up.T))

    def whole(array):
        return pl.BlockSpec(array.shape, lambda g: (0,) * array.ndim)

    def channel(shape):
        return pl.BlockSpec((2, 1) + shape, lambda g: (0, jnp.minimum(g, 3), 0, 0, 0))

    smem = pl.BlockSpec(memory_space=pltpu.SMEM)
    constants = [combine, polar_cos, polar_sin, azimuth_three, polar_down, azimuth_down, phase]
    return pl.pallas_call(
        functools.partial(
            parent_kernel, (rows, columns, rows_up, columns_up, parents, entries, table_steps, table_rows)
        ),
        grid=(5,),
        in_specs=[
            smem,
            smem,
            channel((rows, columns, boxes)),
            channel((3, columns, boxes)),
            channel((3, columns, boxes)),
            channel((rows + 6, 8, boxes)),
            pl.BlockSpec(
                (2, table_rows, columns_up, translators), lambda g: (0, jnp.minimum(g, table_steps - 1), 0, 0)
            ),
        ]
        + [whole(c) for c in constants],
        out_specs=pl.BlockSpec((rows + 6, columns + 8, 8 * parents), lambda g: (0, 0, 0)),
        out_shape=jax.ShapeDtypeStruct((rows + 6, columns + 8, 8 * parents), F32),
        scratch_shapes=[
            pltpu.VMEM((2, 128 * (t_pad + 8), f_pad), F32),
            pltpu.VMEM((2, 128 * (t_pad + 8), f_pad), F32),
            pltpu.VMEM((4, parents * p_pad, 3 * f_pad), BF16),
            pltpu.VMEM((q_pad // LANES * (p_pad // 8), 2, translators * 8, LANES), F32),
            pltpu.VMEM((q_pad // LANES * (p_pad // 8), parents * 64, LANES), F32),
            pltpu.VMEM((8 * parents * p_pad, q_pad), BF16),
            pltpu.VMEM((8 * parents * p_pad, q_pad), BF16),
            pltpu.VMEM((8 * parents * (t_pad + 8), f_pad), F32),
        ],
        compiler_params=pltpu.CompilerParams(vmem_limit_bytes=60 * MIB),
        cost_estimate=pl.CostEstimate(
            flops=20_000_000_000, bytes_accessed=child_out.size * 8, transcendentals=0
        ),
        name="parent_level",
    )(
        sources,
        kinds,
        child_out.reshape((2, 4) + child_out.shape[1:]),
        after.reshape((2, 4) + after.shape[1:]),
        before.reshape((2, 4) + before.shape[1:]),
        side.reshape((2, 4) + side.shape[1:]),
        table,
        *constants,
    )


def chain(count, periodic):
    pairs = [(i, i + 1) for i in range(count - 1)]
    return pairs + [(count - 1, 0)] if periodic else pairs


def send(block, axis, up):
    pairs = chain(lax.axis_size(axis), axis == "phi")
    return lax.ppermute(block, axis, pairs if up else [(b, a) for a, b in pairs])


def plain(array):
    return with_layout_constraint(array, Layout(major_to_minor=tuple(range(array.ndim))))


def per_device(
    child_out,
    child_slot,
    sources_child,
    kinds_child,
    table_child,
    sources_parent,
    kinds_parent,
    table_parent,
):
    _, rows, columns, boxes = child_out.shape
    _, rows_up, columns_up, _ = table_parent.shape
    parents = boxes // 8
    n_theta, n_phi = lax.axis_size("theta"), lax.axis_size("phi")
    t_pad, p_pad = round_up(rows + 6, 16), round_up(rows_up, 16)
    q_pad = round_up(columns_up, LANES)
    barrier = lax.optimization_barrier

    polar_up = local_up(rows_up * n_theta, rows * n_theta, True, rows_up, rows, 3, (p_pad, t_pad))
    sizes = (rows, columns, rows_up, columns_up, parents, n_theta, n_phi)
    combine, polar_cos, polar_sin, phase, phase_child = tables(
        child_slot, sizes, p_pad, t_pad, q_pad, jnp.asarray(polar_up)
    )

    samples = rows * columns
    flat_child = child_out.reshape(2, 4, samples, boxes)
    flat_table = table_child.reshape(2, samples, table_child.shape[3])
    pieces = segments(samples)
    local = [None] * len(pieces)
    chunks = [(n, i) for n, piece in enumerate(pieces) for i in range(piece[1])]

    def translate_next(child):
        if chunks:
            n, i = chunks.pop(0)
            local[n] = child_translate(
                child, flat_table, sources_child.T, kinds_child.T, pieces[n], i, local[n]
            )

    after = plain(send(plain(child_out[:, :3]), "theta", False))
    before = plain(send(plain(child_out[:, rows - 3 :]), "theta", True))
    first_child, made = barrier((flat_child, (combine, polar_cos, polar_sin, phase, phase_child)))
    combine, polar_cos, polar_sin, phase, phase_child = made
    translate_next(first_child)
    after, before, local = barrier((after, before, local))

    low, high = (
        jnp.concatenate([edge[:, :, at] for edge in (child_out, after, before)], axis=1)
        for at in (slice(0, 3), slice(columns - 2, columns))
    )
    low, high, later_child = barrier((low, high, flat_child))
    right = send(low, "phi", False)
    left = send(high, "phi", True)
    if len(chunks) > 1:
        translate_next(later_child)
    right, left, local = barrier((right, left, local))
    side = jnp.concatenate([right, left, jnp.zeros((8, rows + 6, 3, boxes), F32)], axis=2)

    lowered = parent_level(
        child_out,
        after,
        before,
        side,
        table_parent,
        sources_parent,
        kinds_parent,
        combine,
        polar_cos,
        polar_sin,
        phase,
    )
    lowered, later_child = barrier((lowered, flat_child))

    low = send(lowered[rows : rows + 3], "theta", True)
    high = send(lowered[rows + 3 : rows + 6], "theta", False)
    while chunks:
        translate_next(later_child)
    local, lowered = barrier((local, lowered))
    here = lowered[:rows]
    here = here + jnp.pad(low, ((0, rows - 3), (0, 0), (0, 0))) + jnp.pad(high, ((rows - 3, 0), (0, 0), (0, 0)))
    low = send(here[:, columns : columns + 3], "phi", True)
    high = send(here[:, columns + 3 : columns + 5], "phi", False)
    here = here[:, :columns]
    here = here + jnp.pad(low, ((0, 0), (0, columns - 3), (0, 0))) + jnp.pad(high, ((0, 0), (columns - 2, 0), (0, 0)))
    here = here.reshape(samples, boxes)

    result = None
    for piece, part in zip(pieces, local):
        result = final_sum(flat_child.shape, part, here, phase_child, child_slot, piece, result)
    return result.reshape(child_out.shape)


def solution(mesh):
    placed = (
        P(None, "theta", "phi", None),
        P(),
        P(),
        P(),
        P(None, "theta", "phi", None),
        P(),
        P(),
        P(None, "theta", "phi", None),
    )
    return jax.shard_map(
        per_device,
        mesh=mesh,
        in_specs=placed,
        out_specs=P(None, "theta", "phi", None),
        check_vma=False,
    )
```

```python
import functools
import math

import jax
import jax.numpy as jnp
import numpy as np
from jax import lax
from jax.experimental import pallas as pl
from jax.experimental.layout import Layout, with_layout_constraint
from jax.experimental.pallas import tpu as pltpu
from jax.sharding import PartitionSpec as P

BAND1 = 180
WAVE = BAND1 / (2.0 * math.sqrt(3.0))
LANES = 128
MIB = 1 << 20
F32 = jnp.float32
BF16 = jnp.bfloat16


def round_up(count, step):
    return -(-count // step) * step


def stencil_entries(count_out, count_in, centered, out_rows):
    entries = []
    for row_out in out_rows:
        if centered:
            numerator = (2 * row_out + 1) * count_in - count_out
        else:
            numerator = 2 * row_out * count_in
        denominator = 2 * count_out
        base_index = numerator // denominator
        fraction = (numerator - base_index * denominator) / denominator
        for offset_a in range(-2, 4):
            weight = 1.0
            for offset_b in range(-2, 4):
                if offset_b != offset_a:
                    weight = weight * (fraction - offset_b) / (offset_a - offset_b)
            entries.append((row_out, base_index + offset_a, weight))
    return entries


def local_up(count_out, count_in, centered, rows_out, rows_in, below, shape):
    matrix = np.zeros(shape)
    for row_out, column, weight in stencil_entries(count_out, count_in, centered, range(rows_out)):
        assert -below <= column < rows_in + 3 or abs(weight) < 1e-12
        if column >= 0:
            matrix[row_out, column] += weight
        elif column >= -below:
            matrix[row_out, rows_in + 3 + below + column] += weight
    return matrix.astype(np.float32)


def split(x):
    high = x.astype(BF16)
    return high, (x - high.astype(F32)).astype(BF16)


def split_constant(matrix):
    high = matrix.astype(jnp.bfloat16)
    return high, (matrix - high.astype(np.float32)).astype(jnp.bfloat16)


def dot(a, b):
    return jnp.dot(a, b, preferred_element_type=F32)


def dot_transposed(a, b):
    return lax.dot_general(a, b, (((1,), (1,)), ((), ())), preferred_element_type=F32)


def segments(samples):
    full, rest = divmod(samples, 8 * LANES)
    found = [(0, full, 1, 8)] if full else []
    if rest:
        rows = -(-rest // LANES)
        packed = 4 if rows <= 2 else 2 if rows <= 4 else 1
        found.append((full, 1, packed, rows))
    return found


def translate_kernel(packed, rows, source_ref, kind_ref, child_ref, table_ref, *rest):
    out_ref, pattern, table = rest[-3:]
    groups, per = 4 // packed, 8 // packed
    tile = 16 * groups
    pitch = tile + 8
    entries = source_ref.shape[0]
    step = pl.program_id(0)

    @pl.when(step == 0)
    def _():
        for row in range(rows):
            real, imag = (table_ref[part, row * LANES : (row + 1) * LANES].T for part in range(2))
            for part, turned in enumerate((real, imag - real, real + imag)):
                for c in range(packed):
                    table[part, pl.ds(c * per + row, LANES, stride=8), :] = turned

    @pl.when(step < 2)
    def _():
        for i in range(2):
            c = 2 * step + i
            plane, sub = (c, 0) if packed == 1 else (c // packed, c % packed * per)
            for part in range(2):
                for row in range(rows):
                    at = pl.ds((part * groups + plane) * 8 + sub + row, LANES, stride=pitch)
                    pattern[at, :] = child_ref[part, i, row * LANES : (row + 1) * LANES].T

    @pl.when(step >= 2)
    def _():
        half = LANES // 2

        def one_box(i, carry):
            box = (step - 2) * half + i
            sums = [[None] * groups for _ in range(3)]
            for entry in range(entries):
                x = pattern[pl.ds(pl.multiple_of(source_ref[entry, box] * pitch, 8), tile), :]
                kind = pl.ds(pl.multiple_of(kind_ref[entry, box] * 8, 8), 8)
                factors = [table[part, kind, :] for part in range(3)]
                for g in range(groups):
                    xr, xi = x[g * 8 : g * 8 + 8], x[(groups + g) * 8 : (groups + g) * 8 + 8]
                    for part, term in enumerate((xr + xi, xr, xi)):
                        product = term * factors[part]
                        sums[part][g] = product if entry == 0 else sums[part][g] + product
            total = [sums[0][g] - sums[2][g] for g in range(groups)]
            total += [sums[0][g] + sums[1][g] for g in range(groups)]
            for g in range(2 * groups):
                out_ref[0, pl.ds(pl.multiple_of(i * tile, tile) + g * 8, 8), :] = total[g]
            return carry

        lax.fori_loop(0, half, one_box, 0, unroll=2)


def child_translate(child, table, sources, kinds, segment, chunk, onto):
    first, count, packed, rows = segment
    tile = 64 // packed
    smem = pl.BlockSpec(memory_space=pltpu.SMEM)
    in_specs = [
        smem,
        smem,
        pl.BlockSpec((2, 2, 8 * LANES, LANES), lambda s: (0, jnp.minimum(s, 1), first + chunk, 0)),
        pl.BlockSpec((2, 8 * LANES, LANES), lambda s: (0, first + chunk, 0)),
    ]
    operands = [sources, kinds, child, table]
    aliases = {}
    if onto is not None:
        in_specs.append(pl.BlockSpec(memory_space=pl.ANY))
        operands.append(onto)
        aliases = {4: 0}
    work = rows * LANES * LANES
    return pl.pallas_call(
        functools.partial(translate_kernel, packed, rows),
        grid=(4,),
        in_specs=in_specs,
        out_specs=pl.BlockSpec((1, LANES // 2 * tile, LANES), lambda s: (chunk, jnp.maximum(s - 2, 0), 0)),
        out_shape=jax.ShapeDtypeStruct((count, LANES * tile, LANES), F32),
        input_output_aliases=aliases,
        scratch_shapes=[pltpu.VMEM((LANES * (tile + 8), LANES), F32), pltpu.VMEM((3, LANES * 8, LANES), F32)],
        compiler_params=pltpu.CompilerParams(vmem_limit_bytes=60 * MIB),
        cost_estimate=pl.CostEstimate(
            flops=work * sources.shape[0] * 32, bytes_accessed=work * 72, transcendentals=0
        ),
        name="child_translate",
    )(*operands)


def sum_kernel(packed, rows, parents, slot_ref, local_ref, lowered_ref, phase_ref, *rest):
    out_ref, lowered, total, phase = rest[-4:]
    groups, per = 4 // packed, 8 // packed
    tile = 16 * groups
    pitch = tile + 8
    step = pl.program_id(1)

    @pl.when(step == 0)
    def _():
        for row in range(rows):
            lowered[pl.ds(row, LANES, stride=per), :] = lowered_ref[row * LANES : (row + 1) * LANES].T
        for octant in range(8):
            for part in range(2):
                phase[2 * octant + part] = jnp.concatenate([phase_ref[8 * part + octant, :per]] * packed, axis=0)

    @pl.when(step < 2)
    def _():
        half = LANES // 2

        def one_box(i, carry):
            slot = slot_ref[step * half + i]
            octant = slot >> (parents.bit_length() - 1)
            cosine, sine = phase[2 * octant], phase[2 * octant + 1]
            x = lowered[pl.ds(pl.multiple_of((slot & (parents - 1)) * tile, tile), tile), :]
            local = local_ref[0, pl.ds(pl.multiple_of(i * tile, tile), tile), :]
            here = pl.multiple_of((step * half + i) * pitch, 8)
            for g in range(groups):
                at, to = slice(g * 8, g * 8 + 8), slice((groups + g) * 8, (groups + g) * 8 + 8)
                real, imag = x[at], x[to]
                total[pl.ds(here + g * 8, 8), :] = local[at] + (real * cosine + imag * sine)
                total[pl.ds(here + (groups + g) * 8, 8), :] = local[to] + (imag * cosine - real * sine)
            return carry

        lax.fori_loop(0, half, one_box, 0, unroll=4)

    @pl.when(step >= 2)
    def _():
        for i in range(2):
            c = 2 * (step - 2) + i
            plane, sub = (c, 0) if packed == 1 else (c // packed, c % packed * per)
            for part in range(2):
                for row in range(rows):
                    at = pl.ds((part * groups + plane) * 8 + sub + row, LANES, stride=pitch)
                    out_ref[part, i, row * LANES : (row + 1) * LANES] = total[at, :].T


def final_sum(shape, local, lowered, phase, slots, segment, onto):
    first, count, packed, rows = segment
    tile = 64 // packed
    in_specs = [
        pl.BlockSpec(memory_space=pltpu.SMEM),
        pl.BlockSpec((1, LANES // 2 * tile, LANES), lambda i, s: (i, jnp.minimum(s, 1), 0)),
        pl.BlockSpec((8 * LANES, LANES), lambda i, s: (first + i, 0)),
        pl.BlockSpec((16, 8, LANES), lambda i, s: (0, first + i, 0)),
    ]
    operands = [slots, local, lowered, phase]
    aliases = {}
    if onto is not None:
        in_specs.append(pl.BlockSpec(memory_space=pl.ANY))
        operands.append(onto)
        aliases = {4: 0}
    work = count * rows * LANES * LANES
    return pl.pallas_call(
        functools.partial(sum_kernel, packed, rows, LANES // 8),
        grid=(count, 4),
        in_specs=in_specs,
        out_specs=pl.BlockSpec((2, 2, 8 * LANES, LANES), lambda i, s: (0, jnp.maximum(s - 2, 0), first + i, 0)),
        out_shape=jax.ShapeDtypeStruct(shape, F32),
        input_output_aliases=aliases,
        scratch_shapes=[
            pltpu.VMEM((LANES * (8 // packed), LANES), F32),
            pltpu.VMEM((LANES * (tile + 8), LANES), F32),
            pltpu.VMEM((16, 8, LANES), F32),
        ],
        compiler_params=pltpu.CompilerParams(vmem_limit_bytes=60 * MIB),
        cost_estimate=pl.CostEstimate(flops=work * 32, bytes_accessed=work * 72, transcendentals=0),
        name="final_sum",
    )(*operands)


def cos_sin(x):
    turns = jnp.floor(x * (2.0 / math.pi) + 0.5)
    rest = ((x - turns * 1.5703125) - turns * 4.837512969970703e-4) - turns * 7.54978995489188e-8
    square = rest * rest
    sine = rest + rest * square * (
        -1.6666654611e-1 + square * (8.3321608736e-3 + square * -1.9515295891e-4)
    )
    cosine = (1.0 - 0.5 * square) + square * square * (
        4.166664568298827e-2 + square * (-1.388731625493765e-3 + square * 2.443315711809948e-5)
    )
    quarter = turns.astype(jnp.int32)
    odd = (quarter & 1) == 1
    first, second = jnp.where(odd, sine, cosine), jnp.where(odd, cosine, sine)
    first = jnp.where(((quarter + 1) & 2) == 2, -first, first)
    second = jnp.where((quarter & 2) == 2, -second, second)
    return first, second


def tables_kernel(sizes, slot_ref, polar_up_ref, combine_ref, cos_ref, sin_ref, phase_ref, child_ref):
    rows, columns, rows_up, columns_up, parents, n_theta, n_phi = sizes
    polar_index, azimuth_index = lax.axis_index("theta"), lax.axis_index("phi")

    def iota(shape, axis):
        return lax.broadcasted_iota(jnp.int32, shape, axis)

    boxes = slot_ref.shape[1]
    slot = jnp.broadcast_to(slot_ref[...], (parents, boxes))
    same = (slot & (parents - 1)) == iota((parents, boxes), 0)
    octant = slot >> (parents.bit_length() - 1)
    east, north, upper = (2 * ((octant >> n) & 1) - 1 for n in range(3))
    blocks = []
    for z in range(2):
        for kind in range(2):
            for difference in range(2):
                chosen = same & ((east == north) if kind == 0 else (east != north))
                weight = (upper if z else 1) * (east if difference else 1)
                weight = jnp.where(chosen, weight, 0).astype(F32)
                blocks.append(weight)
    combine = jnp.concatenate(blocks, axis=0).astype(BF16)
    combine_ref[...] = jnp.concatenate([combine, combine], axis=1)

    p_pad, t_pad = cos_ref.shape
    q_pad = phase_ref.shape[2]
    polar = (iota((p_pad, LANES), 0) + polar_index * rows_up).astype(F32) + 0.5
    cosine, sine = cos_sin(polar * (math.pi / (rows_up * n_theta)))
    up_cos, up_sin = cos_sin(WAVE * cosine)
    cos_ref[...] = polar_up_ref[...] * up_cos[:, :t_pad]
    sin_ref[...] = polar_up_ref[...] * up_sin[:, :t_pad]
    azimuth = (iota((8, q_pad), 1) + azimuth_index * columns_up).astype(F32)
    east, north = cos_sin(azimuth * (2.0 * math.pi / (columns_up * n_phi)))
    flat = WAVE * sine
    valid = iota((p_pad, LANES), 0) < rows_up
    for lane in range(0, q_pad, LANES):
        lanes = slice(lane, lane + LANES)
        inside = valid & (iota((p_pad, LANES), 1) + lane < columns_up)
        for kind in range(2):
            turned = (east - north if kind else east + north)[:1, lanes]
            found = cos_sin(flat * turned)
            for i in range(2):
                phase_ref[2 * kind + i, :, lanes] = jnp.where(inside, found[i], 0.0)

    count = child_ref.shape[1]
    sample = iota((count, LANES), 0) * LANES + iota((count, LANES), 1)
    row = jnp.floor((sample.astype(F32) + 0.5) * (1.0 / columns))
    polar = row + (polar_index * rows).astype(F32) + 0.5
    azimuth = sample.astype(F32) - row * columns + (azimuth_index * columns).astype(F32)
    up, flat = cos_sin(polar * (math.pi / (rows * n_theta)))
    east, north = cos_sin(azimuth * (2.0 * math.pi / (columns * n_phi)))
    for octant in range(4):
        signs = [2 * ((octant >> n) & 1) - 1 for n in range(3)]
        found = cos_sin(WAVE * (flat * east * signs[0] + flat * north * signs[1] + up * signs[2]))
        child_ref[octant] = found[0]
        child_ref[7 - octant] = found[0]
        child_ref[8 + octant] = found[1]
        child_ref[15 - octant] = -found[1]


def tables(slots, sizes, p_pad, t_pad, q_pad, polar_up):
    rows, columns, rows_up, columns_up, parents, n_theta, n_phi = sizes
    boxes = slots.shape[0]
    assert parents & (parents - 1) == 0
    return pl.pallas_call(
        functools.partial(tables_kernel, sizes),
        out_shape=[
            jax.ShapeDtypeStruct((8 * parents, 2 * boxes), BF16),
            jax.ShapeDtypeStruct((p_pad, t_pad), F32),
            jax.ShapeDtypeStruct((p_pad, t_pad), F32),
            jax.ShapeDtypeStruct((4, p_pad, q_pad), F32),
            jax.ShapeDtypeStruct((16, -(-rows * columns // LANES), LANES), F32),
        ],
        compiler_params=pltpu.CompilerParams(vmem_limit_bytes=60 * MIB),
        name="tables",
    )(slots.reshape(1, boxes), polar_up)


def parent_kernel(
    sizes,
    source_ref,
    kind_ref,
    child_ref,
    next_ref,
    previous_ref,
    side_ref,
    table_ref,
    combine_ref,
    polar_cos_ref,
    polar_sin_ref,
    azimuth_up_ref,
    polar_down_ref,
    azimuth_down_ref,
    phase_ref,
    out_ref,
    wide_even,
    wide_odd,
    rows_done,
    table_by_kind,
    parent_out,
    in_high,
    in_low,
    lowered,
):
    (rows, columns, rows_up, columns_up, parents, entries, table_steps, table_rows) = sizes
    pitch, f_pad = wide_even.shape[1] // 128, wide_even.shape[2]
    t_pad = pitch - 8
    p_pad, q_pad = phase_ref.shape[1], phase_ref.shape[2]
    row_tiles, lane_tiles = p_pad // 8, q_pad // LANES
    step = pl.program_id(0)
    half = 4 * parents
    table_first = jnp.minimum(step, table_steps - 1) * table_rows

    @pl.when(step == 0)
    def _():
        for part in range(2):
            for t in range(rows + 6, t_pad):
                for wide in (wide_even, wide_odd):
                    wide[part, pl.ds(t, 128, stride=pitch), :] = jnp.zeros((128, f_pad), F32)
        for part in range(2):
            for p in range(rows_up, p_pad):
                for lane_tile in range(lane_tiles):
                    at = pl.ds(p % 8, 128, stride=8)
                    table_by_kind[lane_tile * row_tiles + p // 8, part, at, :] = jnp.zeros((128, LANES), F32)

    combine = combine_ref[...]

    def samples(part, main_ref, r, t):
        x = jnp.concatenate(
            [main_ref[part, 0, r], side_ref[part, 0, t], jnp.zeros((f_pad - columns - 8, LANES), F32)], axis=0
        )
        high, low = split(x)
        return jnp.concatenate([high, low], axis=1)

    def turn(rows_here, wide):
        pieces = [(part,) + row for row in rows_here for part in range(2)]
        for i in range(0, len(pieces), 2):
            both = jnp.concatenate([samples(*piece) for piece in pieces[i : i + 2]], axis=0)
            turned = dot_transposed(combine, both)
            for j, piece in enumerate(pieces[i : i + 2]):
                at = pl.ds(piece[3], 128, stride=pitch)
                wide[piece[0], at, :] = turned[:, j * f_pad : (j + 1) * f_pad]

    def turn_table(r):
        p = table_first + r
        at = pl.ds(p & 7, 128, stride=8)
        for part in range(2):
            x = table_ref[part, r]
            if q_pad > columns_up:
                x = jnp.concatenate([x, jnp.zeros((q_pad - columns_up, LANES), F32)], axis=0)
            for lane_tile in range(lane_tiles):
                turned = x[lane_tile * LANES : (lane_tile + 1) * LANES].T
                table_by_kind[lane_tile * row_tiles + (p >> 3), part, at, :] = turned

    def shares(count):
        pairs = -(-count // 2)
        sizes_here = [(pairs + 3 - i) // 4 for i in range(4)]
        return [(2 * sum(sizes_here[:i]), sizes_here[i]) for i in range(4)]

    per = 4

    def channel(read, write):
        if write is not None:
            turn(
                [(next_ref, r, rows + r) for r in range(3)] + [(previous_ref, r, rows + 3 + r) for r in range(3)],
                write,
            )
        if read is not None:
            polar = []
            for sign in (-1.0, 1.0):
                high, low = split(jnp.concatenate([polar_cos_ref[...], sign * polar_sin_ref[...]], axis=1))
                polar.append(jnp.concatenate([high, high, low], axis=1))
        for target in range(2):
            for difference in range(2):
                part = target if difference == 0 else 1 - target
                loop = 2 * target + difference

                def one_kind(kind, carry, part=part, difference=difference, loop=loop):
                    if write is not None:
                        first, count = shares(rows)[loop]
                        here = [jnp.minimum(first + kind * count + j, rows - 1) for j in range(count)]
                        turn([(child_ref, r, r) for r in here], write)
                        first, count = shares(table_rows)[loop]
                        for j in range(count):
                            turn_table(jnp.minimum(first + kind * count + j, table_rows - 1))
                    if read is not None:
                        first = (kind * 2 + difference) * parents
                        for pair in range(parents // 2):
                            stacked = []
                            for source, offset in ((part, 0), (1 - part, half)):
                                at = (offset + first + 2 * pair) * pitch
                                both = [
                                    read[source, pl.ds(pl.multiple_of(at + i * pitch, 8), t_pad), :] for i in range(2)
                                ]
                                stacked.append(jnp.concatenate(both, axis=1))
                            high, low = split(jnp.concatenate(stacked, axis=0))
                            result = dot(polar[part], jnp.concatenate([high, low, high], axis=0))
                            high, low = split(result)
                            for i in range(2):
                                lanes = slice(i * f_pad, (i + 1) * f_pad)
                                rows_done[kind * 2 + difference, pl.ds((2 * pair + i) * p_pad, p_pad), :] = (
                                    jnp.concatenate([high[:, lanes], low[:, lanes], high[:, lanes]], axis=1)
                                )
                    return carry

                lax.fori_loop(0, 2, one_kind, 0)

            if read is None:
                continue

            def one_group(group, carry, target=target):
                at = pl.ds(pl.multiple_of(group * per * p_pad, 16), per * p_pad)
                y = dot(jnp.concatenate([rows_done[k, at, :] for k in range(4)], axis=0), azimuth_up_ref[...])
                for i in range(per):
                    terms = [y[(k * per + i) * p_pad : (k * per + i + 1) * p_pad] * phase_ref[k] for k in range(4)]
                    if target == 0:
                        value = (terms[0] - terms[1]) + (terms[2] - terms[3])
                    else:
                        value = (terms[0] + terms[1]) + (terms[2] + terms[3])
                    at = pl.ds(pl.multiple_of((group * per + i) * 64 + target * 32 + (step - 1) * 8, 8), 8)
                    for lane_tile in range(lane_tiles):
                        lanes = slice(lane_tile * LANES, (lane_tile + 1) * LANES)
                        for row_tile in range(row_tiles):
                            tile = value[row_tile * 8 : row_tile * 8 + 8, lanes]
                            parent_out[lane_tile * row_tiles + row_tile, at, :] = tile
                return carry

            lax.fori_loop(0, parents // per, one_group, 0)

    pl.when(step == 0)(lambda: channel(None, wide_even))
    pl.when((step == 1) | (step == 3))(lambda: channel(wide_even, wide_odd))
    pl.when(step == 2)(lambda: channel(wide_odd, wide_even))
    pl.when(step == 4)(lambda: channel(wide_odd, None))

    @pl.when(step == 4)
    def _():
        def one_tile(tile, carry):
            box = tile // (p_pad // 16)
            row_pair = tile % (p_pad // 16)
            sources = [pl.ds(pl.multiple_of(source_ref[box, e] * 64, 64), 64) for e in range(entries)]
            kinds = [pl.ds(pl.multiple_of(kind_ref[box, e] * 8, 8), 8) for e in range(entries)]
            for lane_tile in range(lane_tiles):
                halves = []
                for i in range(2):
                    where = lane_tile * row_tiles + 2 * row_pair + i
                    total = [None] * 8
                    for e in range(entries):
                        x = parent_out[where, sources[e], :]
                        real, imag = (table_by_kind[where, part, kinds[e], :] for part in range(2))
                        for c in range(4):
                            xr, xi = x[c * 8 : c * 8 + 8], x[(4 + c) * 8 : (4 + c) * 8 + 8]
                            re = xr * real - xi * imag
                            im = xr * imag + xi * real
                            total[c] = re if e == 0 else total[c] + re
                            total[4 + c] = im if e == 0 else total[4 + c] + im
                    halves.append(total)
                for c in range(8):
                    high, low = split(jnp.concatenate([halves[0][c], halves[1][c]], axis=0))
                    at = pl.ds(pl.multiple_of((c * parents + box) * p_pad + row_pair * 16, 16), 16)
                    lanes = slice(lane_tile * LANES, (lane_tile + 1) * LANES)
                    in_high[at, lanes] = high
                    in_low[at, lanes] = low
            return carry

        lax.fori_loop(0, parents * (p_pad // 16), one_tile, 0)

        down = azimuth_down_ref[...]
        down_high = down[:, :f_pad]
        high, low = split(polar_down_ref[...])
        polar_back = jnp.concatenate([high, high, low], axis=1)
        per = parents

        def one_group(group, carry):
            at = pl.ds(pl.multiple_of(group * per * p_pad, 16), per * p_pad)
            high = in_high[at, :]
            low = in_low[at, :]
            both = dot(high, down)
            y = both[:, :f_pad] + both[:, f_pad:] + dot(low, down_high)
            for i in range(0, per, 2):
                x = jnp.concatenate([y[i * p_pad : (i + 1) * p_pad], y[(i + 1) * p_pad : (i + 2) * p_pad]], axis=1)
                high, low = split(x)
                z = dot(polar_back, jnp.concatenate([high, low, high], axis=0))
                for j in range(2):
                    lowered[pl.ds(pl.multiple_of(((i + j) * 8 + group) * pitch, 8), t_pad), :] = z[
                        :, j * f_pad : (j + 1) * f_pad
                    ]
            return carry

        lax.fori_loop(0, 8 * parents // per, one_group, 0)

        per_turn = next(n for n in (6, 5, 3, 2, 1) if (rows + 6) % n == 0)

        def some_rows(i, carry):
            for r in range(per_turn):
                turned = lowered[pl.ds(i * per_turn + r, 8 * parents, stride=pitch), :].T
                out_ref[i * per_turn + r] = turned[: columns + 8]
            return carry

        lax.fori_loop(0, (rows + 6) // per_turn, some_rows, 0)


def parent_level(child_out, after, before, side, table, sources, kinds, combine, polar_cos, polar_sin, phase):
    _, rows, columns, boxes = child_out.shape
    _, rows_up, columns_up, translators = table.shape
    assert boxes == LANES and translators == LANES
    parents, entries = sources.shape
    t_pad, p_pad = polar_cos.shape[1], polar_cos.shape[0]
    f_pad, q_pad = round_up(columns + 8, LANES), round_up(columns_up, LANES)
    assert f_pad == LANES
    table_steps = next(s for s in (4, 2, 1) if rows_up % s == 0)
    table_rows = rows_up // table_steps
    n_theta, n_phi = lax.axis_size("theta"), lax.axis_size("phi")
    polar_up = local_up(rows_up * n_theta, rows * n_theta, True, rows_up, rows, 3, (p_pad, t_pad))
    azimuth_up = local_up(columns_up * n_phi, columns * n_phi, False, columns_up, columns, 2, (q_pad, f_pad))
    high, low = split_constant(np.ascontiguousarray(azimuth_up.T))
    azimuth_three = jnp.asarray(np.concatenate([high, high, low], axis=0))
    high, low = split_constant(azimuth_up)
    azimuth_down = jnp.asarray(np.concatenate([high, low], axis=1))
    polar_down = jnp.asarray(np.ascontiguousarray(polar_up.T))

    def whole(array):
        return pl.BlockSpec(array.shape, lambda g: (0,) * array.ndim)

    def channel(shape):
        return pl.BlockSpec((2, 1) + shape, lambda g: (0, jnp.minimum(g, 3), 0, 0, 0))

    smem = pl.BlockSpec(memory_space=pltpu.SMEM)
    constants = [combine, polar_cos, polar_sin, azimuth_three, polar_down, azimuth_down, phase]
    return pl.pallas_call(
        functools.partial(
            parent_kernel, (rows, columns, rows_up, columns_up, parents, entries, table_steps, table_rows)
        ),
        grid=(5,),
        in_specs=[
            smem,
            smem,
            channel((rows, columns, boxes)),
            channel((3, columns, boxes)),
            channel((3, columns, boxes)),
            channel((rows + 6, 8, boxes)),
            pl.BlockSpec(
                (2, table_rows, columns_up, translators), lambda g: (0, jnp.minimum(g, table_steps - 1), 0, 0)
            ),
        ]
        + [whole(c) for c in constants],
        out_specs=pl.BlockSpec((rows + 6, columns + 8, 8 * parents), lambda g: (0, 0, 0)),
        out_shape=jax.ShapeDtypeStruct((rows + 6, columns + 8, 8 * parents), F32),
        scratch_shapes=[
            pltpu.VMEM((2, 128 * (t_pad + 8), f_pad), F32),
            pltpu.VMEM((2, 128 * (t_pad + 8), f_pad), F32),
            pltpu.VMEM((4, parents * p_pad, 3 * f_pad), BF16),
            pltpu.VMEM((q_pad // LANES * (p_pad // 8), 2, translators * 8, LANES), F32),
            pltpu.VMEM((q_pad // LANES * (p_pad // 8), parents * 64, LANES), F32),
            pltpu.VMEM((8 * parents * p_pad, q_pad), BF16),
            pltpu.VMEM((8 * parents * p_pad, q_pad), BF16),
            pltpu.VMEM((8 * parents * (t_pad + 8), f_pad), F32),
        ],
        compiler_params=pltpu.CompilerParams(vmem_limit_bytes=60 * MIB),
        cost_estimate=pl.CostEstimate(
            flops=20_000_000_000, bytes_accessed=child_out.size * 8, transcendentals=0
        ),
        name="parent_level",
    )(
        sources,
        kinds,
        child_out.reshape((2, 4) + child_out.shape[1:]),
        after.reshape((2, 4) + after.shape[1:]),
        before.reshape((2, 4) + before.shape[1:]),
        side.reshape((2, 4) + side.shape[1:]),
        table,
        *constants,
    )


def chain(count, periodic):
    pairs = [(i, i + 1) for i in range(count - 1)]
    return pairs + [(count - 1, 0)] if periodic else pairs


def send(block, axis, up):
    pairs = chain(lax.axis_size(axis), axis == "phi")
    return lax.ppermute(block, axis, pairs if up else [(b, a) for a, b in pairs])


def plain(array):
    return with_layout_constraint(array, Layout(major_to_minor=tuple(range(array.ndim))))


def per_device(
    child_out,
    child_slot,
    sources_child,
    kinds_child,
    table_child,
    sources_parent,
    kinds_parent,
    table_parent,
):
    _, rows, columns, boxes = child_out.shape
    _, rows_up, columns_up, _ = table_parent.shape
    parents = boxes // 8
    n_theta, n_phi = lax.axis_size("theta"), lax.axis_size("phi")
    t_pad, p_pad = round_up(rows + 6, 16), round_up(rows_up, 16)
    q_pad = round_up(columns_up, LANES)
    barrier = lax.optimization_barrier

    polar_up = local_up(rows_up * n_theta, rows * n_theta, True, rows_up, rows, 3, (p_pad, t_pad))
    sizes = (rows, columns, rows_up, columns_up, parents, n_theta, n_phi)
    combine, polar_cos, polar_sin, phase, phase_child = tables(
        child_slot, sizes, p_pad, t_pad, q_pad, jnp.asarray(polar_up)
    )

    samples = rows * columns
    flat_child = child_out.reshape(2, 4, samples, boxes)
    flat_table = table_child.reshape(2, samples, table_child.shape[3])
    pieces = segments(samples)
    local = [None] * len(pieces)
    chunks = [(n, i) for n, piece in enumerate(pieces) for i in range(piece[1])]

    def translate_next(child, last=False):
        if chunks:
            n, i = chunks.pop(-1 if last else 0)
            local[n] = child_translate(
                child, flat_table, sources_child.T, kinds_child.T, pieces[n], i, local[n]
            )

    after = plain(send(plain(child_out[:, :3]), "theta", False))
    before = plain(send(plain(child_out[:, rows - 3 :]), "theta", True))
    first_child, made = barrier((flat_child, (combine, polar_cos, polar_sin, phase, phase_child)))
    combine, polar_cos, polar_sin, phase, phase_child = made
    translate_next(first_child)
    if len(chunks) > 1:
        translate_next(first_child, last=True)
    after, before, local = barrier((after, before, local))

    low, high = (
        jnp.concatenate([edge[:, :, at] for edge in (child_out, after, before)], axis=1)
        for at in (slice(0, 3), slice(columns - 2, columns))
    )
    low, high, later_child = barrier((low, high, flat_child))
    right = send(low, "phi", False)
    left = send(high, "phi", True)
    translate_next(later_child)
    right, left, local = barrier((right, left, local))
    side = jnp.concatenate([right, left, jnp.zeros((8, rows + 6, 3, boxes), F32)], axis=2)

    lowered = parent_level(
        child_out,
        after,
        before,
        side,
        table_parent,
        sources_parent,
        kinds_parent,
        combine,
        polar_cos,
        polar_sin,
        phase,
    )
    lowered, later_child = barrier((lowered, flat_child))

    low = send(lowered[rows : rows + 3], "theta", True)
    high = send(lowered[rows + 3 : rows + 6], "theta", False)
    while chunks:
        translate_next(later_child)
    local, lowered = barrier((local, lowered))
    here = lowered[:rows]
    here = here + jnp.pad(low, ((0, rows - 3), (0, 0), (0, 0))) + jnp.pad(high, ((rows - 3, 0), (0, 0), (0, 0)))
    low = send(here[:, columns : columns + 3], "phi", True)
    high = send(here[:, columns + 3 : columns + 5], "phi", False)
    here = here[:, :columns]
    here = here + jnp.pad(low, ((0, 0), (0, columns - 3), (0, 0))) + jnp.pad(high, ((0, 0), (columns - 2, 0), (0, 0)))
    here = here.reshape(samples, boxes)

    result = None
    for piece, part in zip(pieces, local):
        result = final_sum(flat_child.shape, part, here, phase_child, child_slot, piece, result)
    return result.reshape(child_out.shape)


def solution(mesh):
    placed = (
        P(None, "theta", "phi", None),
        P(),
        P(),
        P(),
        P(None, "theta", "phi", None),
        P(),
        P(),
        P(None, "theta", "phi", None),
    )
    return jax.shard_map(
        per_device,
        mesh=mesh,
        in_specs=placed,
        out_specs=P(None, "theta", "phi", None),
        check_vma=False,
    )
```

```python
import functools
import math

import jax
import jax.numpy as jnp
import numpy as np
from jax import lax
from jax.experimental import pallas as pl
from jax.experimental.layout import Layout, with_layout_constraint
from jax.experimental.pallas import tpu as pltpu
from jax.sharding import PartitionSpec as P

BAND1 = 180
WAVE = BAND1 / (2.0 * math.sqrt(3.0))
LANES = 128
MIB = 1 << 20
F32 = jnp.float32
BF16 = jnp.bfloat16


def round_up(count, step):
    return -(-count // step) * step


def stencil_entries(count_out, count_in, centered, out_rows):
    entries = []
    for row_out in out_rows:
        if centered:
            numerator = (2 * row_out + 1) * count_in - count_out
        else:
            numerator = 2 * row_out * count_in
        denominator = 2 * count_out
        base_index = numerator // denominator
        fraction = (numerator - base_index * denominator) / denominator
        for offset_a in range(-2, 4):
            weight = 1.0
            for offset_b in range(-2, 4):
                if offset_b != offset_a:
                    weight = weight * (fraction - offset_b) / (offset_a - offset_b)
            entries.append((row_out, base_index + offset_a, weight))
    return entries


def local_up(count_out, count_in, centered, rows_out, rows_in, below, shape):
    matrix = np.zeros(shape)
    for row_out, column, weight in stencil_entries(count_out, count_in, centered, range(rows_out)):
        assert -below <= column < rows_in + 3 or abs(weight) < 1e-12
        if column >= 0:
            matrix[row_out, column] += weight
        elif column >= -below:
            matrix[row_out, rows_in + 3 + below + column] += weight
    return matrix.astype(np.float32)


def split(x):
    high = x.astype(BF16)
    return high, (x - high.astype(F32)).astype(BF16)


def split_constant(matrix):
    high = matrix.astype(jnp.bfloat16)
    return high, (matrix - high.astype(np.float32)).astype(jnp.bfloat16)


def dot(a, b):
    return jnp.dot(a, b, preferred_element_type=F32)


def dot_transposed(a, b):
    return lax.dot_general(a, b, (((1,), (1,)), ((), ())), preferred_element_type=F32)


def segments(samples):
    full, rest = divmod(samples, 8 * LANES)
    found = [(0, full, 1, 8)] if full else []
    if rest:
        rows = -(-rest // LANES)
        packed = 4 if rows <= 2 else 2 if rows <= 4 else 1
        found.append((full, 1, packed, rows))
    return found


def translate_kernel(packed, rows, source_ref, kind_ref, child_ref, table_ref, *rest):
    out_ref, pattern, table = rest[-3:]
    groups, per = 4 // packed, 8 // packed
    tile = 16 * groups
    pitch = tile + 8
    entries = source_ref.shape[0]
    step = pl.program_id(0)

    @pl.when(step == 0)
    def _():
        for row in range(rows):
            real, imag = (table_ref[part, row * LANES : (row + 1) * LANES].T for part in range(2))
            for part, turned in enumerate((real, imag - real, real + imag)):
                for c in range(packed):
                    table[part, pl.ds(c * per + row, LANES, stride=8), :] = turned

    @pl.when(step < 2)
    def _():
        for i in range(2):
            c = 2 * step + i
            plane, sub = (c, 0) if packed == 1 else (c // packed, c % packed * per)
            for part in range(2):
                for row in range(rows):
                    at = pl.ds((part * groups + plane) * 8 + sub + row, LANES, stride=pitch)
                    pattern[at, :] = child_ref[part, i, row * LANES : (row + 1) * LANES].T

    @pl.when(step >= 2)
    def _():
        half = LANES // 2

        def one_box(i, carry):
            box = (step - 2) * half + i
            sums = [[None] * groups for _ in range(3)]
            for entry in range(entries):
                x = pattern[pl.ds(pl.multiple_of(source_ref[entry, box] * pitch, 8), tile), :]
                kind = pl.ds(pl.multiple_of(kind_ref[entry, box] * 8, 8), 8)
                factors = [table[part, kind, :] for part in range(3)]
                for g in range(groups):
                    xr, xi = x[g * 8 : g * 8 + 8], x[(groups + g) * 8 : (groups + g) * 8 + 8]
                    for part, term in enumerate((xr + xi, xr, xi)):
                        product = term * factors[part]
                        sums[part][g] = product if entry == 0 else sums[part][g] + product
            total = [sums[0][g] - sums[2][g] for g in range(groups)]
            total += [sums[0][g] + sums[1][g] for g in range(groups)]
            for g in range(2 * groups):
                out_ref[0, pl.ds(pl.multiple_of(i * tile, tile) + g * 8, 8), :] = total[g]
            return carry

        lax.fori_loop(0, half, one_box, 0, unroll=2)


def child_translate(child, table, sources, kinds, segment, chunk, onto):
    first, count, packed, rows = segment
    tile = 64 // packed
    smem = pl.BlockSpec(memory_space=pltpu.SMEM)
    in_specs = [
        smem,
        smem,
        pl.BlockSpec((2, 2, 8 * LANES, LANES), lambda s: (0, jnp.minimum(s, 1), first + chunk, 0)),
        pl.BlockSpec((2, 8 * LANES, LANES), lambda s: (0, first + chunk, 0)),
    ]
    operands = [sources, kinds, child, table]
    aliases = {}
    if onto is not None:
        in_specs.append(pl.BlockSpec(memory_space=pl.ANY))
        operands.append(onto)
        aliases = {4: 0}
    work = rows * LANES * LANES
    return pl.pallas_call(
        functools.partial(translate_kernel, packed, rows),
        grid=(4,),
        in_specs=in_specs,
        out_specs=pl.BlockSpec((1, LANES // 2 * tile, LANES), lambda s: (chunk, jnp.maximum(s - 2, 0), 0)),
        out_shape=jax.ShapeDtypeStruct((count, LANES * tile, LANES), F32),
        input_output_aliases=aliases,
        scratch_shapes=[pltpu.VMEM((LANES * (tile + 8), LANES), F32), pltpu.VMEM((3, LANES * 8, LANES), F32)],
        compiler_params=pltpu.CompilerParams(vmem_limit_bytes=60 * MIB),
        cost_estimate=pl.CostEstimate(
            flops=work * sources.shape[0] * 32, bytes_accessed=work * 72, transcendentals=0
        ),
        name="child_translate",
    )(*operands)


def sum_kernel(packed, rows, parents, slot_ref, local_ref, lowered_ref, phase_ref, *rest):
    out_ref, lowered, total, phase = rest[-4:]
    groups, per = 4 // packed, 8 // packed
    tile = 16 * groups
    pitch = tile + 8
    step = pl.program_id(1)

    @pl.when(step == 0)
    def _():
        for row in range(rows):
            lowered[pl.ds(row, LANES, stride=per), :] = lowered_ref[row * LANES : (row + 1) * LANES].T
        for octant in range(8):
            for part in range(2):
                phase[2 * octant + part] = jnp.concatenate([phase_ref[8 * part + octant, :per]] * packed, axis=0)

    @pl.when(step < 2)
    def _():
        half = LANES // 2

        def one_box(i, carry):
            slot = slot_ref[step * half + i]
            octant = slot >> (parents.bit_length() - 1)
            cosine, sine = phase[2 * octant], phase[2 * octant + 1]
            x = lowered[pl.ds(pl.multiple_of((slot & (parents - 1)) * tile, tile), tile), :]
            local = local_ref[0, pl.ds(pl.multiple_of(i * tile, tile), tile), :]
            here = pl.multiple_of((step * half + i) * pitch, 8)
            for g in range(groups):
                at, to = slice(g * 8, g * 8 + 8), slice((groups + g) * 8, (groups + g) * 8 + 8)
                real, imag = x[at], x[to]
                total[pl.ds(here + g * 8, 8), :] = local[at] + (real * cosine + imag * sine)
                total[pl.ds(here + (groups + g) * 8, 8), :] = local[to] + (imag * cosine - real * sine)
            return carry

        lax.fori_loop(0, half, one_box, 0, unroll=4)

    @pl.when(step >= 2)
    def _():
        for i in range(2):
            c = 2 * (step - 2) + i
            plane, sub = (c, 0) if packed == 1 else (c // packed, c % packed * per)
            for part in range(2):
                for row in range(rows):
                    at = pl.ds((part * groups + plane) * 8 + sub + row, LANES, stride=pitch)
                    out_ref[part, i, row * LANES : (row + 1) * LANES] = total[at, :].T


def final_sum(shape, local, lowered, phase, slots, segment, onto):
    first, count, packed, rows = segment
    tile = 64 // packed
    in_specs = [
        pl.BlockSpec(memory_space=pltpu.SMEM),
        pl.BlockSpec((1, LANES // 2 * tile, LANES), lambda i, s: (i, jnp.minimum(s, 1), 0)),
        pl.BlockSpec((8 * LANES, LANES), lambda i, s: (first + i, 0)),
        pl.BlockSpec((16, 8, LANES), lambda i, s: (0, first + i, 0)),
    ]
    operands = [slots, local, lowered, phase]
    aliases = {}
    if onto is not None:
        in_specs.append(pl.BlockSpec(memory_space=pl.ANY))
        operands.append(onto)
        aliases = {4: 0}
    work = count * rows * LANES * LANES
    return pl.pallas_call(
        functools.partial(sum_kernel, packed, rows, LANES // 8),
        grid=(count, 4),
        in_specs=in_specs,
        out_specs=pl.BlockSpec((2, 2, 8 * LANES, LANES), lambda i, s: (0, jnp.maximum(s - 2, 0), first + i, 0)),
        out_shape=jax.ShapeDtypeStruct(shape, F32),
        input_output_aliases=aliases,
        scratch_shapes=[
            pltpu.VMEM((LANES * (8 // packed), LANES), F32),
            pltpu.VMEM((LANES * (tile + 8), LANES), F32),
            pltpu.VMEM((16, 8, LANES), F32),
        ],
        compiler_params=pltpu.CompilerParams(vmem_limit_bytes=60 * MIB),
        cost_estimate=pl.CostEstimate(flops=work * 32, bytes_accessed=work * 72, transcendentals=0),
        name="final_sum",
    )(*operands)


def cos_sin(x):
    turns = jnp.floor(x * (2.0 / math.pi) + 0.5)
    rest = ((x - turns * 1.5703125) - turns * 4.837512969970703e-4) - turns * 7.54978995489188e-8
    square = rest * rest
    sine = rest + rest * square * (
        -1.6666654611e-1 + square * (8.3321608736e-3 + square * -1.9515295891e-4)
    )
    cosine = (1.0 - 0.5 * square) + square * square * (
        4.166664568298827e-2 + square * (-1.388731625493765e-3 + square * 2.443315711809948e-5)
    )
    quarter = turns.astype(jnp.int32)
    odd = (quarter & 1) == 1
    first, second = jnp.where(odd, sine, cosine), jnp.where(odd, cosine, sine)
    first = jnp.where(((quarter + 1) & 2) == 2, -first, first)
    second = jnp.where((quarter & 2) == 2, -second, second)
    return first, second


def tables_kernel(sizes, slot_ref, polar_up_ref, combine_ref, cos_ref, sin_ref, phase_ref, child_ref):
    rows, columns, rows_up, columns_up, parents, n_theta, n_phi = sizes
    polar_index, azimuth_index = lax.axis_index("theta"), lax.axis_index("phi")

    def iota(shape, axis):
        return lax.broadcasted_iota(jnp.int32, shape, axis)

    boxes = slot_ref.shape[1]
    slot = jnp.broadcast_to(slot_ref[...], (parents, boxes))
    same = (slot & (parents - 1)) == iota((parents, boxes), 0)
    octant = slot >> (parents.bit_length() - 1)
    east, north, upper = (2 * ((octant >> n) & 1) - 1 for n in range(3))
    blocks = []
    for z in range(2):
        for kind in range(2):
            for difference in range(2):
                chosen = same & ((east == north) if kind == 0 else (east != north))
                weight = (upper if z else 1) * (east if difference else 1)
                weight = jnp.where(chosen, weight, 0).astype(F32)
                blocks.append(weight)
    combine = jnp.concatenate(blocks, axis=0).astype(BF16)
    combine_ref[...] = jnp.concatenate([combine, combine], axis=1)

    p_pad, t_pad = cos_ref.shape
    q_pad = phase_ref.shape[2]
    polar = (iota((p_pad, LANES), 0) + polar_index * rows_up).astype(F32) + 0.5
    cosine, sine = cos_sin(polar * (math.pi / (rows_up * n_theta)))
    up_cos, up_sin = cos_sin(WAVE * cosine)
    cos_ref[...] = polar_up_ref[...] * up_cos[:, :t_pad]
    sin_ref[...] = polar_up_ref[...] * up_sin[:, :t_pad]
    azimuth = (iota((8, q_pad), 1) + azimuth_index * columns_up).astype(F32)
    east, north = cos_sin(azimuth * (2.0 * math.pi / (columns_up * n_phi)))
    flat = WAVE * sine
    valid = iota((p_pad, LANES), 0) < rows_up
    for lane in range(0, q_pad, LANES):
        lanes = slice(lane, lane + LANES)
        inside = valid & (iota((p_pad, LANES), 1) + lane < columns_up)
        for kind in range(2):
            turned = (east - north if kind else east + north)[:1, lanes]
            found = cos_sin(flat * turned)
            for i in range(2):
                phase_ref[2 * kind + i, :, lanes] = jnp.where(inside, found[i], 0.0)

    count = child_ref.shape[1]
    sample = iota((count, LANES), 0) * LANES + iota((count, LANES), 1)
    row = jnp.floor((sample.astype(F32) + 0.5) * (1.0 / columns))
    polar = row + (polar_index * rows).astype(F32) + 0.5
    azimuth = sample.astype(F32) - row * columns + (azimuth_index * columns).astype(F32)
    up, flat = cos_sin(polar * (math.pi / (rows * n_theta)))
    east, north = cos_sin(azimuth * (2.0 * math.pi / (columns * n_phi)))
    for octant in range(4):
        signs = [2 * ((octant >> n) & 1) - 1 for n in range(3)]
        found = cos_sin(WAVE * (flat * east * signs[0] + flat * north * signs[1] + up * signs[2]))
        child_ref[octant] = found[0]
        child_ref[7 - octant] = found[0]
        child_ref[8 + octant] = found[1]
        child_ref[15 - octant] = -found[1]


def tables(slots, sizes, p_pad, t_pad, q_pad, polar_up):
    rows, columns, rows_up, columns_up, parents, n_theta, n_phi = sizes
    boxes = slots.shape[0]
    assert parents & (parents - 1) == 0
    return pl.pallas_call(
        functools.partial(tables_kernel, sizes),
        out_shape=[
            jax.ShapeDtypeStruct((8 * parents, 2 * boxes), BF16),
            jax.ShapeDtypeStruct((p_pad, t_pad), F32),
            jax.ShapeDtypeStruct((p_pad, t_pad), F32),
            jax.ShapeDtypeStruct((4, p_pad, q_pad), F32),
            jax.ShapeDtypeStruct((16, -(-rows * columns // LANES), LANES), F32),
        ],
        compiler_params=pltpu.CompilerParams(vmem_limit_bytes=60 * MIB),
        name="tables",
    )(slots.reshape(1, boxes), polar_up)


def parent_kernel(
    sizes,
    source_ref,
    kind_ref,
    child_ref,
    next_ref,
    previous_ref,
    side_ref,
    table_ref,
    combine_ref,
    polar_cos_ref,
    polar_sin_ref,
    azimuth_up_ref,
    polar_down_ref,
    azimuth_down_ref,
    phase_ref,
    out_ref,
    wide_even,
    wide_odd,
    rows_done,
    table_by_kind,
    parent_out,
    in_high,
    in_low,
    lowered,
):
    (rows, columns, rows_up, columns_up, parents, entries, table_steps, table_rows) = sizes
    pitch, f_pad = wide_even.shape[1] // 128, wide_even.shape[2]
    t_pad = pitch - 8
    p_pad, q_pad = phase_ref.shape[1], phase_ref.shape[2]
    row_tiles, lane_tiles = p_pad // 8, q_pad // LANES
    step = pl.program_id(0)
    half = 4 * parents
    table_first = jnp.minimum(step, table_steps - 1) * table_rows

    @pl.when(step == 0)
    def _():
        for part in range(2):
            for t in range(rows + 6, t_pad):
                for wide in (wide_even, wide_odd):
                    wide[part, pl.ds(t, 128, stride=pitch), :] = jnp.zeros((128, f_pad), F32)
        for part in range(2):
            for p in range(rows_up, p_pad):
                for lane_tile in range(lane_tiles):
                    at = pl.ds(p % 8, 128, stride=8)
                    table_by_kind[lane_tile * row_tiles + p // 8, part, at, :] = jnp.zeros((128, LANES), F32)

    combine = combine_ref[...]

    def samples(part, main_ref, r, t):
        x = jnp.concatenate(
            [main_ref[part, 0, r], side_ref[part, 0, t], jnp.zeros((f_pad - columns - 8, LANES), F32)], axis=0
        )
        high, low = split(x)
        return jnp.concatenate([high, low], axis=1)

    def turn(rows_here, wide):
        pieces = [(part,) + row for row in rows_here for part in range(2)]
        for i in range(0, len(pieces), 2):
            both = jnp.concatenate([samples(*piece) for piece in pieces[i : i + 2]], axis=0)
            turned = dot_transposed(combine, both)
            for j, piece in enumerate(pieces[i : i + 2]):
                at = pl.ds(piece[3], 128, stride=pitch)
                wide[piece[0], at, :] = turned[:, j * f_pad : (j + 1) * f_pad]

    def turn_table(r):
        p = table_first + r
        at = pl.ds(p & 7, 128, stride=8)
        for part in range(2):
            x = table_ref[part, r]
            if q_pad > columns_up:
                x = jnp.concatenate([x, jnp.zeros((q_pad - columns_up, LANES), F32)], axis=0)
            for lane_tile in range(lane_tiles):
                turned = x[lane_tile * LANES : (lane_tile + 1) * LANES].T
                table_by_kind[lane_tile * row_tiles + (p >> 3), part, at, :] = turned

    def shares(count):
        pairs = -(-count // 2)
        sizes_here = [(pairs + 3 - i) // 4 for i in range(4)]
        return [(2 * sum(sizes_here[:i]), sizes_here[i]) for i in range(4)]

    per = 4

    def channel(read, write):
        if write is not None:
            turn(
                [(next_ref, r, rows + r) for r in range(3)] + [(previous_ref, r, rows + 3 + r) for r in range(3)],
                write,
            )
        if read is not None:
            polar = []
            for sign in (-1.0, 1.0):
                high, low = split(jnp.concatenate([polar_cos_ref[...], sign * polar_sin_ref[...]], axis=1))
                polar.append(jnp.concatenate([high, high, low], axis=1))
        for target in range(2):
            for difference in range(2):
                part = target if difference == 0 else 1 - target
                loop = 2 * target + difference

                def one_kind(kind, carry, part=part, difference=difference, loop=loop):
                    if write is not None:
                        first, count = shares(rows)[loop]
                        here = [jnp.minimum(first + kind * count + j, rows - 1) for j in range(count)]
                        turn([(child_ref, r, r) for r in here], write)
                        first, count = shares(table_rows)[loop]
                        for j in range(count):
                            turn_table(jnp.minimum(first + kind * count + j, table_rows - 1))
                    if read is not None:
                        first = (kind * 2 + difference) * parents
                        for pair in range(parents // 2):
                            stacked = []
                            for source, offset in ((part, 0), (1 - part, half)):
                                at = (offset + first + 2 * pair) * pitch
                                both = [
                                    read[source, pl.ds(pl.multiple_of(at + i * pitch, 8), t_pad), :] for i in range(2)
                                ]
                                stacked.append(jnp.concatenate(both, axis=1))
                            high, low = split(jnp.concatenate(stacked, axis=0))
                            result = dot(polar[part], jnp.concatenate([high, low, high], axis=0))
                            high, low = split(result)
                            for i in range(2):
                                lanes = slice(i * f_pad, (i + 1) * f_pad)
                                rows_done[kind * 2 + difference, pl.ds((2 * pair + i) * p_pad, p_pad), :] = (
                                    jnp.concatenate([high[:, lanes], low[:, lanes], high[:, lanes]], axis=1)
                                )
                    return carry

                lax.fori_loop(0, 2, one_kind, 0)

            if read is None:
                continue

            def one_group(group, carry, target=target):
                at = pl.ds(pl.multiple_of(group * per * p_pad, 16), per * p_pad)
                y = dot(jnp.concatenate([rows_done[k, at, :] for k in range(4)], axis=0), azimuth_up_ref[...])
                for i in range(per):
                    terms = [y[(k * per + i) * p_pad : (k * per + i + 1) * p_pad] * phase_ref[k] for k in range(4)]
                    if target == 0:
                        value = (terms[0] - terms[1]) + (terms[2] - terms[3])
                    else:
                        value = (terms[0] + terms[1]) + (terms[2] + terms[3])
                    at, to, both = (
                        pl.ds(pl.multiple_of((group * per + i) * 96 + part * 32 + (step - 1) * 8, 8), 8)
                        for part in range(3)
                    )
                    for lane_tile in range(lane_tiles):
                        lanes = slice(lane_tile * LANES, (lane_tile + 1) * LANES)
                        for row_tile in range(row_tiles):
                            tile = value[row_tile * 8 : row_tile * 8 + 8, lanes]
                            where = lane_tile * row_tiles + row_tile
                            if target == 0:
                                parent_out[where, at, :] = tile
                            else:
                                parent_out[where, to, :] = tile
                                parent_out[where, both, :] = parent_out[where, at, :] + tile
                return carry

            lax.fori_loop(0, parents // per, one_group, 0)

    pl.when(step == 0)(lambda: channel(None, wide_even))
    pl.when((step == 1) | (step == 3))(lambda: channel(wide_even, wide_odd))
    pl.when(step == 2)(lambda: channel(wide_odd, wide_even))
    pl.when(step == 4)(lambda: channel(wide_odd, None))

    @pl.when(step == 4)
    def _():
        def one_tile(tile, carry):
            box = tile // (p_pad // 16)
            row_pair = tile % (p_pad // 16)
            sources = [pl.ds(pl.multiple_of(source_ref[box, e] * 96, 32), 96) for e in range(entries)]
            kinds = [pl.ds(pl.multiple_of(kind_ref[box, e] * 8, 8), 8) for e in range(entries)]
            for lane_tile in range(lane_tiles):
                halves = []
                for i in range(2):
                    where = lane_tile * row_tiles + 2 * row_pair + i
                    sums = [[None] * 4 for _ in range(3)]
                    for e in range(entries):
                        x = parent_out[where, sources[e], :]
                        real, imag = (table_by_kind[where, part, kinds[e], :] for part in range(2))
                        factors = (imag - real, real + imag, real)
                        for c in range(4):
                            for part in range(3):
                                product = x[(4 * part + c) * 8 : (4 * part + c) * 8 + 8] * factors[part]
                                sums[part][c] = product if e == 0 else sums[part][c] + product
                    total = [sums[2][c] - sums[1][c] for c in range(4)]
                    total += [sums[2][c] + sums[0][c] for c in range(4)]
                    halves.append(total)
                for c in range(8):
                    high, low = split(jnp.concatenate([halves[0][c], halves[1][c]], axis=0))
                    at = pl.ds(pl.multiple_of((c * parents + box) * p_pad + row_pair * 16, 16), 16)
                    lanes = slice(lane_tile * LANES, (lane_tile + 1) * LANES)
                    in_high[at, lanes] = high
                    in_low[at, lanes] = low
            return carry

        lax.fori_loop(0, parents * (p_pad // 16), one_tile, 0)

        down = azimuth_down_ref[...]
        down_high = down[:, :f_pad]
        high, low = split(polar_down_ref[...])
        polar_back = jnp.concatenate([high, high, low], axis=1)
        per = parents

        def one_group(group, carry):
            at = pl.ds(pl.multiple_of(group * per * p_pad, 16), per * p_pad)
            high = in_high[at, :]
            low = in_low[at, :]
            both = dot(high, down)
            y = both[:, :f_pad] + both[:, f_pad:] + dot(low, down_high)
            for i in range(0, per, 2):
                x = jnp.concatenate([y[i * p_pad : (i + 1) * p_pad], y[(i + 1) * p_pad : (i + 2) * p_pad]], axis=1)
                high, low = split(x)
                z = dot(polar_back, jnp.concatenate([high, low, high], axis=0))
                for j in range(2):
                    lowered[pl.ds(pl.multiple_of(((i + j) * 8 + group) * pitch, 8), t_pad), :] = z[
                        :, j * f_pad : (j + 1) * f_pad
                    ]
            return carry

        lax.fori_loop(0, 8 * parents // per, one_group, 0)

        per_turn = next(n for n in (6, 5, 3, 2, 1) if (rows + 6) % n == 0)

        def some_rows(i, carry):
            for r in range(per_turn):
                turned = lowered[pl.ds(i * per_turn + r, 8 * parents, stride=pitch), :].T
                out_ref[i * per_turn + r] = turned[: columns + 8]
            return carry

        lax.fori_loop(0, (rows + 6) // per_turn, some_rows, 0)


def parent_level(child_out, after, before, side, table, sources, kinds, combine, polar_cos, polar_sin, phase):
    _, rows, columns, boxes = child_out.shape
    _, rows_up, columns_up, translators = table.shape
    assert boxes == LANES and translators == LANES
    parents, entries = sources.shape
    t_pad, p_pad = polar_cos.shape[1], polar_cos.shape[0]
    f_pad, q_pad = round_up(columns + 8, LANES), round_up(columns_up, LANES)
    assert f_pad == LANES
    table_steps = next(s for s in (4, 2, 1) if rows_up % s == 0)
    table_rows = rows_up // table_steps
    n_theta, n_phi = lax.axis_size("theta"), lax.axis_size("phi")
    polar_up = local_up(rows_up * n_theta, rows * n_theta, True, rows_up, rows, 3, (p_pad, t_pad))
    azimuth_up = local_up(columns_up * n_phi, columns * n_phi, False, columns_up, columns, 2, (q_pad, f_pad))
    high, low = split_constant(np.ascontiguousarray(azimuth_up.T))
    azimuth_three = jnp.asarray(np.concatenate([high, high, low], axis=0))
    high, low = split_constant(azimuth_up)
    azimuth_down = jnp.asarray(np.concatenate([high, low], axis=1))
    polar_down = jnp.asarray(np.ascontiguousarray(polar_up.T))

    def whole(array):
        return pl.BlockSpec(array.shape, lambda g: (0,) * array.ndim)

    def channel(shape):
        return pl.BlockSpec((2, 1) + shape, lambda g: (0, jnp.minimum(g, 3), 0, 0, 0))

    smem = pl.BlockSpec(memory_space=pltpu.SMEM)
    constants = [combine, polar_cos, polar_sin, azimuth_three, polar_down, azimuth_down, phase]
    return pl.pallas_call(
        functools.partial(
            parent_kernel, (rows, columns, rows_up, columns_up, parents, entries, table_steps, table_rows)
        ),
        grid=(5,),
        in_specs=[
            smem,
            smem,
            channel((rows, columns, boxes)),
            channel((3, columns, boxes)),
            channel((3, columns, boxes)),
            channel((rows + 6, 8, boxes)),
            pl.BlockSpec(
                (2, table_rows, columns_up, translators), lambda g: (0, jnp.minimum(g, table_steps - 1), 0, 0)
            ),
        ]
        + [whole(c) for c in constants],
        out_specs=pl.BlockSpec((rows + 6, columns + 8, 8 * parents), lambda g: (0, 0, 0)),
        out_shape=jax.ShapeDtypeStruct((rows + 6, columns + 8, 8 * parents), F32),
        scratch_shapes=[
            pltpu.VMEM((2, 128 * (t_pad + 8), f_pad), F32),
            pltpu.VMEM((2, 128 * (t_pad + 8), f_pad), F32),
            pltpu.VMEM((4, parents * p_pad, 3 * f_pad), BF16),
            pltpu.VMEM((q_pad // LANES * (p_pad // 8), 2, translators * 8, LANES), F32),
            pltpu.VMEM((q_pad // LANES * (p_pad // 8), parents * 96, LANES), F32),
            pltpu.VMEM((8 * parents * p_pad, q_pad), BF16),
            pltpu.VMEM((8 * parents * p_pad, q_pad), BF16),
            pltpu.VMEM((8 * parents * (t_pad + 8), f_pad), F32),
        ],
        compiler_params=pltpu.CompilerParams(vmem_limit_bytes=60 * MIB),
        cost_estimate=pl.CostEstimate(
            flops=20_000_000_000, bytes_accessed=child_out.size * 8, transcendentals=0
        ),
        name="parent_level",
    )(
        sources,
        kinds,
        child_out.reshape((2, 4) + child_out.shape[1:]),
        after.reshape((2, 4) + after.shape[1:]),
        before.reshape((2, 4) + before.shape[1:]),
        side.reshape((2, 4) + side.shape[1:]),
        table,
        *constants,
    )


def chain(count, periodic):
    pairs = [(i, i + 1) for i in range(count - 1)]
    return pairs + [(count - 1, 0)] if periodic else pairs


def send(block, axis, up):
    pairs = chain(lax.axis_size(axis), axis == "phi")
    return lax.ppermute(block, axis, pairs if up else [(b, a) for a, b in pairs])


def plain(array):
    return with_layout_constraint(array, Layout(major_to_minor=tuple(range(array.ndim))))


def per_device(
    child_out,
    child_slot,
    sources_child,
    kinds_child,
    table_child,
    sources_parent,
    kinds_parent,
    table_parent,
):
    _, rows, columns, boxes = child_out.shape
    _, rows_up, columns_up, _ = table_parent.shape
    parents = boxes // 8
    n_theta, n_phi = lax.axis_size("theta"), lax.axis_size("phi")
    t_pad, p_pad = round_up(rows + 6, 16), round_up(rows_up, 16)
    q_pad = round_up(columns_up, LANES)
    barrier = lax.optimization_barrier

    polar_up = local_up(rows_up * n_theta, rows * n_theta, True, rows_up, rows, 3, (p_pad, t_pad))
    sizes = (rows, columns, rows_up, columns_up, parents, n_theta, n_phi)
    combine, polar_cos, polar_sin, phase, phase_child = tables(
        child_slot, sizes, p_pad, t_pad, q_pad, jnp.asarray(polar_up)
    )

    samples = rows * columns
    flat_child = child_out.reshape(2, 4, samples, boxes)
    flat_table = table_child.reshape(2, samples, table_child.shape[3])
    pieces = segments(samples)
    local = [None] * len(pieces)
    chunks = [(n, i) for n, piece in enumerate(pieces) for i in range(piece[1])]

    def translate_next(child):
        if chunks:
            n, i = chunks.pop(0)
            local[n] = child_translate(
                child, flat_table, sources_child.T, kinds_child.T, pieces[n], i, local[n]
            )

    after = plain(send(plain(child_out[:, :3]), "theta", False))
    before = plain(send(plain(child_out[:, rows - 3 :]), "theta", True))
    first_child, made = barrier((flat_child, (combine, polar_cos, polar_sin, phase, phase_child)))
    combine, polar_cos, polar_sin, phase, phase_child = made
    translate_next(first_child)
    after, before, local = barrier((after, before, local))

    low, high = (
        jnp.concatenate([edge[:, :, at] for edge in (child_out, after, before)], axis=1)
        for at in (slice(0, 3), slice(columns - 2, columns))
    )
    low, high, later_child = barrier((low, high, flat_child))
    right = send(low, "phi", False)
    left = send(high, "phi", True)
    if len(chunks) > 1:
        translate_next(later_child)
    right, left, local = barrier((right, left, local))
    side = jnp.concatenate([right, left, jnp.zeros((8, rows + 6, 3, boxes), F32)], axis=2)

    lowered = parent_level(
        child_out,
        after,
        before,
        side,
        table_parent,
        sources_parent,
        kinds_parent,
        combine,
        polar_cos,
        polar_sin,
        phase,
    )
    lowered, later_child = barrier((lowered, flat_child))

    low = send(lowered[rows : rows + 3], "theta", True)
    high = send(lowered[rows + 3 : rows + 6], "theta", False)
    while chunks:
        translate_next(later_child)
    local, lowered = barrier((local, lowered))
    here = lowered[:rows]
    here = here + jnp.pad(low, ((0, rows - 3), (0, 0), (0, 0))) + jnp.pad(high, ((rows - 3, 0), (0, 0), (0, 0)))
    low = send(here[:, columns : columns + 3], "phi", True)
    high = send(here[:, columns + 3 : columns + 5], "phi", False)
    here = here[:, :columns]
    here = here + jnp.pad(low, ((0, 0), (0, columns - 3), (0, 0))) + jnp.pad(high, ((0, 0), (columns - 2, 0), (0, 0)))
    here = here.reshape(samples, boxes)

    result = None
    for piece, part in zip(pieces, local):
        result = final_sum(flat_child.shape, part, here, phase_child, child_slot, piece, result)
    return result.reshape(child_out.shape)


def solution(mesh):
    placed = (
        P(None, "theta", "phi", None),
        P(),
        P(),
        P(),
        P(None, "theta", "phi", None),
        P(),
        P(),
        P(None, "theta", "phi", None),
    )
    return jax.shard_map(
        per_device,
        mesh=mesh,
        in_specs=placed,
        out_specs=P(None, "theta", "phi", None),
        check_vma=False,
    )
```

```python
import functools
import math

import jax
import jax.numpy as jnp
import numpy as np
from jax import lax
from jax.experimental import pallas as pl
from jax.experimental.layout import Layout, with_layout_constraint
from jax.experimental.pallas import tpu as pltpu
from jax.sharding import PartitionSpec as P

BAND1 = 180
WAVE = BAND1 / (2.0 * math.sqrt(3.0))
LANES = 128
MIB = 1 << 20
F32 = jnp.float32
BF16 = jnp.bfloat16


def round_up(count, step):
    return -(-count // step) * step


def stencil_entries(count_out, count_in, centered, out_rows):
    entries = []
    for row_out in out_rows:
        if centered:
            numerator = (2 * row_out + 1) * count_in - count_out
        else:
            numerator = 2 * row_out * count_in
        denominator = 2 * count_out
        base_index = numerator // denominator
        fraction = (numerator - base_index * denominator) / denominator
        for offset_a in range(-2, 4):
            weight = 1.0
            for offset_b in range(-2, 4):
                if offset_b != offset_a:
                    weight = weight * (fraction - offset_b) / (offset_a - offset_b)
            entries.append((row_out, base_index + offset_a, weight))
    return entries


def local_up(count_out, count_in, centered, rows_out, rows_in, below, shape):
    matrix = np.zeros(shape)
    for row_out, column, weight in stencil_entries(count_out, count_in, centered, range(rows_out)):
        assert -below <= column < rows_in + 3 or abs(weight) < 1e-12
        if column >= 0:
            matrix[row_out, column] += weight
        elif column >= -below:
            matrix[row_out, rows_in + 3 + below + column] += weight
    return matrix.astype(np.float32)


def split(x):
    high = x.astype(BF16)
    return high, (x - high.astype(F32)).astype(BF16)


def split_constant(matrix):
    high = matrix.astype(jnp.bfloat16)
    return high, (matrix - high.astype(np.float32)).astype(jnp.bfloat16)


def dot(a, b):
    return jnp.dot(a, b, preferred_element_type=F32)


def dot_transposed(a, b):
    return lax.dot_general(a, b, (((1,), (1,)), ((), ())), preferred_element_type=F32)


def segments(samples):
    full, rest = divmod(samples, 8 * LANES)
    found = [(0, full, 1, 8)] if full else []
    if rest:
        rows = -(-rest // LANES)
        packed = 4 if rows <= 2 else 2 if rows <= 4 else 1
        found.append((full, 1, packed, rows))
    return found


def translate_kernel(packed, rows, source_ref, kind_ref, child_ref, table_ref, *rest):
    out_ref, pattern, table = rest[-3:]
    groups, per = 4 // packed, 8 // packed
    tile = 16 * groups
    pitch = tile + 8
    entries = source_ref.shape[0]
    step = pl.program_id(0)

    @pl.when(step == 0)
    def _():
        for row in range(rows):
            real, imag = (table_ref[part, row * LANES : (row + 1) * LANES].T for part in range(2))
            for part, turned in enumerate((real, imag - real, real + imag)):
                for c in range(packed):
                    table[part, pl.ds(c * per + row, LANES, stride=8), :] = turned

    @pl.when(step < 2)
    def _():
        for i in range(2):
            c = 2 * step + i
            plane, sub = (c, 0) if packed == 1 else (c // packed, c % packed * per)
            for part in range(2):
                for row in range(rows):
                    at = pl.ds((part * groups + plane) * 8 + sub + row, LANES, stride=pitch)
                    pattern[at, :] = child_ref[part, i, row * LANES : (row + 1) * LANES].T

    @pl.when(step >= 2)
    def _():
        half = LANES // 2

        def one_box(i, carry):
            box = (step - 2) * half + i
            sums = [[None] * groups for _ in range(3)]
            for entry in range(entries):
                x = pattern[pl.ds(pl.multiple_of(source_ref[entry, box] * pitch, 8), tile), :]
                kind = pl.ds(pl.multiple_of(kind_ref[entry, box] * 8, 8), 8)
                factors = [table[part, kind, :] for part in range(3)]
                for g in range(groups):
                    xr, xi = x[g * 8 : g * 8 + 8], x[(groups + g) * 8 : (groups + g) * 8 + 8]
                    for part, term in enumerate((xr + xi, xr, xi)):
                        product = term * factors[part]
                        sums[part][g] = product if entry == 0 else sums[part][g] + product
            total = [sums[0][g] - sums[2][g] for g in range(groups)]
            total += [sums[0][g] + sums[1][g] for g in range(groups)]
            for g in range(2 * groups):
                out_ref[0, pl.ds(pl.multiple_of(i * tile, tile) + g * 8, 8), :] = total[g]
            return carry

        lax.fori_loop(0, half, one_box, 0, unroll=4)


def child_translate(child, table, sources, kinds, segment, chunk, onto):
    first, count, packed, rows = segment
    tile = 64 // packed
    smem = pl.BlockSpec(memory_space=pltpu.SMEM)
    in_specs = [
        smem,
        smem,
        pl.BlockSpec((2, 2, 8 * LANES, LANES), lambda s: (0, jnp.minimum(s, 1), first + chunk, 0)),
        pl.BlockSpec((2, 8 * LANES, LANES), lambda s: (0, first + chunk, 0)),
    ]
    operands = [sources, kinds, child, table]
    aliases = {}
    if onto is not None:
        in_specs.append(pl.BlockSpec(memory_space=pl.ANY))
        operands.append(onto)
        aliases = {4: 0}
    work = rows * LANES * LANES
    return pl.pallas_call(
        functools.partial(translate_kernel, packed, rows),
        grid=(4,),
        in_specs=in_specs,
        out_specs=pl.BlockSpec((1, LANES // 2 * tile, LANES), lambda s: (chunk, jnp.maximum(s - 2, 0), 0)),
        out_shape=jax.ShapeDtypeStruct((count, LANES * tile, LANES), F32),
        input_output_aliases=aliases,
        scratch_shapes=[pltpu.VMEM((LANES * (tile + 8), LANES), F32), pltpu.VMEM((3, LANES * 8, LANES), F32)],
        compiler_params=pltpu.CompilerParams(vmem_limit_bytes=60 * MIB),
        cost_estimate=pl.CostEstimate(
            flops=work * sources.shape[0] * 32, bytes_accessed=work * 72, transcendentals=0
        ),
        name="child_translate",
    )(*operands)


def sum_kernel(packed, rows, parents, slot_ref, local_ref, lowered_ref, phase_ref, *rest):
    out_ref, lowered, total, phase = rest[-4:]
    groups, per = 4 // packed, 8 // packed
    tile = 16 * groups
    pitch = tile + 8
    step = pl.program_id(1)

    @pl.when(step == 0)
    def _():
        for row in range(rows):
            lowered[pl.ds(row, LANES, stride=per), :] = lowered_ref[row * LANES : (row + 1) * LANES].T
        for octant in range(8):
            for part in range(2):
                phase[2 * octant + part] = jnp.concatenate([phase_ref[8 * part + octant, :per]] * packed, axis=0)

    @pl.when(step < 2)
    def _():
        half = LANES // 2

        def one_box(i, carry):
            slot = slot_ref[step * half + i]
            octant = slot >> (parents.bit_length() - 1)
            cosine, sine = phase[2 * octant], phase[2 * octant + 1]
            x = lowered[pl.ds(pl.multiple_of((slot & (parents - 1)) * tile, tile), tile), :]
            local = local_ref[0, pl.ds(pl.multiple_of(i * tile, tile), tile), :]
            here = pl.multiple_of((step * half + i) * pitch, 8)
            for g in range(groups):
                at, to = slice(g * 8, g * 8 + 8), slice((groups + g) * 8, (groups + g) * 8 + 8)
                real, imag = x[at], x[to]
                total[pl.ds(here + g * 8, 8), :] = local[at] + (real * cosine + imag * sine)
                total[pl.ds(here + (groups + g) * 8, 8), :] = local[to] + (imag * cosine - real * sine)
            return carry

        lax.fori_loop(0, half, one_box, 0, unroll=8)

    @pl.when(step >= 2)
    def _():
        for i in range(2):
            c = 2 * (step - 2) + i
            plane, sub = (c, 0) if packed == 1 else (c // packed, c % packed * per)
            for part in range(2):
                for row in range(rows):
                    at = pl.ds((part * groups + plane) * 8 + sub + row, LANES, stride=pitch)
                    out_ref[part, i, row * LANES : (row + 1) * LANES] = total[at, :].T


def final_sum(shape, local, lowered, phase, slots, segment, onto):
    first, count, packed, rows = segment
    tile = 64 // packed
    in_specs = [
        pl.BlockSpec(memory_space=pltpu.SMEM),
        pl.BlockSpec((1, LANES // 2 * tile, LANES), lambda i, s: (i, jnp.minimum(s, 1), 0)),
        pl.BlockSpec((8 * LANES, LANES), lambda i, s: (first + i, 0)),
        pl.BlockSpec((16, 8, LANES), lambda i, s: (0, first + i, 0)),
    ]
    operands = [slots, local, lowered, phase]
    aliases = {}
    if onto is not None:
        in_specs.append(pl.BlockSpec(memory_space=pl.ANY))
        operands.append(onto)
        aliases = {4: 0}
    work = count * rows * LANES * LANES
    return pl.pallas_call(
        functools.partial(sum_kernel, packed, rows, LANES // 8),
        grid=(count, 4),
        in_specs=in_specs,
        out_specs=pl.BlockSpec((2, 2, 8 * LANES, LANES), lambda i, s: (0, jnp.maximum(s - 2, 0), first + i, 0)),
        out_shape=jax.ShapeDtypeStruct(shape, F32),
        input_output_aliases=aliases,
        scratch_shapes=[
            pltpu.VMEM((LANES * (8 // packed), LANES), F32),
            pltpu.VMEM((LANES * (tile + 8), LANES), F32),
            pltpu.VMEM((16, 8, LANES), F32),
        ],
        compiler_params=pltpu.CompilerParams(vmem_limit_bytes=60 * MIB),
        cost_estimate=pl.CostEstimate(flops=work * 32, bytes_accessed=work * 72, transcendentals=0),
        name="final_sum",
    )(*operands)


def cos_sin(x):
    turns = jnp.floor(x * (2.0 / math.pi) + 0.5)
    rest = ((x - turns * 1.5703125) - turns * 4.837512969970703e-4) - turns * 7.54978995489188e-8
    square = rest * rest
    sine = rest + rest * square * (
        -1.6666654611e-1 + square * (8.3321608736e-3 + square * -1.9515295891e-4)
    )
    cosine = (1.0 - 0.5 * square) + square * square * (
        4.166664568298827e-2 + square * (-1.388731625493765e-3 + square * 2.443315711809948e-5)
    )
    quarter = turns.astype(jnp.int32)
    odd = (quarter & 1) == 1
    first, second = jnp.where(odd, sine, cosine), jnp.where(odd, cosine, sine)
    first = jnp.where(((quarter + 1) & 2) == 2, -first, first)
    second = jnp.where((quarter & 2) == 2, -second, second)
    return first, second


def tables_kernel(sizes, slot_ref, polar_up_ref, combine_ref, cos_ref, sin_ref, phase_ref, child_ref):
    rows, columns, rows_up, columns_up, parents, n_theta, n_phi = sizes
    polar_index, azimuth_index = lax.axis_index("theta"), lax.axis_index("phi")

    def iota(shape, axis):
        return lax.broadcasted_iota(jnp.int32, shape, axis)

    boxes = slot_ref.shape[1]
    slot = jnp.broadcast_to(slot_ref[...], (parents, boxes))
    same = (slot & (parents - 1)) == iota((parents, boxes), 0)
    octant = slot >> (parents.bit_length() - 1)
    east, north, upper = (2 * ((octant >> n) & 1) - 1 for n in range(3))
    blocks = []
    for z in range(2):
        for kind in range(2):
            for difference in range(2):
                chosen = same & ((east == north) if kind == 0 else (east != north))
                weight = (upper if z else 1) * (east if difference else 1)
                weight = jnp.where(chosen, weight, 0).astype(F32)
                blocks.append(weight)
    combine = jnp.concatenate(blocks, axis=0).astype(BF16)
    combine_ref[...] = jnp.concatenate([combine, combine], axis=1)

    p_pad, t_pad = cos_ref.shape
    q_pad = phase_ref.shape[2]
    polar = (iota((p_pad, LANES), 0) + polar_index * rows_up).astype(F32) + 0.5
    cosine, sine = cos_sin(polar * (math.pi / (rows_up * n_theta)))
    up_cos, up_sin = cos_sin(WAVE * cosine)
    cos_ref[...] = polar_up_ref[...] * up_cos[:, :t_pad]
    sin_ref[...] = polar_up_ref[...] * up_sin[:, :t_pad]
    azimuth = (iota((8, q_pad), 1) + azimuth_index * columns_up).astype(F32)
    east, north = cos_sin(azimuth * (2.0 * math.pi / (columns_up * n_phi)))
    flat = WAVE * sine
    valid = iota((p_pad, LANES), 0) < rows_up
    for lane in range(0, q_pad, LANES):
        lanes = slice(lane, lane + LANES)
        inside = valid & (iota((p_pad, LANES), 1) + lane < columns_up)
        for kind in range(2):
            turned = (east - north if kind else east + north)[:1, lanes]
            found = cos_sin(flat * turned)
            for i in range(2):
                phase_ref[2 * kind + i, :, lanes] = jnp.where(inside, found[i], 0.0)

    count = child_ref.shape[1]
    sample = iota((count, LANES), 0) * LANES + iota((count, LANES), 1)
    row = jnp.floor((sample.astype(F32) + 0.5) * (1.0 / columns))
    polar = row + (polar_index * rows).astype(F32) + 0.5
    azimuth = sample.astype(F32) - row * columns + (azimuth_index * columns).astype(F32)
    up, flat = cos_sin(polar * (math.pi / (rows * n_theta)))
    east, north = cos_sin(azimuth * (2.0 * math.pi / (columns * n_phi)))
    for octant in range(4):
        signs = [2 * ((octant >> n) & 1) - 1 for n in range(3)]
        found = cos_sin(WAVE * (flat * east * signs[0] + flat * north * signs[1] + up * signs[2]))
        child_ref[octant] = found[0]
        child_ref[7 - octant] = found[0]
        child_ref[8 + octant] = found[1]
        child_ref[15 - octant] = -found[1]


def tables(slots, sizes, p_pad, t_pad, q_pad, polar_up):
    rows, columns, rows_up, columns_up, parents, n_theta, n_phi = sizes
    boxes = slots.shape[0]
    assert parents & (parents - 1) == 0
    return pl.pallas_call(
        functools.partial(tables_kernel, sizes),
        out_shape=[
            jax.ShapeDtypeStruct((8 * parents, 2 * boxes), BF16),
            jax.ShapeDtypeStruct((p_pad, t_pad), F32),
            jax.ShapeDtypeStruct((p_pad, t_pad), F32),
            jax.ShapeDtypeStruct((4, p_pad, q_pad), F32),
            jax.ShapeDtypeStruct((16, -(-rows * columns // LANES), LANES), F32),
        ],
        compiler_params=pltpu.CompilerParams(vmem_limit_bytes=60 * MIB),
        name="tables",
    )(slots.reshape(1, boxes), polar_up)


def parent_kernel(
    sizes,
    source_ref,
    kind_ref,
    child_ref,
    next_ref,
    previous_ref,
    side_ref,
    table_ref,
    combine_ref,
    polar_cos_ref,
    polar_sin_ref,
    azimuth_up_ref,
    polar_down_ref,
    azimuth_down_ref,
    phase_ref,
    out_ref,
    wide_even,
    wide_odd,
    rows_done,
    table_by_kind,
    parent_out,
    in_high,
    in_low,
    lowered,
):
    (rows, columns, rows_up, columns_up, parents, entries, table_steps, table_rows) = sizes
    pitch, f_pad = wide_even.shape[1] // 128, wide_even.shape[2]
    t_pad = pitch - 8
    p_pad, q_pad = phase_ref.shape[1], phase_ref.shape[2]
    row_tiles, lane_tiles = p_pad // 8, q_pad // LANES
    step = pl.program_id(0)
    half = 4 * parents
    table_first = jnp.minimum(step, table_steps - 1) * table_rows

    @pl.when(step == 0)
    def _():
        for part in range(2):
            for t in range(rows + 6, t_pad):
                for wide in (wide_even, wide_odd):
                    wide[part, pl.ds(t, 128, stride=pitch), :] = jnp.zeros((128, f_pad), F32)
        for part in range(2):
            for p in range(rows_up, p_pad):
                for lane_tile in range(lane_tiles):
                    at = pl.ds(p % 8, 128, stride=8)
                    table_by_kind[lane_tile * row_tiles + p // 8, part, at, :] = jnp.zeros((128, LANES), F32)

    combine = combine_ref[...]

    def samples(part, main_ref, r, t):
        x = jnp.concatenate(
            [main_ref[part, 0, r], side_ref[part, 0, t], jnp.zeros((f_pad - columns - 8, LANES), F32)], axis=0
        )
        high, low = split(x)
        return jnp.concatenate([high, low], axis=1)

    def turn(rows_here, wide):
        pieces = [(part,) + row for row in rows_here for part in range(2)]
        for i in range(0, len(pieces), 2):
            both = jnp.concatenate([samples(*piece) for piece in pieces[i : i + 2]], axis=0)
            turned = dot_transposed(combine, both)
            for j, piece in enumerate(pieces[i : i + 2]):
                at = pl.ds(piece[3], 128, stride=pitch)
                wide[piece[0], at, :] = turned[:, j * f_pad : (j + 1) * f_pad]

    def turn_table(r):
        p = table_first + r
        at = pl.ds(p & 7, 128, stride=8)
        for part in range(2):
            x = table_ref[part, r]
            if q_pad > columns_up:
                x = jnp.concatenate([x, jnp.zeros((q_pad - columns_up, LANES), F32)], axis=0)
            for lane_tile in range(lane_tiles):
                turned = x[lane_tile * LANES : (lane_tile + 1) * LANES].T
                table_by_kind[lane_tile * row_tiles + (p >> 3), part, at, :] = turned

    def shares(count):
        pairs = -(-count // 2)
        sizes_here = [(pairs + 3 - i) // 4 for i in range(4)]
        return [(2 * sum(sizes_here[:i]), sizes_here[i]) for i in range(4)]

    per = 4

    def channel(read, write):
        if write is not None:
            turn(
                [(next_ref, r, rows + r) for r in range(3)] + [(previous_ref, r, rows + 3 + r) for r in range(3)],
                write,
            )
        if read is not None:
            polar = []
            for sign in (-1.0, 1.0):
                high, low = split(jnp.concatenate([polar_cos_ref[...], sign * polar_sin_ref[...]], axis=1))
                polar.append(jnp.concatenate([high, high, low], axis=1))
        for target in range(2):
            for difference in range(2):
                part = target if difference == 0 else 1 - target
                loop = 2 * target + difference

                def one_kind(kind, carry, part=part, difference=difference, loop=loop):
                    if write is not None:
                        first, count = shares(rows)[loop]
                        here = [jnp.minimum(first + kind * count + j, rows - 1) for j in range(count)]
                        turn([(child_ref, r, r) for r in here], write)
                        first, count = shares(table_rows)[loop]
                        for j in range(count):
                            turn_table(jnp.minimum(first + kind * count + j, table_rows - 1))
                    if read is not None:
                        first = (kind * 2 + difference) * parents
                        for pair in range(parents // 2):
                            stacked = []
                            for source, offset in ((part, 0), (1 - part, half)):
                                at = (offset + first + 2 * pair) * pitch
                                both = [
                                    read[source, pl.ds(pl.multiple_of(at + i * pitch, 8), t_pad), :] for i in range(2)
                                ]
                                stacked.append(jnp.concatenate(both, axis=1))
                            high, low = split(jnp.concatenate(stacked, axis=0))
                            result = dot(polar[part], jnp.concatenate([high, low, high], axis=0))
                            high, low = split(result)
                            for i in range(2):
                                lanes = slice(i * f_pad, (i + 1) * f_pad)
                                rows_done[kind * 2 + difference, pl.ds((2 * pair + i) * p_pad, p_pad), :] = (
                                    jnp.concatenate([high[:, lanes], low[:, lanes], high[:, lanes]], axis=1)
                                )
                    return carry

                lax.fori_loop(0, 2, one_kind, 0)

            if read is None:
                continue

            def one_group(group, carry, target=target):
                at = pl.ds(pl.multiple_of(group * per * p_pad, 16), per * p_pad)
                y = dot(jnp.concatenate([rows_done[k, at, :] for k in range(4)], axis=0), azimuth_up_ref[...])
                for i in range(per):
                    terms = [y[(k * per + i) * p_pad : (k * per + i + 1) * p_pad] * phase_ref[k] for k in range(4)]
                    if target == 0:
                        value = (terms[0] - terms[1]) + (terms[2] - terms[3])
                    else:
                        value = (terms[0] + terms[1]) + (terms[2] + terms[3])
                    at, to, both = (
                        pl.ds(pl.multiple_of((group * per + i) * 96 + part * 32 + (step - 1) * 8, 8), 8)
                        for part in range(3)
                    )
                    for lane_tile in range(lane_tiles):
                        lanes = slice(lane_tile * LANES, (lane_tile + 1) * LANES)
                        for row_tile in range(row_tiles):
                            tile = value[row_tile * 8 : row_tile * 8 + 8, lanes]
                            where = lane_tile * row_tiles + row_tile
                            if target == 0:
                                parent_out[where, at, :] = tile
                            else:
                                parent_out[where, to, :] = tile
                                parent_out[where, both, :] = parent_out[where, at, :] + tile
                return carry

            lax.fori_loop(0, parents // per, one_group, 0)

    pl.when(step == 0)(lambda: channel(None, wide_even))
    pl.when((step == 1) | (step == 3))(lambda: channel(wide_even, wide_odd))
    pl.when(step == 2)(lambda: channel(wide_odd, wide_even))
    pl.when(step == 4)(lambda: channel(wide_odd, None))

    @pl.when(step == 4)
    def _():
        def one_tile(tile, carry):
            box = tile // (p_pad // 16)
            row_pair = tile % (p_pad // 16)
            sources = [pl.ds(pl.multiple_of(source_ref[box, e] * 96, 32), 96) for e in range(entries)]
            kinds = [pl.ds(pl.multiple_of(kind_ref[box, e] * 8, 8), 8) for e in range(entries)]
            for lane_tile in range(lane_tiles):
                halves = []
                for i in range(2):
                    where = lane_tile * row_tiles + 2 * row_pair + i
                    sums = [[None] * 4 for _ in range(3)]
                    for e in range(entries):
                        x = parent_out[where, sources[e], :]
                        real, imag = (table_by_kind[where, part, kinds[e], :] for part in range(2))
                        factors = (imag - real, real + imag, real)
                        for c in range(4):
                            for part in range(3):
                                product = x[(4 * part + c) * 8 : (4 * part + c) * 8 + 8] * factors[part]
                                sums[part][c] = product if e == 0 else sums[part][c] + product
                    total = [sums[2][c] - sums[1][c] for c in range(4)]
                    total += [sums[2][c] + sums[0][c] for c in range(4)]
                    halves.append(total)
                for c in range(8):
                    high, low = split(jnp.concatenate([halves[0][c], halves[1][c]], axis=0))
                    at = pl.ds(pl.multiple_of((c * parents + box) * p_pad + row_pair * 16, 16), 16)
                    lanes = slice(lane_tile * LANES, (lane_tile + 1) * LANES)
                    in_high[at, lanes] = high
                    in_low[at, lanes] = low
            return carry

        lax.fori_loop(0, parents * (p_pad // 16), one_tile, 0)

        down = azimuth_down_ref[...]
        down_high = down[:, :f_pad]
        high, low = split(polar_down_ref[...])
        polar_back = jnp.concatenate([high, high, low], axis=1)
        per = parents

        def one_group(group, carry):
            at = pl.ds(pl.multiple_of(group * per * p_pad, 16), per * p_pad)
            high = in_high[at, :]
            low = in_low[at, :]
            both = dot(high, down)
            y = both[:, :f_pad] + both[:, f_pad:] + dot(low, down_high)
            for i in range(0, per, 2):
                x = jnp.concatenate([y[i * p_pad : (i + 1) * p_pad], y[(i + 1) * p_pad : (i + 2) * p_pad]], axis=1)
                high, low = split(x)
                z = dot(polar_back, jnp.concatenate([high, low, high], axis=0))
                for j in range(2):
                    lowered[pl.ds(pl.multiple_of(((i + j) * 8 + group) * pitch, 8), t_pad), :] = z[
                        :, j * f_pad : (j + 1) * f_pad
                    ]
            return carry

        lax.fori_loop(0, 8 * parents // per, one_group, 0)

        per_turn = next(n for n in (6, 5, 3, 2, 1) if (rows + 6) % n == 0)

        def some_rows(i, carry):
            for r in range(per_turn):
                turned = lowered[pl.ds(i * per_turn + r, 8 * parents, stride=pitch), :].T
                out_ref[i * per_turn + r] = turned[: columns + 8]
            return carry

        lax.fori_loop(0, (rows + 6) // per_turn, some_rows, 0)


def parent_level(child_out, after, before, side, table, sources, kinds, combine, polar_cos, polar_sin, phase):
    _, rows, columns, boxes = child_out.shape
    _, rows_up, columns_up, translators = table.shape
    assert boxes == LANES and translators == LANES
    parents, entries = sources.shape
    t_pad, p_pad = polar_cos.shape[1], polar_cos.shape[0]
    f_pad, q_pad = round_up(columns + 8, LANES), round_up(columns_up, LANES)
    assert f_pad == LANES
    table_steps = next(s for s in (4, 2, 1) if rows_up % s == 0)
    table_rows = rows_up // table_steps
    n_theta, n_phi = lax.axis_size("theta"), lax.axis_size("phi")
    polar_up = local_up(rows_up * n_theta, rows * n_theta, True, rows_up, rows, 3, (p_pad, t_pad))
    azimuth_up = local_up(columns_up * n_phi, columns * n_phi, False, columns_up, columns, 2, (q_pad, f_pad))
    high, low = split_constant(np.ascontiguousarray(azimuth_up.T))
    azimuth_three = jnp.asarray(np.concatenate([high, high, low], axis=0))
    high, low = split_constant(azimuth_up)
    azimuth_down = jnp.asarray(np.concatenate([high, low], axis=1))
    polar_down = jnp.asarray(np.ascontiguousarray(polar_up.T))

    def whole(array):
        return pl.BlockSpec(array.shape, lambda g: (0,) * array.ndim)

    def channel(shape):
        return pl.BlockSpec((2, 1) + shape, lambda g: (0, jnp.minimum(g, 3), 0, 0, 0))

    smem = pl.BlockSpec(memory_space=pltpu.SMEM)
    constants = [combine, polar_cos, polar_sin, azimuth_three, polar_down, azimuth_down, phase]
    return pl.pallas_call(
        functools.partial(
            parent_kernel, (rows, columns, rows_up, columns_up, parents, entries, table_steps, table_rows)
        ),
        grid=(5,),
        in_specs=[
            smem,
            smem,
            channel((rows, columns, boxes)),
            channel((3, columns, boxes)),
            channel((3, columns, boxes)),
            channel((rows + 6, 8, boxes)),
            pl.BlockSpec(
                (2, table_rows, columns_up, translators), lambda g: (0, jnp.minimum(g, table_steps - 1), 0, 0)
            ),
        ]
        + [whole(c) for c in constants],
        out_specs=pl.BlockSpec((rows + 6, columns + 8, 8 * parents), lambda g: (0, 0, 0)),
        out_shape=jax.ShapeDtypeStruct((rows + 6, columns + 8, 8 * parents), F32),
        scratch_shapes=[
            pltpu.VMEM((2, 128 * (t_pad + 8), f_pad), F32),
            pltpu.VMEM((2, 128 * (t_pad + 8), f_pad), F32),
            pltpu.VMEM((4, parents * p_pad, 3 * f_pad), BF16),
            pltpu.VMEM((q_pad // LANES * (p_pad // 8), 2, translators * 8, LANES), F32),
            pltpu.VMEM((q_pad // LANES * (p_pad // 8), parents * 96, LANES), F32),
            pltpu.VMEM((8 * parents * p_pad, q_pad), BF16),
            pltpu.VMEM((8 * parents * p_pad, q_pad), BF16),
            pltpu.VMEM((8 * parents * (t_pad + 8), f_pad), F32),
        ],
        compiler_params=pltpu.CompilerParams(vmem_limit_bytes=60 * MIB),
        cost_estimate=pl.CostEstimate(
            flops=20_000_000_000, bytes_accessed=child_out.size * 8, transcendentals=0
        ),
        name="parent_level",
    )(
        sources,
        kinds,
        child_out.reshape((2, 4) + child_out.shape[1:]),
        after.reshape((2, 4) + after.shape[1:]),
        before.reshape((2, 4) + before.shape[1:]),
        side.reshape((2, 4) + side.shape[1:]),
        table,
        *constants,
    )


def chain(count, periodic):
    pairs = [(i, i + 1) for i in range(count - 1)]
    return pairs + [(count - 1, 0)] if periodic else pairs


def send(block, axis, up):
    pairs = chain(lax.axis_size(axis), axis == "phi")
    return lax.ppermute(block, axis, pairs if up else [(b, a) for a, b in pairs])


def plain(array):
    return with_layout_constraint(array, Layout(major_to_minor=tuple(range(array.ndim))))


def per_device(
    child_out,
    child_slot,
    sources_child,
    kinds_child,
    table_child,
    sources_parent,
    kinds_parent,
    table_parent,
):
    _, rows, columns, boxes = child_out.shape
    _, rows_up, columns_up, _ = table_parent.shape
    parents = boxes // 8
    n_theta, n_phi = lax.axis_size("theta"), lax.axis_size("phi")
    t_pad, p_pad = round_up(rows + 6, 16), round_up(rows_up, 16)
    q_pad = round_up(columns_up, LANES)
    barrier = lax.optimization_barrier

    polar_up = local_up(rows_up * n_theta, rows * n_theta, True, rows_up, rows, 3, (p_pad, t_pad))
    sizes = (rows, columns, rows_up, columns_up, parents, n_theta, n_phi)
    combine, polar_cos, polar_sin, phase, phase_child = tables(
        child_slot, sizes, p_pad, t_pad, q_pad, jnp.asarray(polar_up)
    )

    samples = rows * columns
    flat_child = child_out.reshape(2, 4, samples, boxes)
    flat_table = table_child.reshape(2, samples, table_child.shape[3])
    pieces = segments(samples)
    local = [None] * len(pieces)
    chunks = [(n, i) for n, piece in enumerate(pieces) for i in range(piece[1])]

    def translate_next(child):
        if chunks:
            n, i = chunks.pop(0)
            local[n] = child_translate(
                child, flat_table, sources_child.T, kinds_child.T, pieces[n], i, local[n]
            )

    after = plain(send(plain(child_out[:, :3]), "theta", False))
    before = plain(send(plain(child_out[:, rows - 3 :]), "theta", True))
    first_child, made = barrier((flat_child, (combine, polar_cos, polar_sin, phase, phase_child)))
    combine, polar_cos, polar_sin, phase, phase_child = made
    translate_next(first_child)
    after, before, local = barrier((after, before, local))

    low, high = (
        jnp.concatenate([edge[:, :, at] for edge in (child_out, after, before)], axis=1)
        for at in (slice(0, 3), slice(columns - 2, columns))
    )
    low, high, later_child = barrier((low, high, flat_child))
    right = send(low, "phi", False)
    left = send(high, "phi", True)
    if len(chunks) > 1:
        translate_next(later_child)
    right, left, local = barrier((right, left, local))
    side = jnp.concatenate([right, left, jnp.zeros((8, rows + 6, 3, boxes), F32)], axis=2)

    lowered = parent_level(
        child_out,
        after,
        before,
        side,
        table_parent,
        sources_parent,
        kinds_parent,
        combine,
        polar_cos,
        polar_sin,
        phase,
    )
    lowered, later_child = barrier((lowered, flat_child))

    low = send(lowered[rows : rows + 3], "theta", True)
    high = send(lowered[rows + 3 : rows + 6], "theta", False)
    while chunks:
        translate_next(later_child)
    local, lowered = barrier((local, lowered))
    here = lowered[:rows]
    here = here + jnp.pad(low, ((0, rows - 3), (0, 0), (0, 0))) + jnp.pad(high, ((rows - 3, 0), (0, 0), (0, 0)))
    low = send(here[:, columns : columns + 3], "phi", True)
    high = send(here[:, columns + 3 : columns + 5], "phi", False)
    here = here[:, :columns]
    here = here + jnp.pad(low, ((0, 0), (0, columns - 3), (0, 0))) + jnp.pad(high, ((0, 0), (columns - 2, 0), (0, 0)))
    here = here.reshape(samples, boxes)

    result = None
    for piece, part in zip(pieces, local):
        result = final_sum(flat_child.shape, part, here, phase_child, child_slot, piece, result)
    return result.reshape(child_out.shape)


def solution(mesh):
    placed = (
        P(None, "theta", "phi", None),
        P(),
        P(),
        P(),
        P(None, "theta", "phi", None),
        P(),
        P(),
        P(None, "theta", "phi", None),
    )
    return jax.shard_map(
        per_device,
        mesh=mesh,
        in_specs=placed,
        out_specs=P(None, "theta", "phi", None),
        check_vma=False,
    )
```

```python
import functools
import math

import jax
import jax.numpy as jnp
import numpy as np
from jax import lax
from jax.experimental import pallas as pl
from jax.experimental.layout import Layout, with_layout_constraint
from jax.experimental.pallas import tpu as pltpu
from jax.sharding import PartitionSpec as P

BAND1 = 180
WAVE = BAND1 / (2.0 * math.sqrt(3.0))
LANES = 128
MIB = 1 << 20
F32 = jnp.float32
BF16 = jnp.bfloat16


def round_up(count, step):
    return -(-count // step) * step


def stencil_entries(count_out, count_in, centered, out_rows):
    entries = []
    for row_out in out_rows:
        if centered:
            numerator = (2 * row_out + 1) * count_in - count_out
        else:
            numerator = 2 * row_out * count_in
        denominator = 2 * count_out
        base_index = numerator // denominator
        fraction = (numerator - base_index * denominator) / denominator
        for offset_a in range(-2, 4):
            weight = 1.0
            for offset_b in range(-2, 4):
                if offset_b != offset_a:
                    weight = weight * (fraction - offset_b) / (offset_a - offset_b)
            entries.append((row_out, base_index + offset_a, weight))
    return entries


def local_up(count_out, count_in, centered, rows_out, rows_in, below, shape):
    matrix = np.zeros(shape)
    for row_out, column, weight in stencil_entries(count_out, count_in, centered, range(rows_out)):
        assert -below <= column < rows_in + 3 or abs(weight) < 1e-12
        if column >= 0:
            matrix[row_out, column] += weight
        elif column >= -below:
            matrix[row_out, rows_in + 3 + below + column] += weight
    return matrix.astype(np.float32)


def split(x):
    high = x.astype(BF16)
    return high, (x - high.astype(F32)).astype(BF16)


def split_constant(matrix):
    high = matrix.astype(jnp.bfloat16)
    return high, (matrix - high.astype(np.float32)).astype(jnp.bfloat16)


def dot(a, b):
    return jnp.dot(a, b, preferred_element_type=F32)


def dot_transposed(a, b):
    return lax.dot_general(a, b, (((1,), (1,)), ((), ())), preferred_element_type=F32)


def segments(samples):
    full, rest = divmod(samples, 8 * LANES)
    found = [(0, full, 1, 8)] if full else []
    if rest:
        rows = -(-rest // LANES)
        packed = 4 if rows <= 2 else 2 if rows <= 4 else 1
        found.append((full, 1, packed, rows))
    return found


def translate_kernel(packed, rows, source_ref, kind_ref, child_ref, table_ref, *rest):
    out_ref, pattern, table = rest[-3:]
    groups, per = 4 // packed, 8 // packed
    tile = 16 * groups
    pitch = tile + 8
    entries = source_ref.shape[0]
    step = pl.program_id(0)

    @pl.when(step == 0)
    def _():
        for row in range(rows):
            real, imag = (table_ref[part, row * LANES : (row + 1) * LANES].T for part in range(2))
            for part, turned in enumerate((real, imag - real, real + imag)):
                for c in range(packed):
                    table[part, pl.ds(c * per + row, LANES, stride=8), :] = turned

    @pl.when(step < 2)
    def _():
        for i in range(2):
            c = 2 * step + i
            plane, sub = (c, 0) if packed == 1 else (c // packed, c % packed * per)
            for part in range(2):
                for row in range(rows):
                    at = pl.ds((part * groups + plane) * 8 + sub + row, LANES, stride=pitch)
                    pattern[at, :] = child_ref[part, i, row * LANES : (row + 1) * LANES].T

    @pl.when(step >= 2)
    def _():
        half = LANES // 2

        def one_box(i, carry):
            box = (step - 2) * half + i
            sums = [[None] * groups for _ in range(3)]
            for entry in range(entries):
                x = pattern[pl.ds(pl.multiple_of(source_ref[entry, box] * pitch, 8), tile), :]
                kind = pl.ds(pl.multiple_of(kind_ref[entry, box] * 8, 8), 8)
                factors = [table[part, kind, :] for part in range(3)]
                for g in range(groups):
                    xr, xi = x[g * 8 : g * 8 + 8], x[(groups + g) * 8 : (groups + g) * 8 + 8]
                    for part, term in enumerate((xr + xi, xr, xi)):
                        product = term * factors[part]
                        sums[part][g] = product if entry == 0 else sums[part][g] + product
            total = [sums[0][g] - sums[2][g] for g in range(groups)]
            total += [sums[0][g] + sums[1][g] for g in range(groups)]
            for g in range(2 * groups):
                out_ref[0, pl.ds(pl.multiple_of(i * tile, tile) + g * 8, 8), :] = total[g]
            return carry

        lax.fori_loop(0, half, one_box, 0, unroll=4)


def child_translate(child, table, sources, kinds, segment, chunk, onto):
    first, count, packed, rows = segment
    tile = 64 // packed
    smem = pl.BlockSpec(memory_space=pltpu.SMEM)
    in_specs = [
        smem,
        smem,
        pl.BlockSpec((2, 2, 8 * LANES, LANES), lambda s: (0, jnp.minimum(s, 1), first + chunk, 0)),
        pl.BlockSpec((2, 8 * LANES, LANES), lambda s: (0, first + chunk, 0)),
    ]
    operands = [sources, kinds, child, table]
    aliases = {}
    if onto is not None:
        in_specs.append(pl.BlockSpec(memory_space=pl.ANY))
        operands.append(onto)
        aliases = {4: 0}
    work = rows * LANES * LANES
    return pl.pallas_call(
        functools.partial(translate_kernel, packed, rows),
        grid=(4,),
        in_specs=in_specs,
        out_specs=pl.BlockSpec((1, LANES // 2 * tile, LANES), lambda s: (chunk, jnp.maximum(s - 2, 0), 0)),
        out_shape=jax.ShapeDtypeStruct((count, LANES * tile, LANES), F32),
        input_output_aliases=aliases,
        scratch_shapes=[
            pltpu.VMEM((LANES * (tile + 8) + tile + 8, LANES), F32),
            pltpu.VMEM((3, LANES * 8 + 8, LANES), F32),
        ],
        compiler_params=pltpu.CompilerParams(vmem_limit_bytes=60 * MIB),
        cost_estimate=pl.CostEstimate(
            flops=work * sources.shape[0] * 32, bytes_accessed=work * 72, transcendentals=0
        ),
        name="child_translate",
    )(*operands)


def sum_kernel(packed, rows, parents, slot_ref, local_ref, lowered_ref, phase_ref, *rest):
    out_ref, lowered, total, phase = rest[-4:]
    groups, per = 4 // packed, 8 // packed
    tile = 16 * groups
    pitch = tile + 8
    step = pl.program_id(1)

    @pl.when(step == 0)
    def _():
        for row in range(rows):
            lowered[pl.ds(row, LANES, stride=per), :] = lowered_ref[row * LANES : (row + 1) * LANES].T
        for octant in range(8):
            for part in range(2):
                phase[2 * octant + part] = jnp.concatenate([phase_ref[8 * part + octant, :per]] * packed, axis=0)

    @pl.when(step < 2)
    def _():
        half = LANES // 2

        def one_box(i, carry):
            slot = slot_ref[step * half + i]
            octant = slot >> (parents.bit_length() - 1)
            cosine, sine = phase[2 * octant], phase[2 * octant + 1]
            x = lowered[pl.ds(pl.multiple_of((slot & (parents - 1)) * tile, tile), tile), :]
            local = local_ref[0, pl.ds(pl.multiple_of(i * tile, tile), tile), :]
            here = pl.multiple_of((step * half + i) * pitch, 8)
            for g in range(groups):
                at, to = slice(g * 8, g * 8 + 8), slice((groups + g) * 8, (groups + g) * 8 + 8)
                real, imag = x[at], x[to]
                total[pl.ds(here + g * 8, 8), :] = local[at] + (real * cosine + imag * sine)
                total[pl.ds(here + (groups + g) * 8, 8), :] = local[to] + (imag * cosine - real * sine)
            return carry

        lax.fori_loop(0, half, one_box, 0, unroll=8)

    @pl.when(step >= 2)
    def _():
        for i in range(2):
            c = 2 * (step - 2) + i
            plane, sub = (c, 0) if packed == 1 else (c // packed, c % packed * per)
            for part in range(2):
                for row in range(rows):
                    at = pl.ds((part * groups + plane) * 8 + sub + row, LANES, stride=pitch)
                    out_ref[part, i, row * LANES : (row + 1) * LANES] = total[at, :].T


def final_sum(shape, local, lowered, phase, slots, segment, onto):
    first, count, packed, rows = segment
    tile = 64 // packed
    in_specs = [
        pl.BlockSpec(memory_space=pltpu.SMEM),
        pl.BlockSpec((1, LANES // 2 * tile, LANES), lambda i, s: (i, jnp.minimum(s, 1), 0)),
        pl.BlockSpec((8 * LANES, LANES), lambda i, s: (first + i, 0)),
        pl.BlockSpec((16, 8, LANES), lambda i, s: (0, first + i, 0)),
    ]
    operands = [slots, local, lowered, phase]
    aliases = {}
    if onto is not None:
        in_specs.append(pl.BlockSpec(memory_space=pl.ANY))
        operands.append(onto)
        aliases = {4: 0}
    work = count * rows * LANES * LANES
    return pl.pallas_call(
        functools.partial(sum_kernel, packed, rows, LANES // 8),
        grid=(count, 4),
        in_specs=in_specs,
        out_specs=pl.BlockSpec((2, 2, 8 * LANES, LANES), lambda i, s: (0, jnp.maximum(s - 2, 0), first + i, 0)),
        out_shape=jax.ShapeDtypeStruct(shape, F32),
        input_output_aliases=aliases,
        scratch_shapes=[
            pltpu.VMEM((LANES * (8 // packed) + 8, LANES), F32),
            pltpu.VMEM((LANES * (tile + 8) + tile + 8, LANES), F32),
            pltpu.VMEM((16, 8, LANES), F32),
        ],
        compiler_params=pltpu.CompilerParams(vmem_limit_bytes=60 * MIB),
        cost_estimate=pl.CostEstimate(flops=work * 32, bytes_accessed=work * 72, transcendentals=0),
        name="final_sum",
    )(*operands)


def cos_sin(x):
    turns = jnp.floor(x * (2.0 / math.pi) + 0.5)
    rest = ((x - turns * 1.5703125) - turns * 4.837512969970703e-4) - turns * 7.54978995489188e-8
    square = rest * rest
    sine = rest + rest * square * (
        -1.6666654611e-1 + square * (8.3321608736e-3 + square * -1.9515295891e-4)
    )
    cosine = (1.0 - 0.5 * square) + square * square * (
        4.166664568298827e-2 + square * (-1.388731625493765e-3 + square * 2.443315711809948e-5)
    )
    quarter = turns.astype(jnp.int32)
    odd = (quarter & 1) == 1
    first, second = jnp.where(odd, sine, cosine), jnp.where(odd, cosine, sine)
    first = jnp.where(((quarter + 1) & 2) == 2, -first, first)
    second = jnp.where((quarter & 2) == 2, -second, second)
    return first, second


def tables_kernel(sizes, slot_ref, polar_up_ref, combine_ref, cos_ref, sin_ref, phase_ref, child_ref):
    rows, columns, rows_up, columns_up, parents, n_theta, n_phi = sizes
    polar_index, azimuth_index = lax.axis_index("theta"), lax.axis_index("phi")

    def iota(shape, axis):
        return lax.broadcasted_iota(jnp.int32, shape, axis)

    boxes = slot_ref.shape[1]
    slot = jnp.broadcast_to(slot_ref[...], (parents, boxes))
    same = (slot & (parents - 1)) == iota((parents, boxes), 0)
    octant = slot >> (parents.bit_length() - 1)
    east, north, upper = (2 * ((octant >> n) & 1) - 1 for n in range(3))
    blocks = []
    for z in range(2):
        for kind in range(2):
            for difference in range(2):
                chosen = same & ((east == north) if kind == 0 else (east != north))
                weight = (upper if z else 1) * (east if difference else 1)
                weight = jnp.where(chosen, weight, 0).astype(F32)
                blocks.append(weight)
    combine = jnp.concatenate(blocks, axis=0).astype(BF16)
    combine_ref[...] = jnp.concatenate([combine, combine], axis=1)

    p_pad, t_pad = cos_ref.shape
    q_pad = phase_ref.shape[2]
    polar = (iota((p_pad, LANES), 0) + polar_index * rows_up).astype(F32) + 0.5
    cosine, sine = cos_sin(polar * (math.pi / (rows_up * n_theta)))
    up_cos, up_sin = cos_sin(WAVE * cosine)
    cos_ref[...] = polar_up_ref[...] * up_cos[:, :t_pad]
    sin_ref[...] = polar_up_ref[...] * up_sin[:, :t_pad]
    azimuth = (iota((8, q_pad), 1) + azimuth_index * columns_up).astype(F32)
    east, north = cos_sin(azimuth * (2.0 * math.pi / (columns_up * n_phi)))
    flat = WAVE * sine
    valid = iota((p_pad, LANES), 0) < rows_up
    for lane in range(0, q_pad, LANES):
        lanes = slice(lane, lane + LANES)
        inside = valid & (iota((p_pad, LANES), 1) + lane < columns_up)
        for kind in range(2):
            turned = (east - north if kind else east + north)[:1, lanes]
            found = cos_sin(flat * turned)
            for i in range(2):
                phase_ref[2 * kind + i, :, lanes] = jnp.where(inside, found[i], 0.0)

    count = child_ref.shape[1]
    sample = iota((count, LANES), 0) * LANES + iota((count, LANES), 1)
    row = jnp.floor((sample.astype(F32) + 0.5) * (1.0 / columns))
    polar = row + (polar_index * rows).astype(F32) + 0.5
    azimuth = sample.astype(F32) - row * columns + (azimuth_index * columns).astype(F32)
    up, flat = cos_sin(polar * (math.pi / (rows * n_theta)))
    east, north = cos_sin(azimuth * (2.0 * math.pi / (columns * n_phi)))
    for octant in range(4):
        signs = [2 * ((octant >> n) & 1) - 1 for n in range(3)]
        found = cos_sin(WAVE * (flat * east * signs[0] + flat * north * signs[1] + up * signs[2]))
        child_ref[octant] = found[0]
        child_ref[7 - octant] = found[0]
        child_ref[8 + octant] = found[1]
        child_ref[15 - octant] = -found[1]


def tables(slots, sizes, p_pad, t_pad, q_pad, polar_up):
    rows, columns, rows_up, columns_up, parents, n_theta, n_phi = sizes
    boxes = slots.shape[0]
    assert parents & (parents - 1) == 0
    return pl.pallas_call(
        functools.partial(tables_kernel, sizes),
        out_shape=[
            jax.ShapeDtypeStruct((8 * parents, 2 * boxes), BF16),
            jax.ShapeDtypeStruct((p_pad, t_pad), F32),
            jax.ShapeDtypeStruct((p_pad, t_pad), F32),
            jax.ShapeDtypeStruct((4, p_pad, q_pad), F32),
            jax.ShapeDtypeStruct((16, -(-rows * columns // LANES), LANES), F32),
        ],
        compiler_params=pltpu.CompilerParams(vmem_limit_bytes=60 * MIB),
        name="tables",
    )(slots.reshape(1, boxes), polar_up)


def parent_kernel(
    sizes,
    source_ref,
    kind_ref,
    child_ref,
    next_ref,
    previous_ref,
    side_ref,
    table_ref,
    combine_ref,
    polar_cos_ref,
    polar_sin_ref,
    azimuth_up_ref,
    polar_down_ref,
    azimuth_down_ref,
    phase_ref,
    out_ref,
    wide_even,
    wide_odd,
    rows_done,
    table_by_kind,
    parent_out,
    in_high,
    in_low,
    lowered,
):
    (rows, columns, rows_up, columns_up, parents, entries, table_steps, table_rows) = sizes
    pitch, f_pad = wide_even.shape[1] // 129, wide_even.shape[2]
    t_pad = pitch - 8
    p_pad, q_pad = phase_ref.shape[1], phase_ref.shape[2]
    row_tiles, lane_tiles = p_pad // 8, q_pad // LANES
    step = pl.program_id(0)
    half = 4 * parents
    table_first = jnp.minimum(step, table_steps - 1) * table_rows

    @pl.when(step == 0)
    def _():
        for part in range(2):
            for t in range(rows + 6, t_pad):
                for wide in (wide_even, wide_odd):
                    wide[part, pl.ds(t, 128, stride=pitch), :] = jnp.zeros((128, f_pad), F32)
        for part in range(2):
            for p in range(rows_up, p_pad):
                for lane_tile in range(lane_tiles):
                    at = pl.ds(p % 8, 128, stride=8)
                    table_by_kind[lane_tile * row_tiles + p // 8, part, at, :] = jnp.zeros((128, LANES), F32)

    combine = combine_ref[...]

    def samples(part, main_ref, r, t):
        x = jnp.concatenate(
            [main_ref[part, 0, r], side_ref[part, 0, t], jnp.zeros((f_pad - columns - 8, LANES), F32)], axis=0
        )
        high, low = split(x)
        return jnp.concatenate([high, low], axis=1)

    def turn(rows_here, wide):
        pieces = [(part,) + row for row in rows_here for part in range(2)]
        for i in range(0, len(pieces), 2):
            both = jnp.concatenate([samples(*piece) for piece in pieces[i : i + 2]], axis=0)
            turned = dot_transposed(combine, both)
            for j, piece in enumerate(pieces[i : i + 2]):
                at = pl.ds(piece[3], 128, stride=pitch)
                wide[piece[0], at, :] = turned[:, j * f_pad : (j + 1) * f_pad]

    def turn_table(r):
        p = table_first + r
        at = pl.ds(p & 7, 128, stride=8)
        for part in range(2):
            x = table_ref[part, r]
            if q_pad > columns_up:
                x = jnp.concatenate([x, jnp.zeros((q_pad - columns_up, LANES), F32)], axis=0)
            for lane_tile in range(lane_tiles):
                turned = x[lane_tile * LANES : (lane_tile + 1) * LANES].T
                table_by_kind[lane_tile * row_tiles + (p >> 3), part, at, :] = turned

    def shares(count):
        pairs = -(-count // 2)
        sizes_here = [(pairs + 3 - i) // 4 for i in range(4)]
        return [(2 * sum(sizes_here[:i]), sizes_here[i]) for i in range(4)]

    per = 4

    def channel(read, write):
        if write is not None:
            turn(
                [(next_ref, r, rows + r) for r in range(3)] + [(previous_ref, r, rows + 3 + r) for r in range(3)],
                write,
            )
        if read is not None:
            polar = []
            for sign in (-1.0, 1.0):
                high, low = split(jnp.concatenate([polar_cos_ref[...], sign * polar_sin_ref[...]], axis=1))
                polar.append(jnp.concatenate([high, high, low], axis=1))
        for target in range(2):
            for difference in range(2):
                part = target if difference == 0 else 1 - target
                loop = 2 * target + difference

                def one_kind(kind, carry, part=part, difference=difference, loop=loop):
                    if write is not None:
                        first, count = shares(rows)[loop]
                        here = [jnp.minimum(first + kind * count + j, rows - 1) for j in range(count)]
                        turn([(child_ref, r, r) for r in here], write)
                        first, count = shares(table_rows)[loop]
                        for j in range(count):
                            turn_table(jnp.minimum(first + kind * count + j, table_rows - 1))
                    if read is not None:
                        first = (kind * 2 + difference) * parents
                        for pair in range(parents // 2):
                            stacked = []
                            for source, offset in ((part, 0), (1 - part, half)):
                                at = (offset + first + 2 * pair) * pitch
                                both = [
                                    read[source, pl.ds(pl.multiple_of(at + i * pitch, 8), t_pad), :] for i in range(2)
                                ]
                                stacked.append(jnp.concatenate(both, axis=1))
                            high, low = split(jnp.concatenate(stacked, axis=0))
                            result = dot(polar[part], jnp.concatenate([high, low, high], axis=0))
                            high, low = split(result)
                            for i in range(2):
                                lanes = slice(i * f_pad, (i + 1) * f_pad)
                                rows_done[kind * 2 + difference, pl.ds((2 * pair + i) * p_pad, p_pad), :] = (
                                    jnp.concatenate([high[:, lanes], low[:, lanes], high[:, lanes]], axis=1)
                                )
                    return carry

                lax.fori_loop(0, 2, one_kind, 0)

            if read is None:
                continue

            def one_group(group, carry, target=target):
                at = pl.ds(pl.multiple_of(group * per * p_pad, 16), per * p_pad)
                y = dot(jnp.concatenate([rows_done[k, at, :] for k in range(4)], axis=0), azimuth_up_ref[...])
                for i in range(per):
                    terms = [y[(k * per + i) * p_pad : (k * per + i + 1) * p_pad] * phase_ref[k] for k in range(4)]
                    if target == 0:
                        value = (terms[0] - terms[1]) + (terms[2] - terms[3])
                    else:
                        value = (terms[0] + terms[1]) + (terms[2] + terms[3])
                    at, to, both = (
                        pl.ds(pl.multiple_of((group * per + i) * 96 + part * 32 + (step - 1) * 8, 8), 8)
                        for part in range(3)
                    )
                    for lane_tile in range(lane_tiles):
                        lanes = slice(lane_tile * LANES, (lane_tile + 1) * LANES)
                        for row_tile in range(row_tiles):
                            tile = value[row_tile * 8 : row_tile * 8 + 8, lanes]
                            where = lane_tile * row_tiles + row_tile
                            if target == 0:
                                parent_out[where, at, :] = tile
                            else:
                                parent_out[where, to, :] = tile
                                parent_out[where, both, :] = parent_out[where, at, :] + tile
                return carry

            lax.fori_loop(0, parents // per, one_group, 0)

    pl.when(step == 0)(lambda: channel(None, wide_even))
    pl.when((step == 1) | (step == 3))(lambda: channel(wide_even, wide_odd))
    pl.when(step == 2)(lambda: channel(wide_odd, wide_even))
    pl.when(step == 4)(lambda: channel(wide_odd, None))

    @pl.when(step == 4)
    def _():
        def one_tile(tile, carry):
            box = tile // (p_pad // 16)
            row_pair = tile % (p_pad // 16)
            sources = [pl.ds(pl.multiple_of(source_ref[box, e] * 96, 32), 96) for e in range(entries)]
            kinds = [pl.ds(pl.multiple_of(kind_ref[box, e] * 8, 8), 8) for e in range(entries)]
            for lane_tile in range(lane_tiles):
                halves = []
                for i in range(2):
                    where = lane_tile * row_tiles + 2 * row_pair + i
                    sums = [[None] * 4 for _ in range(3)]
                    for e in range(entries):
                        x = parent_out[where, sources[e], :]
                        real, imag = (table_by_kind[where, part, kinds[e], :] for part in range(2))
                        factors = (imag - real, real + imag, real)
                        for c in range(4):
                            for part in range(3):
                                product = x[(4 * part + c) * 8 : (4 * part + c) * 8 + 8] * factors[part]
                                sums[part][c] = product if e == 0 else sums[part][c] + product
                    total = [sums[2][c] - sums[1][c] for c in range(4)]
                    total += [sums[2][c] + sums[0][c] for c in range(4)]
                    halves.append(total)
                for c in range(8):
                    high, low = split(jnp.concatenate([halves[0][c], halves[1][c]], axis=0))
                    at = pl.ds(pl.multiple_of((c * parents + box) * p_pad + row_pair * 16, 16), 16)
                    lanes = slice(lane_tile * LANES, (lane_tile + 1) * LANES)
                    in_high[at, lanes] = high
                    in_low[at, lanes] = low
            return carry

        lax.fori_loop(0, parents * (p_pad // 16), one_tile, 0)

        down = azimuth_down_ref[...]
        down_high = down[:, :f_pad]
        high, low = split(polar_down_ref[...])
        polar_back = jnp.concatenate([high, high, low], axis=1)
        per = parents

        def one_group(group, carry):
            at = pl.ds(pl.multiple_of(group * per * p_pad, 16), per * p_pad)
            high = in_high[at, :]
            low = in_low[at, :]
            both = dot(high, down)
            y = both[:, :f_pad] + both[:, f_pad:] + dot(low, down_high)
            for i in range(0, per, 2):
                x = jnp.concatenate([y[i * p_pad : (i + 1) * p_pad], y[(i + 1) * p_pad : (i + 2) * p_pad]], axis=1)
                high, low = split(x)
                z = dot(polar_back, jnp.concatenate([high, low, high], axis=0))
                for j in range(2):
                    lowered[pl.ds(pl.multiple_of(((i + j) * 8 + group) * pitch, 8), t_pad), :] = z[
                        :, j * f_pad : (j + 1) * f_pad
                    ]
            return carry

        lax.fori_loop(0, 8 * parents // per, one_group, 0)

        per_turn = next(n for n in (6, 5, 3, 2, 1) if (rows + 6) % n == 0)

        def some_rows(i, carry):
            for r in range(per_turn):
                turned = lowered[pl.ds(i * per_turn + r, 8 * parents, stride=pitch), :].T
                out_ref[i * per_turn + r] = turned[: columns + 8]
            return carry

        lax.fori_loop(0, (rows + 6) // per_turn, some_rows, 0)


def parent_level(child_out, after, before, side, table, sources, kinds, combine, polar_cos, polar_sin, phase):
    _, rows, columns, boxes = child_out.shape
    _, rows_up, columns_up, translators = table.shape
    assert boxes == LANES and translators == LANES
    parents, entries = sources.shape
    t_pad, p_pad = polar_cos.shape[1], polar_cos.shape[0]
    f_pad, q_pad = round_up(columns + 8, LANES), round_up(columns_up, LANES)
    assert f_pad == LANES
    table_steps = next(s for s in (4, 2, 1) if rows_up % s == 0)
    table_rows = rows_up // table_steps
    n_theta, n_phi = lax.axis_size("theta"), lax.axis_size("phi")
    polar_up = local_up(rows_up * n_theta, rows * n_theta, True, rows_up, rows, 3, (p_pad, t_pad))
    azimuth_up = local_up(columns_up * n_phi, columns * n_phi, False, columns_up, columns, 2, (q_pad, f_pad))
    high, low = split_constant(np.ascontiguousarray(azimuth_up.T))
    azimuth_three = jnp.asarray(np.concatenate([high, high, low], axis=0))
    high, low = split_constant(azimuth_up)
    azimuth_down = jnp.asarray(np.concatenate([high, low], axis=1))
    polar_down = jnp.asarray(np.ascontiguousarray(polar_up.T))

    def whole(array):
        return pl.BlockSpec(array.shape, lambda g: (0,) * array.ndim)

    def channel(shape):
        return pl.BlockSpec((2, 1) + shape, lambda g: (0, jnp.minimum(g, 3), 0, 0, 0))

    smem = pl.BlockSpec(memory_space=pltpu.SMEM)
    constants = [combine, polar_cos, polar_sin, azimuth_three, polar_down, azimuth_down, phase]
    return pl.pallas_call(
        functools.partial(
            parent_kernel, (rows, columns, rows_up, columns_up, parents, entries, table_steps, table_rows)
        ),
        grid=(5,),
        in_specs=[
            smem,
            smem,
            channel((rows, columns, boxes)),
            channel((3, columns, boxes)),
            channel((3, columns, boxes)),
            channel((rows + 6, 8, boxes)),
            pl.BlockSpec(
                (2, table_rows, columns_up, translators), lambda g: (0, jnp.minimum(g, table_steps - 1), 0, 0)
            ),
        ]
        + [whole(c) for c in constants],
        out_specs=pl.BlockSpec((rows + 6, columns + 8, 8 * parents), lambda g: (0, 0, 0)),
        out_shape=jax.ShapeDtypeStruct((rows + 6, columns + 8, 8 * parents), F32),
        scratch_shapes=[
            pltpu.VMEM((2, 129 * (t_pad + 8), f_pad), F32),
            pltpu.VMEM((2, 129 * (t_pad + 8), f_pad), F32),
            pltpu.VMEM((4, parents * p_pad, 3 * f_pad), BF16),
            pltpu.VMEM((q_pad // LANES * (p_pad // 8), 2, translators * 8 + 8, LANES), F32),
            pltpu.VMEM((q_pad // LANES * (p_pad // 8), parents * 96, LANES), F32),
            pltpu.VMEM((8 * parents * p_pad, q_pad), BF16),
            pltpu.VMEM((8 * parents * p_pad, q_pad), BF16),
            pltpu.VMEM(((8 * parents + 1) * (t_pad + 8), f_pad), F32),
        ],
        compiler_params=pltpu.CompilerParams(vmem_limit_bytes=60 * MIB),
        cost_estimate=pl.CostEstimate(
            flops=20_000_000_000, bytes_accessed=child_out.size * 8, transcendentals=0
        ),
        name="parent_level",
    )(
        sources,
        kinds,
        child_out.reshape((2, 4) + child_out.shape[1:]),
        after.reshape((2, 4) + after.shape[1:]),
        before.reshape((2, 4) + before.shape[1:]),
        side.reshape((2, 4) + side.shape[1:]),
        table,
        *constants,
    )


def chain(count, periodic):
    pairs = [(i, i + 1) for i in range(count - 1)]
    return pairs + [(count - 1, 0)] if periodic else pairs


def send(block, axis, up):
    pairs = chain(lax.axis_size(axis), axis == "phi")
    return lax.ppermute(block, axis, pairs if up else [(b, a) for a, b in pairs])


def plain(array):
    return with_layout_constraint(array, Layout(major_to_minor=tuple(range(array.ndim))))


def per_device(
    child_out,
    child_slot,
    sources_child,
    kinds_child,
    table_child,
    sources_parent,
    kinds_parent,
    table_parent,
):
    _, rows, columns, boxes = child_out.shape
    _, rows_up, columns_up, _ = table_parent.shape
    parents = boxes // 8
    n_theta, n_phi = lax.axis_size("theta"), lax.axis_size("phi")
    t_pad, p_pad = round_up(rows + 6, 16), round_up(rows_up, 16)
    q_pad = round_up(columns_up, LANES)
    barrier = lax.optimization_barrier

    polar_up = local_up(rows_up * n_theta, rows * n_theta, True, rows_up, rows, 3, (p_pad, t_pad))
    sizes = (rows, columns, rows_up, columns_up, parents, n_theta, n_phi)
    combine, polar_cos, polar_sin, phase, phase_child = tables(
        child_slot, sizes, p_pad, t_pad, q_pad, jnp.asarray(polar_up)
    )

    samples = rows * columns
    flat_child = child_out.reshape(2, 4, samples, boxes)
    flat_table = table_child.reshape(2, samples, table_child.shape[3])
    pieces = segments(samples)
    local = [None] * len(pieces)
    chunks = [(n, i) for n, piece in enumerate(pieces) for i in range(piece[1])]

    def translate_next(child):
        if chunks:
            n, i = chunks.pop(0)
            local[n] = child_translate(
                child, flat_table, sources_child.T, kinds_child.T, pieces[n], i, local[n]
            )

    after = plain(send(plain(child_out[:, :3]), "theta", False))
    before = plain(send(plain(child_out[:, rows - 3 :]), "theta", True))
    first_child, made = barrier((flat_child, (combine, polar_cos, polar_sin, phase, phase_child)))
    combine, polar_cos, polar_sin, phase, phase_child = made
    translate_next(first_child)
    after, before, local = barrier((after, before, local))

    low, high = (
        jnp.concatenate([edge[:, :, at] for edge in (child_out, after, before)], axis=1)
        for at in (slice(0, 3), slice(columns - 2, columns))
    )
    low, high, later_child = barrier((low, high, flat_child))
    right = send(low, "phi", False)
    left = send(high, "phi", True)
    if len(chunks) > 1:
        translate_next(later_child)
    right, left, local = barrier((right, left, local))
    side = jnp.concatenate([right, left, jnp.zeros((8, rows + 6, 3, boxes), F32)], axis=2)

    lowered = parent_level(
        child_out,
        after,
        before,
        side,
        table_parent,
        sources_parent,
        kinds_parent,
        combine,
        polar_cos,
        polar_sin,
        phase,
    )
    lowered, later_child = barrier((lowered, flat_child))

    low = send(lowered[rows : rows + 3], "theta", True)
    high = send(lowered[rows + 3 : rows + 6], "theta", False)
    while chunks:
        translate_next(later_child)
    local, lowered = barrier((local, lowered))
    here = lowered[:rows]
    here = here + jnp.pad(low, ((0, rows - 3), (0, 0), (0, 0))) + jnp.pad(high, ((rows - 3, 0), (0, 0), (0, 0)))
    low = send(here[:, columns : columns + 3], "phi", True)
    high = send(here[:, columns + 3 : columns + 5], "phi", False)
    here = here[:, :columns]
    here = here + jnp.pad(low, ((0, 0), (0, columns - 3), (0, 0))) + jnp.pad(high, ((0, 0), (columns - 2, 0), (0, 0)))
    here = here.reshape(samples, boxes)

    result = None
    for piece, part in zip(pieces, local):
        result = final_sum(flat_child.shape, part, here, phase_child, child_slot, piece, result)
    return result.reshape(child_out.shape)


def solution(mesh):
    placed = (
        P(None, "theta", "phi", None),
        P(),
        P(),
        P(),
        P(None, "theta", "phi", None),
        P(),
        P(),
        P(None, "theta", "phi", None),
    )
    return jax.shard_map(
        per_device,
        mesh=mesh,
        in_specs=placed,
        out_specs=P(None, "theta", "phi", None),
        check_vma=False,
    )
```
